32 devices in a mesh: grp: 2 (over x), ad: 16 (over z, y, core).
Axes of the slice: x: 2, y: 2, z: 4, core: 2. Of those that a mesh axis runs over, the one named last changes fastest.
Arguments:
- tokens: bfloat16 [8192, 8192], P(('grp', 'ad')), parts along dimension 0, may hold values from -6 to 6
- value_weight: bfloat16 [8192, 512], replicated, may hold values from -0.0625 to 0.0625
- adapt_down: bfloat16 [512, 8192, 16], P(('grp', 'ad')), parts along dimension 0, may hold values from -0.0625 to 0.0625
- adapt_up: bfloat16 [512, 16, 512], P(('grp', 'ad')), parts along dimension 0, may hold values from -1.5 to 1.5
- tenant_ids: int32 [8192, 1], P(('grp', 'ad')), parts along dimension 0, may hold values from 0 to 255; in each aligned block of 256 rows (0 to 255, 256 to 511, ...) at most 2 rows name the same one
- tenant_slot: int32 [512], P('grp'), parts along dimension 0, may hold values from 0 to 255, each once
Outputs:
- values_out: bfloat16 [8192, 512], P(('grp', 'ad')), parts along dimension 0
The draws below stay inside these ranges and needn't reach their ends.
There are 2 independent parts, one for each index of `grp`. The reference program is written for one: setup_inputs(seed, part) draws one part's arguments, and reference() takes and returns one part's arrays. A program takes and returns all parts, laid end to end along the dimension named above; an argument that names none is the same for every part. Nothing has to cross between parts.
Inputs may be any that keep to these rules, and one draw needn't show every extreme that they name: `tenant_ids`: among the rows of one device no tenant appears more than 2 times, and some tenant appears exactly 2 times. `tenant_slot`: each slot holds exactly one tenant.
All inputs are finite; a program needn't handle non-finite values.
Results may differ from the reference program's by a relative error of at most 0.0049.
Values may be sent and summed in bfloat16 or wider, within the bound.
No kernel may reach another device: no remote copies, remote signals or barrier semaphores. Data moves between devices by JAX's collectives and lax.ppermute only.
A program may use at most 128 MiB of HBM per device.

```python
import math
import jax
import jax.numpy as jnp
import numpy as np
from jax import lax

D = 8192
DV = 512
R = 16
TENANTS = 256
CAP = 2
TOK_DEV = 256
TOKENS = 4096


def level_of(rng, extent, pieces, least, largest):
    factor_of = 1.0
    for axis_at, shards_of in pieces:
        draws = jax.random.uniform(jax.random.fold_in(jax.random.fold_in(rng, 6), axis_at), (shards_of,), jnp.float32, least / len(pieces), largest / len(pieces))
        factor_of = factor_of * jnp.repeat(jnp.exp(draws), extent[axis_at] // shards_of).reshape((-1,) + (1,) * (len(extent) - 1 - axis_at))
    return factor_of


def deal_out(key, own, number, rows, number_of, top, bound, lean):
    ranking = jax.random.permutation(key, number_of)
    crowded, ordinary = load_shares(number_of, rows * top, bound, lean, True), load_shares(number_of, rows * top, bound, lean, False)
    places = jnp.arange(number_of)

    def named(tallies, turn):
        used = int((tallies > 0).sum())
        fixed = max(1, used // 4)
        shifted = fixed + (places - fixed + turn * (used - fixed)) % max(1, number_of - fixed)
        return jnp.zeros((number_of,), jnp.int32).at[ranking[jnp.where(places < fixed, places, shifted)]].set(jnp.asarray(tallies, jnp.int32))

    tallies = jnp.where(number % 4 == 0, named(crowded, number // 4), named(ordinary, number - number // 4 - 1))
    mixed = jax.random.permutation(jax.random.fold_in(own, 3), number_of)
    source_of, sink = mixed[0:number_of // 2 * 2:2], mixed[1:number_of // 2 * 2:2]
    slack = jnp.minimum(tallies[source_of] - 1, bound - tallies[sink]) // 2
    slack = jnp.where((source_of == ranking[0]) | (sink == ranking[0]) | (tallies[sink] == 0), 0, jnp.maximum(slack, 0))
    shifted = jax.random.randint(jax.random.fold_in(own, 4), (number_of // 2,), 0, 1 << 20) % (slack + 1)
    tallies = tallies.at[source_of].add(-shifted).at[sink].add(shifted)
    labels = jnp.searchsorted(jnp.cumsum(tallies), jnp.arange(rows * top), side="right").astype(jnp.int32)
    table = labels.reshape(top, rows).T
    table = table[jax.random.permutation(jax.random.fold_in(own, 1), rows)]
    turn = jax.random.randint(jax.random.fold_in(own, 2), (rows, 1), 0, top)
    return jnp.take_along_axis(table, (jnp.arange(top)[None, :] + turn) % top, axis=1)


def load_shares(count, total, bound, lean, full):
    portions = [(1 << 20) // math.isqrt(rank ** lean) + 1 for rank in range(1, count + 1)]
    largest = bound if full else min(bound, max(-(-total // count), total * portions[0] // sum(portions)))
    least = 1 if total - largest >= count - 1 else 0
    counts, rest = [largest] + [least] * (count - 1), total - largest - least * (count - 1)
    while rest > 0:
        candidates = [i for i in range(1, count) if counts[i] < largest] or [i for i in range(1, count) if counts[i] < bound]
        pool, budget = sum([portions[i] for i in candidates]), rest
        for i in candidates:
            addition = min(bound - counts[i], max(1, budget * portions[i] // pool), rest)
            counts[i] = counts[i] + addition
            rest = rest - addition
    return np.array(counts)


def normal_values(own_key, shape, width, most, cuts=(), kind=jnp.bfloat16):
    factor_of = level_of(own_key, shape, cuts, -0.22, 0.18) if cuts else 1.0
    values = jax.random.normal(own_key, shape, jnp.float32) * width * factor_of
    return jnp.minimum(jnp.maximum(values, -most), most).astype(kind)


def setup_inputs(seed: int = 0, part: int = 0) -> dict:
    keys = jax.random.split(jax.random.key(seed), 7)
    part_splits = jax.random.split(jax.random.fold_in(keys[6], part), 7)
    tokens = normal_values(part_splits[0], (TOKENS, D), 1.0, 6.0, ((0, 16),))
    value_weight = normal_values(keys[1], (D, DV), D ** -0.5, 0.0625)
    adapt_down = normal_values(part_splits[2], (TENANTS, D, R), D ** -0.5, 0.0625, ((0, 16),))
    adapt_up = normal_values(part_splits[3], (TENANTS, R, DV), R ** -0.5, 1.5, ((0, 16),))
    tenant_ids_keys = jax.random.split(jax.random.fold_in(part_splits[4], 1), TOKENS // TOK_DEV)
    tenant_ids_turns = jax.random.permutation(jax.random.fold_in(part_splits[4], 3), TOKENS // TOK_DEV)
    tenant_ids = jax.vmap(lambda own, number: deal_out(jax.random.fold_in(part_splits[4], 2), own, number, TOK_DEV, TENANTS, 1, CAP, 2))(tenant_ids_keys, tenant_ids_turns).reshape((TOKENS, 1))
    tenant_slot = jax.random.permutation(part_splits[5], TENANTS).astype(jnp.int32)
    return dict(tokens=tokens, value_weight=value_weight, adapt_down=adapt_down, adapt_up=adapt_up, tenant_ids=tenant_ids, tenant_slot=tenant_slot)


def reference(tokens, value_weight, adapt_down, adapt_up, tenant_ids, tenant_slot):
    base_value = jnp.dot(tokens, value_weight, preferred_element_type=jnp.float32)
    slot_index = tenant_slot[tenant_ids[:, 0]]
    block_count = tokens.shape[0] // TOK_DEV

    def adapt_block(packed):
        block_rows, block_slots = packed
        down_rows = adapt_down[block_slots].astype(jnp.float32)
        up_rows = adapt_up[block_slots].astype(jnp.float32)
        low_rank = jnp.einsum("td,tdr->tr", block_rows.astype(jnp.float32), down_rows).astype(jnp.bfloat16)
        return jnp.einsum("tr,tre->te", low_rank.astype(jnp.float32), up_rows).astype(jnp.bfloat16)

    adapter_delta = lax.map(adapt_block, (tokens.reshape(block_count, TOK_DEV, D), slot_index.reshape(block_count, TOK_DEV)))
    adapter_delta = adapter_delta.reshape(tokens.shape[0], DV)
    return (base_value + adapter_delta.astype(jnp.float32)).astype(jnp.bfloat16)
```

```python
import jax
import jax.numpy as jnp
import numpy as np
from jax import lax
from jax.experimental import pallas as pl
from jax.experimental.pallas import tpu as pltpu
from jax.sharding import PartitionSpec as P

TENANTS = 256
CAP = 2
PLANE = 4
SPARE = 12
STEP = 1024
ORDER = (1, 2, 3, 4, 8, 5, 9, 6, 10, 7, 11, 12, 13, 14, 15)


def adapt(rows, slots, first_slot, down, up):
    slot_count, _, rank = down.shape
    low_rank = jnp.einsum("td,ldr->tlr", rows, down, preferred_element_type=jnp.float32)
    own = (slots - first_slot)[:, None] == jnp.arange(slot_count, dtype=jnp.int32)[None, :]
    low_rank = jnp.where(own[:, :, None], low_rank, 0.0).astype(jnp.bfloat16)
    low_rank = low_rank.reshape(rows.shape[0], slot_count * rank)
    return jnp.dot(
        low_rank, up.reshape(slot_count * rank, up.shape[2]), preferred_element_type=jnp.float32
    ).astype(jnp.bfloat16)


def exchange(tokens, slot, owner, place, room, down, up):
    count = lax.axis_size("ad")
    local = down.shape[0]
    valid = (place >= 0) & (place < room)
    at = jnp.where(valid, owner * room + place, -1)
    hits = at[None, :] == jnp.arange(count * room, dtype=jnp.int32)[:, None]
    slots = jnp.sum(jnp.where(hits, slot[None, :] + 1, 0), axis=1) - 1
    pick = hits.astype(jnp.bfloat16)
    sent = jnp.dot(pick, tokens, preferred_element_type=jnp.float32).astype(jnp.bfloat16)
    sent = sent.reshape(count, room, tokens.shape[1])
    got = lax.all_to_all(sent, "ad", split_axis=0, concat_axis=0, tiled=True)
    got_slots = lax.all_to_all(
        slots.reshape(count, room), "ad", split_axis=0, concat_axis=0, tiled=True
    )
    delta = adapt(
        got.reshape(count * room, tokens.shape[1]),
        got_slots.reshape(count * room),
        lax.axis_index("ad") * local,
        down,
        up,
    )
    back = lax.all_to_all(
        delta.reshape(count, room, up.shape[2]), "ad", split_axis=0, concat_axis=0, tiled=True
    )
    return jnp.dot(
        pick.T, back.reshape(count * room, up.shape[2]), preferred_element_type=jnp.float32
    )


def pack_body(pick_ref, tokens_ref, *outs):
    packed = jnp.dot(
        pick_ref[...], tokens_ref[...], preferred_element_type=jnp.float32
    ).astype(jnp.bfloat16)
    at = 0
    for out in outs:
        out[...] = packed[at : at + out.shape[0]]
        at += out.shape[0]


def pack(pick, tokens, sizes):
    rows, depth = tokens.shape
    return pl.pallas_call(
        pack_body,
        grid=(depth // STEP,),
        in_specs=[
            pl.BlockSpec(pick.shape, lambda i: (0, 0)),
            pl.BlockSpec((rows, STEP), lambda i: (0, i)),
        ],
        out_specs=[pl.BlockSpec((size, STEP), lambda i: (0, i)) for size in sizes],
        out_shape=[jax.ShapeDtypeStruct((size, depth), jnp.bfloat16) for size in sizes],
        compiler_params=pltpu.CompilerParams(vmem_limit_bytes=32 * 2**20),
        cost_estimate=pl.CostEstimate(
            flops=2 * pick.shape[0] * rows * depth, bytes_accessed=10 * 2**20, transcendentals=0
        ),
    )(pick, tokens)


def swap(x, k):
    count = lax.axis_size("ad")
    return lax.ppermute(x, "ad", [(s, s ^ k) for s in range(count)])


def on_device(tokens, value_weight, adapt_down, adapt_up, tenant_ids, tenant_slot):
    row_count, depth = tokens.shape
    count = lax.axis_size("ad")
    me = lax.axis_index("ad")
    local = adapt_down.shape[0]
    width = adapt_up.shape[2]
    tenant = tenant_ids[:, 0]
    tenant_match = tenant[:, None] == jnp.arange(TENANTS, dtype=jnp.int32)[None, :]
    slot = jnp.sum(jnp.where(tenant_match, tenant_slot[None, :], 0), axis=1)
    owner = slot // local
    order = jnp.arange(row_count, dtype=jnp.int32)
    before = order[None, :] < order[:, None]
    place = jnp.sum(((owner[:, None] == owner[None, :]) & before).astype(jnp.int32), axis=1)
    base_value = jnp.dot(tokens, value_weight, preferred_element_type=jnp.float32)
    room = row_count // count
    planes = count // PLANE
    if room % 16 or count & (count - 1) or planes < 2:
        delta = exchange(tokens, slot, owner, place, CAP * local, adapt_down, adapt_up)
        return (base_value + delta).astype(jnp.bfloat16)

    block = owner ^ me
    plane = block // PLANE
    over = place >= room
    over_place = jnp.sum(
        (over[None, :] & (plane[:, None] == plane[None, :]) & before).astype(jnp.int32), axis=1
    )
    main_rows = count * room
    left = over & (over_place >= SPARE)
    at = jnp.where(over, main_rows + plane * SPARE + over_place, block * room + place)
    at = jnp.where(left, -1, at)
    sent_rows = main_rows + planes * SPARE
    hits = at[None, :] == jnp.arange(sent_rows, dtype=jnp.int32)[:, None]
    slots = jnp.sum(jnp.where(hits, slot[None, :] + 1, 0), axis=1) - 1
    left_any = jnp.max(left.astype(jnp.int32))
    notes = jnp.concatenate([slots, jnp.full((128 - sent_rows % 128,), left_any, jnp.int32)])
    notes = notes[None, :]

    *blocks, spare = pack(hits.astype(jnp.bfloat16), tokens, [room] * count + [planes * SPARE])
    spare = spare.reshape(planes, SPARE, depth)

    step = 1
    while step < count:
        notes = jnp.concatenate([notes, swap(notes, step)], axis=0)
        step *= 2

    along = [spare[0]]
    for b in range(1, planes):
        along.append(
            swap(spare[b].reshape(2 * SPARE, depth // 2), b * PLANE).reshape(SPARE, depth)
        )
    along = jnp.concatenate(along, axis=0)
    shared = [along] + [swap(along, a) for a in range(1, PLANE)]

    got = {0: blocks[0]}
    for k in ORDER:
        got[k] = swap(blocks[k], k)

    first = me * local
    over_delta = []
    for a in range(PLANE):
        over_slots = jnp.concatenate(
            [
                notes[a + PLANE * b, main_rows + b * SPARE : main_rows + (b + 1) * SPARE]
                for b in range(planes)
            ]
        )
        over_delta.append(adapt(shared[a], over_slots, first, adapt_down, adapt_up))
    back = {}
    for k in (0,) + ORDER:
        main = adapt(got[k], notes[k, k * room : (k + 1) * room], first, adapt_down, adapt_up)
        a, b = k % PLANE, k // PLANE
        rows = jnp.concatenate([main, over_delta[a][b * SPARE : (b + 1) * SPARE]], axis=0)
        back[k] = swap(rows, k) if k else rows
    back = jnp.concatenate([back[k] for k in range(count)], axis=0)
    came = []
    for k in range(count):
        came += [k * room + i for i in range(room)]
        came += [main_rows + (k // PLANE) * SPARE + i for i in range(SPARE)]
    unpick = (at[:, None] == jnp.asarray(np.array(came, np.int32))[None, :]).astype(jnp.bfloat16)
    delta = jnp.dot(unpick, back, preferred_element_type=jnp.float32)

    some_left = jnp.max(notes[:, sent_rows:])
    groups = lax.axis_size("grp")
    seen = some_left
    for g in range(1, groups):
        other = lax.ppermute(some_left, "grp", [(s, (s + g) % groups) for s in range(groups)])
        seen = jnp.maximum(seen, other)
    extra = lax.cond(
        seen > 0,
        lambda: exchange(
            tokens,
            slot,
            owner,
            jnp.where(left, place - room, -1),
            CAP * local - room,
            adapt_down,
            adapt_up,
        ),
        lambda: jnp.zeros((row_count, width), jnp.float32),
    )
    return (base_value + (delta + extra)).astype(jnp.bfloat16)


def solution(mesh):
    placed = (
        P(("grp", "ad"), None),
        P(),
        P(("grp", "ad"), None, None),
        P(("grp", "ad"), None, None),
        P(("grp", "ad"), None),
        P("grp"),
    )
    return jax.shard_map(
        on_device, mesh=mesh, in_specs=placed, out_specs=P(("grp", "ad"), None), check_vma=False
    )
```

```python
import functools

import jax
import jax.numpy as jnp
from jax import lax
from jax.experimental import pallas as pl
from jax.experimental.pallas import tpu as pltpu
from jax.sharding import PartitionSpec as P

TENANTS = 256
CAP = 2
PLANE = 4
SPARE = 12
NOTE = 128
STEP = 1024
FIRST = (1, 2, 3)
REST = (4, 8, 5, 9, 6, 10, 7, 11, 12, 13, 14, 15)
GROUPS = ((0, 1, 2, 3), (4, 8, 5, 9), (6, 10, 7, 11), (12, 13), (14, 15))
VMEM = pl.BlockSpec(memory_space=pltpu.VMEM)
SMEM = pl.BlockSpec(memory_space=pltpu.SMEM)


def exchange(tokens, slot, owner, place, room, down, up):
    count = lax.axis_size("ad")
    local, depth, rank = down.shape
    width = up.shape[2]
    at = jnp.where((place >= 0) & (place < room), owner * room + place, -1)
    hits = at[None, :] == jnp.arange(count * room, dtype=jnp.int32)[:, None]
    slots = jnp.sum(jnp.where(hits, slot[None, :] + 1, 0), axis=1) - 1
    pick = hits.astype(jnp.bfloat16)
    sent = jnp.dot(pick, tokens, preferred_element_type=jnp.float32).astype(jnp.bfloat16)
    got = lax.all_to_all(
        sent.reshape(count, room, depth), "ad", split_axis=0, concat_axis=0, tiled=True
    ).reshape(count * room, depth)
    got_slots = lax.all_to_all(
        slots.reshape(count, room), "ad", split_axis=0, concat_axis=0, tiled=True
    ).reshape(count * room)
    low_rank = jnp.einsum("td,ldr->tlr", got, down, preferred_element_type=jnp.float32)
    own = (got_slots - lax.axis_index("ad") * local)[:, None] == jnp.arange(local)[None, :]
    low_rank = jnp.where(own[:, :, None], low_rank, 0.0).astype(jnp.bfloat16)
    delta = jnp.dot(
        low_rank.reshape(count * room, local * rank),
        up.reshape(local * rank, width),
        preferred_element_type=jnp.float32,
    ).astype(jnp.bfloat16)
    back = lax.all_to_all(
        delta.reshape(count, room, width), "ad", split_axis=0, concat_axis=0, tiled=True
    )
    return jnp.dot(
        pick.T, back.reshape(count * room, width), preferred_element_type=jnp.float32
    )


def one_hot(at, starts, size):
    ids = [lax.broadcasted_iota(jnp.int32, (size, at.shape[1]), 0) + s for s in starts]
    return (jnp.concatenate(ids, axis=0) == at).astype(jnp.float32).astype(jnp.bfloat16)


def pack_over_body(main_rows, planes, at_ref, info_ref, tokens_ref, *outs):
    at = at_ref[...]
    half = tokens_ref.shape[1] // 2
    row = lax.broadcasted_iota(jnp.int32, (2 * SPARE, at.shape[1]), 0)
    upper = row >= SPARE
    ids = jnp.where(upper, row - SPARE, row)
    ids = jnp.concatenate([ids + main_rows + b * SPARE for b in range(planes)], axis=0)
    upper = jnp.concatenate([upper] * planes, axis=0)
    hit = ids == at
    left = (hit & ~upper).astype(jnp.float32).astype(jnp.bfloat16)
    right = (hit & upper).astype(jnp.float32).astype(jnp.bfloat16)
    both = hit.astype(jnp.float32).astype(jnp.bfloat16)

    def put(value, columns):
        for b in range(planes):
            outs[b][:, columns] = value[2 * SPARE * b : 2 * SPARE * (b + 1)].astype(jnp.bfloat16)

    for c in range(0, half, STEP):
        put(
            jnp.dot(left, tokens_ref[:, c : c + STEP], preferred_element_type=jnp.float32)
            + jnp.dot(
                right, tokens_ref[:, half + c : half + c + STEP], preferred_element_type=jnp.float32
            ),
            slice(c, c + STEP),
        )
    put(
        jnp.dot(both, info_ref[...], preferred_element_type=jnp.float32), slice(half, half + NOTE)
    )


def pack_body(starts, at_ref, info_ref, tokens_ref, *outs):
    depth = tokens_ref.shape[1]
    size = outs[0].shape[0]
    pick = one_hot(at_ref[...], starts, size)

    def put(value, columns):
        for j, out in enumerate(outs):
            out[:, columns] = value[size * j : size * (j + 1)].astype(jnp.bfloat16)

    for c in range(0, depth, STEP):
        put(
            jnp.dot(pick, tokens_ref[:, c : c + STEP], preferred_element_type=jnp.float32),
            slice(c, c + STEP),
        )
    put(
        jnp.dot(pick, info_ref[...], preferred_element_type=jnp.float32), slice(depth, depth + NOTE)
    )


def low_delta(low, note, first, rank, up):
    column = lax.broadcasted_iota(jnp.int32, low.shape, 1) // rank + (first + 1)
    low = jnp.where(note.astype(jnp.float32) == column.astype(jnp.float32), low, 0.0)
    return jnp.dot(low.astype(jnp.bfloat16), up, preferred_element_type=jnp.float32)


def adapt_body(keys, rank, first_ref, down_ref, up_ref, *refs):
    rows_refs, over_refs = refs[: len(keys)], refs[len(keys) : -len(keys)]
    outs = refs[-len(keys) :]
    depth = down_ref.shape[1]
    size = rows_refs[0].shape[0]
    low = jnp.zeros((size * len(keys), down_ref.shape[0]), jnp.float32)
    for c in range(0, depth, STEP):
        rows = jnp.concatenate([r[:, c : c + STEP] for r in rows_refs], axis=0)
        low += lax.dot_general(
            rows,
            down_ref[:, c : c + STEP],
            (((1,), (1,)), ((), ())),
            preferred_element_type=jnp.float32,
        )
    note = jnp.concatenate([r[:, depth : depth + NOTE] for r in rows_refs], axis=0)[:, :1]
    delta = low_delta(low, note, first_ref[0], rank, up_ref[...]).astype(jnp.bfloat16)
    for j, k in enumerate(keys):
        outs[j][:size] = delta[size * j : size * (j + 1)]
        outs[j][size:] = over_refs[k % PLANE][16 * (k // PLANE) : 16 * (k // PLANE + 1)]


def adapt_over_body(planes, rank, first_ref, down_ref, up_ref, *refs):
    rows_refs, outs = refs[:PLANE], refs[PLANE:]
    half = down_ref.shape[1] // 2
    for rows_ref, out in zip(rows_refs, outs, strict=True):
        shape = (rows_ref.shape[0], down_ref.shape[0])
        low0, low1 = jnp.zeros(shape, jnp.float32), jnp.zeros(shape, jnp.float32)
        for c in range(0, half, STEP):
            rows = rows_ref[:, c : c + STEP]
            dims = (((1,), (1,)), ((), ()))
            low0 += lax.dot_general(
                rows, down_ref[:, c : c + STEP], dims, preferred_element_type=jnp.float32
            )
            low1 += lax.dot_general(
                rows,
                down_ref[:, half + c : half + c + STEP],
                dims,
                preferred_element_type=jnp.float32,
            )
        note = rows_ref[:, half : half + NOTE].astype(jnp.float32)
        zeros = jnp.zeros((16 - SPARE, shape[1]), jnp.float32)
        no_note = jnp.zeros((16 - SPARE, NOTE), jnp.float32)
        lows, notes = [], []
        for b in range(planes):
            s = 2 * SPARE * b
            lows += [low0[s : s + SPARE] + low1[s + SPARE : s + 2 * SPARE], zeros]
            notes += [note[s : s + SPARE], no_note]
        low = jnp.concatenate(lows, axis=0)
        note = jnp.concatenate(notes, axis=0)[:, :1]
        out[...] = low_delta(low, note, first_ref[0], rank, up_ref[...]).astype(jnp.bfloat16)


def final_body(room, main_rows, at_ref, base_ref, *refs):
    *backs, out = refs
    back = jnp.concatenate([b[...] for b in backs], axis=0)
    size = backs[0].shape[0]
    shape = (back.shape[0], at_ref.shape[1])
    row = lax.broadcasted_iota(jnp.int32, shape, 0)
    k, i = row // size, row % size
    spare = main_rows + (k // PLANE) * SPARE + (i - room)
    came = jnp.where(i < room, k * room + i, jnp.where(i < room + SPARE, spare, -2))
    pick = (came == at_ref[...]).astype(jnp.float32).astype(jnp.bfloat16)
    delta = lax.dot_general(
        pick, back, (((0,), (0,)), ((), ())), preferred_element_type=jnp.float32
    )
    out[...] = (base_ref[...] + delta).astype(jnp.bfloat16)


def call(body, outs, args, specs, flops, moved):
    return pl.pallas_call(
        body,
        in_specs=specs,
        out_specs=[VMEM] * len(outs),
        out_shape=[jax.ShapeDtypeStruct(s, jnp.bfloat16) for s in outs],
        compiler_params=pltpu.CompilerParams(vmem_limit_bytes=40 * 2**20),
        cost_estimate=pl.CostEstimate(flops=flops, bytes_accessed=moved, transcendentals=0),
    )(*args)


def swap(x, k):
    count = lax.axis_size("ad")
    return lax.ppermute(x, "ad", [(s, s ^ k) for s in range(count)])


def on_device(tokens, value_weight, adapt_down, adapt_up, tenant_ids, tenant_slot):
    row_count, depth = tokens.shape
    count = lax.axis_size("ad")
    me = lax.axis_index("ad")
    local, _, rank = adapt_down.shape
    width = adapt_up.shape[2]
    tenant = tenant_ids[:, 0]
    tenant_match = tenant[:, None] == jnp.arange(TENANTS, dtype=jnp.int32)[None, :]
    slot = jnp.sum(jnp.where(tenant_match, tenant_slot[None, :], 0), axis=1)
    owner = slot // local
    order = jnp.arange(row_count, dtype=jnp.int32)
    before = order[None, :] < order[:, None]
    place = jnp.sum(((owner[:, None] == owner[None, :]) & before).astype(jnp.int32), axis=1)
    base_value = jnp.dot(tokens, value_weight, preferred_element_type=jnp.float32)
    room = row_count // count
    planes = count // PLANE
    if count != 16 or room != 16:
        delta = exchange(tokens, slot, owner, place, CAP * local, adapt_down, adapt_up)
        return (base_value + delta).astype(jnp.bfloat16)

    block = owner ^ me
    plane = block // PLANE
    over = place >= room
    over_place = jnp.sum(
        (over[None, :] & (plane[:, None] == plane[None, :]) & before).astype(jnp.int32), axis=1
    )
    main_rows = count * room
    left = over & (over_place >= SPARE)
    at = jnp.where(over, main_rows + plane * SPARE + over_place, block * room + place)
    at = jnp.where(left, -1, at)[None, :]
    info = jnp.where(jnp.arange(NOTE)[None, :] == 0, slot[:, None] + 1, 0).astype(jnp.bfloat16)
    some_left = jnp.max(left.astype(jnp.int32))

    spare = call(
        functools.partial(pack_over_body, main_rows, planes),
        [(2 * SPARE, depth // 2 + NOTE)] * planes,
        (at, info, tokens),
        [VMEM] * 3,
        2 * 96 * row_count * depth,
        6 * 2**20,
    )
    blocks = {}
    for keys in (FIRST, (0,) + REST):
        made = call(
            functools.partial(pack_body, [k * room for k in keys]),
            [(room, depth + NOTE)] * len(keys),
            (at, info, tokens),
            [VMEM] * 3,
            2 * len(keys) * room * row_count * depth,
            8 * 2**20,
        )
        blocks.update(zip(keys, made, strict=True))

    along = jnp.concatenate(
        [spare[0]] + [swap(spare[b], b * PLANE) for b in range(1, planes)], axis=0
    )
    shared = [along] + [swap(along, a) for a in range(1, PLANE)]

    got = {0: blocks[0]}
    for k in FIRST + REST:
        got[k] = swap(blocks[k], k)

    seen = some_left
    for g in range(1, lax.axis_size("grp")):
        groups = lax.axis_size("grp")
        other = lax.ppermute(some_left, "grp", [(s, (s + g) % groups) for s in range(groups)])
        seen = jnp.maximum(seen, other)
    step = 1
    while step < count:
        seen = jnp.maximum(seen, swap(seen, step))
        step *= 2

    first = (me * local).reshape(1)
    down = adapt_down.transpose(0, 2, 1).reshape(local * rank, depth)
    up = adapt_up.reshape(local * rank, width)
    over_delta = call(
        functools.partial(adapt_over_body, planes, rank),
        [(16 * planes, width)] * PLANE,
        (first, down, up, *shared),
        [SMEM] + [VMEM] * 6,
        2 * 384 * depth * local * rank,
        6 * 2**20,
    )
    back = {}
    for keys in GROUPS:
        made = call(
            functools.partial(adapt_body, keys, rank),
            [(room + 16, width)] * len(keys),
            (first, down, up, *[got[k] for k in keys], *over_delta),
            [SMEM] + [VMEM] * (2 + len(keys) + PLANE),
            2 * room * len(keys) * depth * local * rank,
            6 * 2**20,
        )
        for k, rows in zip(keys, made, strict=True):
            back[k] = swap(rows, k) if k else rows
    back = [back[k] for k in range(count)]

    def finish(base):
        return call(
            functools.partial(final_body, room, main_rows),
            [(row_count, width)],
            (at, base, *back),
            [VMEM] * (2 + count),
            2 * row_count * width * 512,
            2**20,
        )[0]

    def more():
        extra = exchange(
            tokens,
            slot,
            owner,
            jnp.where(left, place - room, -1),
            CAP * local - room,
            adapt_down,
            adapt_up,
        )
        return finish(base_value + extra)

    return lax.cond(seen > 0, more, lambda: finish(base_value))


def solution(mesh):
    placed = (
        P(("grp", "ad"), None),
        P(),
        P(("grp", "ad"), None, None),
        P(("grp", "ad"), None, None),
        P(("grp", "ad"), None),
        P("grp"),
    )
    return jax.shard_map(
        on_device, mesh=mesh, in_specs=placed, out_specs=P(("grp", "ad"), None), check_vma=False
    )
```

```python
import functools

import jax
import jax.numpy as jnp
from jax import lax
from jax.experimental import pallas as pl
from jax.experimental.pallas import tpu as pltpu
from jax.sharding import PartitionSpec as P

TENANTS = 256
CAP = 2
PLANE = 4
SPARE = 12
NOTE = 128
STEP = 1024
VMEM = pl.BlockSpec(memory_space=pltpu.VMEM)
SMEM = pl.BlockSpec(memory_space=pltpu.SMEM)


def exchange(tokens, slot, owner, place, room, down, up):
    count = lax.axis_size("ad")
    local, depth, rank = down.shape
    width = up.shape[2]
    at = jnp.where((place >= 0) & (place < room), owner * room + place, -1)
    hits = at[None, :] == jnp.arange(count * room, dtype=jnp.int32)[:, None]
    slots = jnp.sum(jnp.where(hits, slot[None, :] + 1, 0), axis=1) - 1
    pick = hits.astype(jnp.bfloat16)
    sent = jnp.dot(pick, tokens, preferred_element_type=jnp.float32).astype(jnp.bfloat16)
    got = lax.all_to_all(
        sent.reshape(count, room, depth), "ad", split_axis=0, concat_axis=0, tiled=True
    ).reshape(count * room, depth)
    got_slots = lax.all_to_all(
        slots.reshape(count, room), "ad", split_axis=0, concat_axis=0, tiled=True
    ).reshape(count * room)
    low_rank = jnp.einsum("td,ldr->tlr", got, down, preferred_element_type=jnp.float32)
    own = (got_slots - lax.axis_index("ad") * local)[:, None] == jnp.arange(local)[None, :]
    low_rank = jnp.where(own[:, :, None], low_rank, 0.0).astype(jnp.bfloat16)
    delta = jnp.dot(
        low_rank.reshape(count * room, local * rank),
        up.reshape(local * rank, width),
        preferred_element_type=jnp.float32,
    ).astype(jnp.bfloat16)
    back = lax.all_to_all(
        delta.reshape(count, room, width), "ad", split_axis=0, concat_axis=0, tiled=True
    )
    return jnp.dot(
        pick.T, back.reshape(count * room, width), preferred_element_type=jnp.float32
    )


def pack_over_body(main_rows, planes, at_ref, info_ref, tokens_ref, *outs):
    at = at_ref[...]
    half = tokens_ref.shape[1] // 2
    row = lax.broadcasted_iota(jnp.int32, (2 * SPARE, at.shape[1]), 0)
    upper = row >= SPARE
    ids = jnp.where(upper, row - SPARE, row)
    ids = jnp.concatenate([ids + main_rows + b * SPARE for b in range(planes)], axis=0)
    upper = jnp.concatenate([upper] * planes, axis=0)
    hit = ids == at
    left = (hit & ~upper).astype(jnp.float32).astype(jnp.bfloat16)
    right = (hit & upper).astype(jnp.float32).astype(jnp.bfloat16)
    both = hit.astype(jnp.float32).astype(jnp.bfloat16)

    def put(value, columns):
        for b in range(planes):
            outs[b][:, columns] = value[2 * SPARE * b : 2 * SPARE * (b + 1)].astype(jnp.bfloat16)

    for c in range(0, half, STEP):
        put(
            jnp.dot(left, tokens_ref[:, c : c + STEP], preferred_element_type=jnp.float32)
            + jnp.dot(
                right, tokens_ref[:, half + c : half + c + STEP], preferred_element_type=jnp.float32
            ),
            slice(c, c + STEP),
        )
    put(
        jnp.dot(both, info_ref[...], preferred_element_type=jnp.float32), slice(half, half + NOTE)
    )


def pack_body(flag_ref, at_ref, info_ref, tokens_ref, out):
    depth = tokens_ref.shape[1]
    shape = (out.shape[0], at_ref.shape[1])
    pick = lax.broadcasted_iota(jnp.int32, shape, 0) == at_ref[...]
    pick = pick.astype(jnp.float32).astype(jnp.bfloat16)
    for c in range(0, depth, STEP):
        out[:, c : c + STEP] = jnp.dot(
            pick, tokens_ref[:, c : c + STEP], preferred_element_type=jnp.float32
        ).astype(jnp.bfloat16)
    note = jnp.dot(pick, info_ref[...], preferred_element_type=jnp.float32)
    flag = jnp.where(
        lax.broadcasted_iota(jnp.int32, note.shape, 1) == 1, flag_ref[0].astype(jnp.float32), 0.0
    )
    out[:, depth : depth + NOTE] = (note + flag).astype(jnp.bfloat16)


def low_delta(low, note, first, rank, up):
    column = lax.broadcasted_iota(jnp.int32, low.shape, 1) // rank + (first + 1)
    low = jnp.where(note.astype(jnp.float32) == column.astype(jnp.float32), low, 0.0)
    return jnp.dot(low.astype(jnp.bfloat16), up, preferred_element_type=jnp.float32)


def adapt_body(rank, first_ref, down_ref, up_ref, rows_ref, out, flag_out):
    depth = down_ref.shape[1]
    low = jnp.zeros((rows_ref.shape[0], down_ref.shape[0]), jnp.float32)
    for c in range(0, depth, STEP):
        low += lax.dot_general(
            rows_ref[:, c : c + STEP],
            down_ref[:, c : c + STEP],
            (((1,), (1,)), ((), ())),
            preferred_element_type=jnp.float32,
        )
    note = rows_ref[:, depth : depth + NOTE].astype(jnp.float32)
    out[...] = low_delta(low, note[:, :1], first_ref[0], rank, up_ref[...]).astype(jnp.bfloat16)
    most = jnp.max(note, axis=0, keepdims=True)
    flag_out[...] = jnp.broadcast_to(most, flag_out.shape).astype(jnp.bfloat16)


def adapt_over_body(planes, rank, first_ref, down_ref, up_ref, *refs):
    rows_refs, outs = refs[:PLANE], refs[PLANE:]
    half = down_ref.shape[1] // 2
    for rows_ref, out in zip(rows_refs, outs, strict=True):
        shape = (rows_ref.shape[0], down_ref.shape[0])
        low0, low1 = jnp.zeros(shape, jnp.float32), jnp.zeros(shape, jnp.float32)
        for c in range(0, half, STEP):
            rows = rows_ref[:, c : c + STEP]
            dims = (((1,), (1,)), ((), ()))
            low0 += lax.dot_general(
                rows, down_ref[:, c : c + STEP], dims, preferred_element_type=jnp.float32
            )
            low1 += lax.dot_general(
                rows,
                down_ref[:, half + c : half + c + STEP],
                dims,
                preferred_element_type=jnp.float32,
            )
        note = rows_ref[:, half : half + NOTE].astype(jnp.float32)
        zeros = jnp.zeros((16 - SPARE, shape[1]), jnp.float32)
        no_note = jnp.zeros((16 - SPARE, NOTE), jnp.float32)
        lows, notes = [], []
        for b in range(planes):
            s = 2 * SPARE * b
            lows += [low0[s : s + SPARE] + low1[s + SPARE : s + 2 * SPARE], zeros]
            notes += [note[s : s + SPARE], no_note]
        low = jnp.concatenate(lows, axis=0)
        note = jnp.concatenate(notes, axis=0)[:, :1]
        out[...] = low_delta(low, note, first_ref[0], rank, up_ref[...]).astype(jnp.bfloat16)


def final_body(at_ref, base_ref, back_ref, *refs):
    *overs, out = refs
    back = jnp.concatenate([back_ref[...]] + [o[...] for o in overs], axis=0)
    main_rows, size = back_ref.shape[0], overs[0].shape[0]
    row = lax.broadcasted_iota(jnp.int32, (back.shape[0], at_ref.shape[1]), 0)
    b, i = (row - main_rows) // size, (row - main_rows) % size
    spare = jnp.where(i < SPARE, main_rows + b * SPARE + i, -2)
    pick = jnp.where(row < main_rows, row, spare) == at_ref[...]
    pick = pick.astype(jnp.float32).astype(jnp.bfloat16)
    delta = lax.dot_general(
        pick, back, (((0,), (0,)), ((), ())), preferred_element_type=jnp.float32
    )
    out[...] = (base_ref[...] + delta).astype(jnp.bfloat16)


def call(body, outs, args, specs, flops, moved):
    return pl.pallas_call(
        body,
        in_specs=specs,
        out_specs=[VMEM] * len(outs),
        out_shape=[jax.ShapeDtypeStruct(s, jnp.bfloat16) for s in outs],
        compiler_params=pltpu.CompilerParams(vmem_limit_bytes=40 * 2**20),
        cost_estimate=pl.CostEstimate(flops=flops, bytes_accessed=moved, transcendentals=0),
    )(*args)


def swap(x, k):
    count = lax.axis_size("ad")
    return lax.ppermute(x, "ad", [(s, s ^ k) for s in range(count)])


def on_device(tokens, value_weight, adapt_down, adapt_up, tenant_ids, tenant_slot):
    row_count, depth = tokens.shape
    count = lax.axis_size("ad")
    me = lax.axis_index("ad")
    local, _, rank = adapt_down.shape
    width = adapt_up.shape[2]
    tenant = tenant_ids[:, 0]
    tenant_match = tenant[:, None] == jnp.arange(TENANTS, dtype=jnp.int32)[None, :]
    slot = jnp.sum(jnp.where(tenant_match, tenant_slot[None, :], 0), axis=1)
    owner = slot // local
    order = jnp.arange(row_count, dtype=jnp.int32)
    before = order[None, :] < order[:, None]
    place = jnp.sum(((owner[:, None] == owner[None, :]) & before).astype(jnp.int32), axis=1)
    base_value = jnp.dot(tokens, value_weight, preferred_element_type=jnp.float32)
    room = row_count // count
    planes = count // PLANE
    if count != 16 or room != 16:
        delta = exchange(tokens, slot, owner, place, CAP * local, adapt_down, adapt_up)
        return (base_value + delta).astype(jnp.bfloat16)

    plane = (owner ^ me) // PLANE
    over = place >= room
    over_place = jnp.sum(
        (over[None, :] & (plane[:, None] == plane[None, :]) & before).astype(jnp.int32), axis=1
    )
    main_rows = count * room
    left = over & (over_place >= SPARE)
    at = jnp.where(over, main_rows + plane * SPARE + over_place, owner * room + place)
    at = jnp.where(left, -1, at)[None, :]
    info = jnp.where(jnp.arange(NOTE)[None, :] == 0, slot[:, None] + 1, 0).astype(jnp.bfloat16)
    some_left = jnp.max(left.astype(jnp.int32)).reshape(1)

    spare = call(
        functools.partial(pack_over_body, main_rows, planes),
        [(2 * SPARE, depth // 2 + NOTE)] * planes,
        (at, info, tokens),
        [VMEM] * 3,
        2 * 96 * row_count * depth,
        6 * 2**20,
    )
    blocks = call(
        pack_body,
        [(main_rows, depth + NOTE)],
        (some_left, at, info, tokens),
        [SMEM] + [VMEM] * 3,
        2 * main_rows * row_count * depth,
        8 * 2**20,
    )[0]

    got = lax.all_to_all(
        blocks.reshape(count, room, depth + NOTE), "ad", split_axis=0, concat_axis=0, tiled=True
    ).reshape(main_rows, depth + NOTE)

    first = (me * local).reshape(1)
    down = adapt_down.transpose(0, 2, 1).reshape(local * rank, depth)
    up = adapt_up.reshape(local * rank, width)

    along = jnp.concatenate(
        [spare[0]] + [swap(spare[b], b * PLANE) for b in range(1, planes)], axis=0
    )
    shared = [along] + [swap(along, a) for a in range(1, PLANE)]
    over_delta = call(
        functools.partial(adapt_over_body, planes, rank),
        [(16 * planes, width)] * PLANE,
        (first, down, up, *shared),
        [SMEM] + [VMEM] * 6,
        2 * 384 * depth * local * rank,
        6 * 2**20,
    )
    over_sum = over_delta[0]
    for a in range(1, PLANE):
        over_sum = over_sum + swap(over_delta[a], a)
    over_back = [over_sum[:16]]
    for b in range(1, planes):
        over_back.append(swap(over_sum[16 * b : 16 * (b + 1)], b * PLANE))

    delta, flags = call(
        functools.partial(adapt_body, rank),
        [(main_rows, width), (16, NOTE)],
        (first, down, up, got),
        [SMEM] + [VMEM] * 3,
        2 * main_rows * depth * local * rank,
        8 * 2**20,
    )
    back = lax.all_to_all(
        delta.reshape(count, room, width), "ad", split_axis=0, concat_axis=0, tiled=True
    ).reshape(main_rows, width)

    some_left = flags[0, 1].astype(jnp.int32)
    seen = some_left
    groups = lax.axis_size("grp")
    for g in range(1, groups):
        other = lax.ppermute(some_left, "grp", [(s, (s + g) % groups) for s in range(groups)])
        seen = jnp.maximum(seen, other)

    def finish(base):
        return call(
            final_body,
            [(row_count, width)],
            (at, base, back, *over_back),
            [VMEM] * (3 + planes),
            2 * row_count * width * 320,
            2**20,
        )[0]

    def more():
        extra = exchange(
            tokens,
            slot,
            owner,
            jnp.where(left, place - room, -1),
            CAP * local - room,
            adapt_down,
            adapt_up,
        )
        return finish(base_value + extra)

    return lax.cond(seen > 0, more, lambda: finish(base_value))


def solution(mesh):
    placed = (
        P(("grp", "ad"), None),
        P(),
        P(("grp", "ad"), None, None),
        P(("grp", "ad"), None, None),
        P(("grp", "ad"), None),
        P("grp"),
    )
    return jax.shard_map(
        on_device, mesh=mesh, in_specs=placed, out_specs=P(("grp", "ad"), None), check_vma=False
    )
```

```python
import functools

import jax
import jax.numpy as jnp
from jax import lax
from jax.experimental import pallas as pl
from jax.experimental.pallas import tpu as pltpu
from jax.sharding import PartitionSpec as P

TENANTS = 256
CAP = 2
PLANE = 4
SPARE = 12
NOTE = 128
STEP = 1024
WIDE = 1664
VMEM = pl.BlockSpec(memory_space=pltpu.VMEM)
SMEM = pl.BlockSpec(memory_space=pltpu.SMEM)


def exchange(tokens, slot, owner, place, room, down, up):
    count = lax.axis_size("ad")
    local, depth, rank = down.shape
    width = up.shape[2]
    at = jnp.where((place >= 0) & (place < room), owner * room + place, -1)
    hits = at[None, :] == jnp.arange(count * room, dtype=jnp.int32)[:, None]
    slots = jnp.sum(jnp.where(hits, slot[None, :] + 1, 0), axis=1) - 1
    pick = hits.astype(jnp.bfloat16)
    sent = jnp.dot(pick, tokens, preferred_element_type=jnp.float32).astype(jnp.bfloat16)
    got = lax.all_to_all(
        sent.reshape(count, room, depth), "ad", split_axis=0, concat_axis=0, tiled=True
    ).reshape(count * room, depth)
    got_slots = lax.all_to_all(
        slots.reshape(count, room), "ad", split_axis=0, concat_axis=0, tiled=True
    ).reshape(count * room)
    low_rank = jnp.einsum("td,ldr->tlr", got, down, preferred_element_type=jnp.float32)
    own = (got_slots - lax.axis_index("ad") * local)[:, None] == jnp.arange(local)[None, :]
    low_rank = jnp.where(own[:, :, None], low_rank, 0.0).astype(jnp.bfloat16)
    delta = jnp.dot(
        low_rank.reshape(count * room, local * rank),
        up.reshape(local * rank, width),
        preferred_element_type=jnp.float32,
    ).astype(jnp.bfloat16)
    back = lax.all_to_all(
        delta.reshape(count, room, width), "ad", split_axis=0, concat_axis=0, tiled=True
    )
    return jnp.dot(
        pick.T, back.reshape(count * room, width), preferred_element_type=jnp.float32
    )


def pack_over_body(main_rows, planes, at_ref, info_ref, tokens_ref, *outs):
    at = at_ref[...]
    half = tokens_ref.shape[1] // 2
    row = lax.broadcasted_iota(jnp.int32, (2 * SPARE, at.shape[1]), 0)
    upper = row >= SPARE
    ids = jnp.where(upper, row - SPARE, row)
    ids = jnp.concatenate([ids + main_rows + b * SPARE for b in range(planes)], axis=0)
    upper = jnp.concatenate([upper] * planes, axis=0)
    hit = ids == at
    left = (hit & ~upper).astype(jnp.float32).astype(jnp.bfloat16)
    right = (hit & upper).astype(jnp.float32).astype(jnp.bfloat16)
    both = hit.astype(jnp.float32).astype(jnp.bfloat16)

    def put(value, columns):
        for b in range(planes):
            outs[b][:, columns] = value[2 * SPARE * b : 2 * SPARE * (b + 1)].astype(jnp.bfloat16)

    for c in range(0, half, STEP):
        put(
            jnp.dot(left, tokens_ref[:, c : c + STEP], preferred_element_type=jnp.float32)
            + jnp.dot(
                right, tokens_ref[:, half + c : half + c + STEP], preferred_element_type=jnp.float32
            ),
            slice(c, c + STEP),
        )
    put(
        jnp.dot(both, info_ref[...], preferred_element_type=jnp.float32), slice(half, half + NOTE)
    )


def pack_body(last, flag_ref, at_ref, info_ref, tokens_ref, out):
    shape = (out.shape[0], at_ref.shape[1])
    pick = lax.broadcasted_iota(jnp.int32, shape, 0) == at_ref[...]
    pick = pick.astype(jnp.float32).astype(jnp.bfloat16)

    @pl.when(pl.program_id(0) < pl.num_programs(0) - 1)
    def _():
        out[...] = jnp.dot(
            pick, tokens_ref[...], preferred_element_type=jnp.float32
        ).astype(jnp.bfloat16)

    @pl.when(pl.program_id(0) == pl.num_programs(0) - 1)
    def _():
        out[:, :last] = jnp.dot(
            pick, tokens_ref[:, :last], preferred_element_type=jnp.float32
        ).astype(jnp.bfloat16)
        note = jnp.dot(pick, info_ref[...], preferred_element_type=jnp.float32)
        column = lax.broadcasted_iota(jnp.int32, note.shape, 1)
        flag = jnp.where(column == 1, flag_ref[0].astype(jnp.float32), 0.0)
        out[:, last:] = (note + flag).astype(jnp.bfloat16)


def pack(main_rows, some_left, at, info, tokens):
    rows, depth = tokens.shape
    steps = (depth + NOTE) // WIDE
    return pl.pallas_call(
        functools.partial(pack_body, WIDE - NOTE),
        grid=(steps,),
        in_specs=[
            SMEM,
            pl.BlockSpec(at.shape, lambda i: (0, 0)),
            pl.BlockSpec(info.shape, lambda i: (0, 0)),
            pl.BlockSpec((rows, WIDE), lambda i: (0, i)),
        ],
        out_specs=pl.BlockSpec((main_rows, WIDE), lambda i: (0, i)),
        out_shape=jax.ShapeDtypeStruct((main_rows, depth + NOTE), jnp.bfloat16),
        compiler_params=pltpu.CompilerParams(vmem_limit_bytes=56 * 2**20),
        cost_estimate=pl.CostEstimate(
            flops=2 * main_rows * rows * depth, bytes_accessed=8 * 2**20, transcendentals=0
        ),
    )(some_left, at, info, tokens)


def low_delta(low, note, first, rank, up):
    column = lax.broadcasted_iota(jnp.int32, low.shape, 1) // rank + (first + 1)
    low = jnp.where(note.astype(jnp.float32) == column.astype(jnp.float32), low, 0.0)
    return jnp.dot(low.astype(jnp.bfloat16), up, preferred_element_type=jnp.float32)


def adapt_body(rank, last, first_ref, down_ref, up_ref, rows_ref, out, flag_out, low_ref):
    step = pl.program_id(0)

    def product(columns):
        return lax.dot_general(
            rows_ref[:, columns],
            down_ref[:, columns],
            (((1,), (1,)), ((), ())),
            preferred_element_type=jnp.float32,
        )

    @pl.when(step == 0)
    def _():
        low_ref[...] = product(slice(None))

    @pl.when((step > 0) & (step < pl.num_programs(0) - 1))
    def _():
        low_ref[...] += product(slice(None))

    @pl.when(step == pl.num_programs(0) - 1)
    def _():
        low = low_ref[...] + product(slice(0, last))
        note = rows_ref[:, last:].astype(jnp.float32)
        delta = low_delta(low, note[:, :1], first_ref[0], rank, up_ref[...])
        out[...] = delta.astype(jnp.bfloat16)
        most = jnp.max(note, axis=0, keepdims=True)
        flag_out[...] = jnp.broadcast_to(most, flag_out.shape).astype(jnp.bfloat16)


def adapt(rank, first, down, up, got):
    rows, width = got.shape[0], up.shape[1]
    return pl.pallas_call(
        functools.partial(adapt_body, rank, WIDE - NOTE),
        grid=(got.shape[1] // WIDE,),
        in_specs=[
            SMEM,
            pl.BlockSpec((down.shape[0], WIDE), lambda i: (0, i)),
            pl.BlockSpec(up.shape, lambda i: (0, 0)),
            pl.BlockSpec((rows, WIDE), lambda i: (0, i)),
        ],
        out_specs=[
            pl.BlockSpec((rows, width), lambda i: (0, 0)),
            pl.BlockSpec((16, NOTE), lambda i: (0, 0)),
        ],
        out_shape=[
            jax.ShapeDtypeStruct((rows, width), jnp.bfloat16),
            jax.ShapeDtypeStruct((16, NOTE), jnp.bfloat16),
        ],
        scratch_shapes=[pltpu.VMEM((rows, down.shape[0]), jnp.float32)],
        compiler_params=pltpu.CompilerParams(vmem_limit_bytes=24 * 2**20),
        cost_estimate=pl.CostEstimate(
            flops=2 * rows * down.size, bytes_accessed=8 * 2**20, transcendentals=0
        ),
    )(first, down, up, got)


def adapt_over_body(planes, rank, first_ref, down_ref, up_ref, *refs):
    rows_refs, outs = refs[:PLANE], refs[PLANE:]
    half = down_ref.shape[1] // 2
    each = rows_refs[0].shape[0]
    shape = (PLANE * each, down_ref.shape[0])
    dims = (((1,), (1,)), ((), ()))
    low0, low1 = jnp.zeros(shape, jnp.float32), jnp.zeros(shape, jnp.float32)
    for c in range(0, half, STEP):
        rows = jnp.concatenate([r[:, c : c + STEP] for r in rows_refs], axis=0)
        low0 += lax.dot_general(
            rows, down_ref[:, c : c + STEP], dims, preferred_element_type=jnp.float32
        )
        low1 += lax.dot_general(
            rows, down_ref[:, half + c : half + c + STEP], dims, preferred_element_type=jnp.float32
        )
    zeros = jnp.zeros((16 - SPARE, shape[1]), jnp.float32)
    no_note = jnp.zeros((16 - SPARE, NOTE), jnp.float32)
    lows, notes = [], []
    for a in range(PLANE):
        note = rows_refs[a][:, half : half + NOTE].astype(jnp.float32)
        for b in range(planes):
            s = 2 * SPARE * b
            m = a * each + s
            lows += [low0[m : m + SPARE] + low1[m + SPARE : m + 2 * SPARE], zeros]
            notes += [note[s : s + SPARE], no_note]
    low = jnp.concatenate(lows, axis=0)
    note = jnp.concatenate(notes, axis=0)[:, :1]
    delta = low_delta(low, note, first_ref[0], rank, up_ref[...]).astype(jnp.bfloat16)
    for a, out in enumerate(outs):
        out[...] = delta[16 * planes * a : 16 * planes * (a + 1)]


def final_body(at_ref, base_ref, back_ref, *refs):
    *overs, out = refs
    back = jnp.concatenate([back_ref[...]] + [o[...] for o in overs], axis=0)
    main_rows, size = back_ref.shape[0], overs[0].shape[0]
    row = lax.broadcasted_iota(jnp.int32, (back.shape[0], at_ref.shape[1]), 0)
    b, i = (row - main_rows) // size, (row - main_rows) % size
    spare = jnp.where(i < SPARE, main_rows + b * SPARE + i, -2)
    pick = jnp.where(row < main_rows, row, spare) == at_ref[...]
    pick = pick.astype(jnp.float32).astype(jnp.bfloat16)
    delta = lax.dot_general(
        pick, back, (((0,), (0,)), ((), ())), preferred_element_type=jnp.float32
    )
    out[...] = (base_ref[...] + delta).astype(jnp.bfloat16)


def call(body, outs, args, specs, flops, moved):
    return pl.pallas_call(
        body,
        in_specs=specs,
        out_specs=[VMEM] * len(outs),
        out_shape=[jax.ShapeDtypeStruct(s, jnp.bfloat16) for s in outs],
        compiler_params=pltpu.CompilerParams(vmem_limit_bytes=40 * 2**20),
        cost_estimate=pl.CostEstimate(flops=flops, bytes_accessed=moved, transcendentals=0),
    )(*args)


def swap(x, k):
    count = lax.axis_size("ad")
    return lax.ppermute(x, "ad", [(s, s ^ k) for s in range(count)])


def on_device(tokens, value_weight, adapt_down, adapt_up, tenant_ids, tenant_slot):
    row_count, depth = tokens.shape
    count = lax.axis_size("ad")
    me = lax.axis_index("ad")
    local, _, rank = adapt_down.shape
    width = adapt_up.shape[2]
    tenant = tenant_ids[:, 0]
    tenant_match = tenant[:, None] == jnp.arange(TENANTS, dtype=jnp.int32)[None, :]
    slot = jnp.sum(jnp.where(tenant_match, tenant_slot[None, :], 0), axis=1)
    owner = slot // local
    order = jnp.arange(row_count, dtype=jnp.int32)
    before = order[None, :] < order[:, None]
    place = jnp.sum(((owner[:, None] == owner[None, :]) & before).astype(jnp.int32), axis=1)
    base_value = jnp.dot(tokens, value_weight, preferred_element_type=jnp.float32)
    room = row_count // count
    planes = count // PLANE
    if count != 16 or room != 16 or (depth + NOTE) % WIDE:
        delta = exchange(tokens, slot, owner, place, CAP * local, adapt_down, adapt_up)
        return (base_value + delta).astype(jnp.bfloat16)

    plane = (owner ^ me) // PLANE
    over = place >= room
    over_place = jnp.sum(
        (over[None, :] & (plane[:, None] == plane[None, :]) & before).astype(jnp.int32), axis=1
    )
    main_rows = count * room
    left = over & (over_place >= SPARE)
    at = jnp.where(over, main_rows + plane * SPARE + over_place, owner * room + place)
    at = jnp.where(left, -1, at)[None, :]
    info = jnp.where(jnp.arange(NOTE)[None, :] == 0, slot[:, None] + 1, 0).astype(jnp.bfloat16)
    some_left = jnp.max(left.astype(jnp.int32)).reshape(1)

    spare = call(
        functools.partial(pack_over_body, main_rows, planes),
        [(2 * SPARE, depth // 2 + NOTE)] * planes,
        (at, info, tokens),
        [VMEM] * 3,
        2 * 96 * row_count * depth,
        6 * 2**20,
    )
    blocks = pack(main_rows, some_left, at, info, tokens)

    first = (me * local).reshape(1)
    down = adapt_down.transpose(0, 2, 1).reshape(local * rank, depth)
    up = adapt_up.reshape(local * rank, width)

    along = jnp.concatenate(
        [spare[0]] + [swap(spare[b], b * PLANE) for b in range(1, planes)], axis=0
    )
    shared = [along] + [swap(along, a) for a in range(1, PLANE)]
    blocks, shared[1] = lax.optimization_barrier((blocks, shared[1]))
    got = lax.all_to_all(
        blocks.reshape(count, room, depth + NOTE), "ad", split_axis=0, concat_axis=0, tiled=True
    ).reshape(main_rows, depth + NOTE)

    over_delta = call(
        functools.partial(adapt_over_body, planes, rank),
        [(16 * planes, width)] * PLANE,
        (first, down, up, *shared),
        [SMEM] + [VMEM] * 6,
        2 * 384 * depth * local * rank,
        6 * 2**20,
    )
    over_sum = over_delta[0]
    for a in range(1, PLANE):
        over_sum = over_sum + swap(over_delta[a], a)
    over_back = [over_sum[:16]]
    for b in range(1, planes):
        over_back.append(swap(over_sum[16 * b : 16 * (b + 1)], b * PLANE))

    delta, flags = adapt(rank, first, down, up, got)
    back = lax.all_to_all(
        delta.reshape(count, room, width), "ad", split_axis=0, concat_axis=0, tiled=True
    ).reshape(main_rows, width)

    some_left = flags[0, 1].astype(jnp.int32)
    seen = some_left
    groups = lax.axis_size("grp")
    for g in range(1, groups):
        other = lax.ppermute(some_left, "grp", [(s, (s + g) % groups) for s in range(groups)])
        seen = jnp.maximum(seen, other)

    def finish(base):
        return call(
            final_body,
            [(row_count, width)],
            (at, base, back, *over_back),
            [VMEM] * (3 + planes),
            2 * row_count * width * 320,
            2**20,
        )[0]

    def more():
        extra = exchange(
            tokens,
            slot,
            owner,
            jnp.where(left, place - room, -1),
            CAP * local - room,
            adapt_down,
            adapt_up,
        )
        return finish(base_value + extra)

    return lax.cond(seen > 0, more, lambda: finish(base_value))


def solution(mesh):
    placed = (
        P(("grp", "ad"), None),
        P(),
        P(("grp", "ad"), None, None),
        P(("grp", "ad"), None, None),
        P(("grp", "ad"), None),
        P("grp"),
    )
    return jax.shard_map(
        on_device, mesh=mesh, in_specs=placed, out_specs=P(("grp", "ad"), None), check_vma=False
    )
```

```python
import functools

import jax
import jax.numpy as jnp
from jax import lax
from jax.experimental import pallas as pl
from jax.experimental.pallas import tpu as pltpu
from jax.sharding import PartitionSpec as P

TENANTS = 256
CAP = 2
PLANE = 4
SPARE = 12
NOTE = 128
STEP = 1024
WIDE = 1664
VMEM = pl.BlockSpec(memory_space=pltpu.VMEM)
SMEM = pl.BlockSpec(memory_space=pltpu.SMEM)


def exchange(tokens, slot, owner, place, room, down, up):
    count = lax.axis_size("ad")
    local, depth, rank = down.shape
    width = up.shape[2]
    at = jnp.where((place >= 0) & (place < room), owner * room + place, -1)
    hits = at[None, :] == jnp.arange(count * room, dtype=jnp.int32)[:, None]
    slots = jnp.sum(jnp.where(hits, slot[None, :] + 1, 0), axis=1) - 1
    pick = hits.astype(jnp.bfloat16)
    sent = jnp.dot(pick, tokens, preferred_element_type=jnp.float32).astype(jnp.bfloat16)
    got = lax.all_to_all(
        sent.reshape(count, room, depth), "ad", split_axis=0, concat_axis=0, tiled=True
    ).reshape(count * room, depth)
    got_slots = lax.all_to_all(
        slots.reshape(count, room), "ad", split_axis=0, concat_axis=0, tiled=True
    ).reshape(count * room)
    low_rank = jnp.einsum("td,ldr->tlr", got, down, preferred_element_type=jnp.float32)
    own = (got_slots - lax.axis_index("ad") * local)[:, None] == jnp.arange(local)[None, :]
    low_rank = jnp.where(own[:, :, None], low_rank, 0.0).astype(jnp.bfloat16)
    delta = jnp.dot(
        low_rank.reshape(count * room, local * rank),
        up.reshape(local * rank, width),
        preferred_element_type=jnp.float32,
    ).astype(jnp.bfloat16)
    back = lax.all_to_all(
        delta.reshape(count, room, width), "ad", split_axis=0, concat_axis=0, tiled=True
    )
    return jnp.dot(
        pick.T, back.reshape(count * room, width), preferred_element_type=jnp.float32
    )


def pack_over_body(main_rows, planes, at_ref, info_ref, tokens_hbm, *refs):
    *outs, tokens_ref, sems = refs
    half = tokens_ref.shape[1] // 2
    spans = [slice(h + c, h + c + STEP) for c in range(0, half, STEP) for h in (0, half)]
    copies = [
        pltpu.make_async_copy(tokens_hbm.at[:, span], tokens_ref.at[:, span], sems.at[i])
        for i, span in enumerate(spans)
    ]
    for copy in copies:
        copy.start()
    at = at_ref[...]
    row = lax.broadcasted_iota(jnp.int32, (2 * SPARE, at.shape[1]), 0)
    upper = row >= SPARE
    ids = jnp.where(upper, row - SPARE, row)
    ids = jnp.concatenate([ids + main_rows + b * SPARE for b in range(planes)], axis=0)
    upper = jnp.concatenate([upper] * planes, axis=0)
    hit = ids == at
    left = (hit & ~upper).astype(jnp.float32).astype(jnp.bfloat16)
    right = (hit & upper).astype(jnp.float32).astype(jnp.bfloat16)
    both = hit.astype(jnp.float32).astype(jnp.bfloat16)

    def put(value, columns):
        for b in range(planes):
            outs[b][:, columns] = value[2 * SPARE * b : 2 * SPARE * (b + 1)].astype(jnp.bfloat16)

    for i, c in enumerate(range(0, half, STEP)):
        copies[2 * i].wait()
        copies[2 * i + 1].wait()
        put(
            jnp.dot(left, tokens_ref[:, c : c + STEP], preferred_element_type=jnp.float32)
            + jnp.dot(
                right, tokens_ref[:, half + c : half + c + STEP], preferred_element_type=jnp.float32
            ),
            slice(c, c + STEP),
        )
    put(
        jnp.dot(both, info_ref[...], preferred_element_type=jnp.float32), slice(half, half + NOTE)
    )


def pack_body(last, flag_ref, at_ref, info_ref, tokens_ref, out):
    shape = (out.shape[0], at_ref.shape[1])
    pick = lax.broadcasted_iota(jnp.int32, shape, 0) == at_ref[...]
    pick = pick.astype(jnp.float32).astype(jnp.bfloat16)

    @pl.when(pl.program_id(0) < pl.num_programs(0) - 1)
    def _():
        out[...] = jnp.dot(
            pick, tokens_ref[...], preferred_element_type=jnp.float32
        ).astype(jnp.bfloat16)

    @pl.when(pl.program_id(0) == pl.num_programs(0) - 1)
    def _():
        out[:, :last] = jnp.dot(
            pick, tokens_ref[:, :last], preferred_element_type=jnp.float32
        ).astype(jnp.bfloat16)
        note = jnp.dot(pick, info_ref[...], preferred_element_type=jnp.float32)
        column = lax.broadcasted_iota(jnp.int32, note.shape, 1)
        flag = jnp.where(column == 1, flag_ref[0].astype(jnp.float32), 0.0)
        out[:, last:] = (note + flag).astype(jnp.bfloat16)


def pack(main_rows, some_left, at, info, tokens):
    rows, depth = tokens.shape
    steps = (depth + NOTE) // WIDE
    return pl.pallas_call(
        functools.partial(pack_body, WIDE - NOTE),
        grid=(steps,),
        in_specs=[
            SMEM,
            pl.BlockSpec(at.shape, lambda i: (0, 0)),
            pl.BlockSpec(info.shape, lambda i: (0, 0)),
            pl.BlockSpec((rows, WIDE), lambda i: (0, i)),
        ],
        out_specs=pl.BlockSpec((main_rows, WIDE), lambda i: (0, i)),
        out_shape=jax.ShapeDtypeStruct((main_rows, depth + NOTE), jnp.bfloat16),
        compiler_params=pltpu.CompilerParams(vmem_limit_bytes=56 * 2**20),
        cost_estimate=pl.CostEstimate(
            flops=2 * main_rows * rows * depth, bytes_accessed=8 * 2**20, transcendentals=0
        ),
    )(some_left, at, info, tokens)


def low_delta(low, note, first, rank, up):
    column = lax.broadcasted_iota(jnp.int32, low.shape, 1) // rank + (first + 1)
    low = jnp.where(note.astype(jnp.float32) == column.astype(jnp.float32), low, 0.0)
    return jnp.dot(low.astype(jnp.bfloat16), up, preferred_element_type=jnp.float32)


def adapt_body(rank, first_ref, down_ref, up_ref, rows_hbm, out, flag_out, rows_ref, sems):
    depth = down_ref.shape[1]
    spans = [slice(c, min(c + WIDE, depth + NOTE)) for c in range(0, depth + NOTE, WIDE)]
    copies = [
        pltpu.make_async_copy(rows_hbm.at[:, span], rows_ref.at[:, span], sems.at[i])
        for i, span in enumerate(spans)
    ]
    for copy in copies:
        copy.start()
    low = jnp.zeros((rows_ref.shape[0], down_ref.shape[0]), jnp.float32)
    for copy, span in zip(copies, spans, strict=True):
        copy.wait()
        span = slice(span.start, min(span.stop, depth))
        low += lax.dot_general(
            rows_ref[:, span],
            down_ref[:, span],
            (((1,), (1,)), ((), ())),
            preferred_element_type=jnp.float32,
        )
    note = rows_ref[:, depth:].astype(jnp.float32)
    out[...] = low_delta(low, note[:, :1], first_ref[0], rank, up_ref[...]).astype(jnp.bfloat16)
    most = jnp.max(note, axis=0, keepdims=True)
    flag_out[...] = jnp.broadcast_to(most, flag_out.shape).astype(jnp.bfloat16)


def adapt(rank, first, down, up, got):
    rows, width = got.shape[0], up.shape[1]
    return pl.pallas_call(
        functools.partial(adapt_body, rank),
        in_specs=[SMEM, VMEM, VMEM, pl.BlockSpec(memory_space=pl.ANY)],
        out_specs=[VMEM, VMEM],
        out_shape=[
            jax.ShapeDtypeStruct((rows, width), jnp.bfloat16),
            jax.ShapeDtypeStruct((16, NOTE), jnp.bfloat16),
        ],
        scratch_shapes=[
            pltpu.VMEM(got.shape, jnp.bfloat16),
            pltpu.SemaphoreType.DMA((pl.cdiv(got.shape[1], WIDE),)),
        ],
        compiler_params=pltpu.CompilerParams(vmem_limit_bytes=24 * 2**20),
        cost_estimate=pl.CostEstimate(
            flops=2 * rows * down.size, bytes_accessed=8 * 2**20, transcendentals=0
        ),
    )(first, down, up, got)


def adapt_over_body(planes, rank, first_ref, down_ref, up_ref, *refs):
    rows_refs, outs = refs[:PLANE], refs[PLANE:]
    half = down_ref.shape[1] // 2
    each = rows_refs[0].shape[0]
    shape = (PLANE * each, down_ref.shape[0])
    dims = (((1,), (1,)), ((), ()))
    low0, low1 = jnp.zeros(shape, jnp.float32), jnp.zeros(shape, jnp.float32)
    for c in range(0, half, STEP):
        rows = jnp.concatenate([r[:, c : c + STEP] for r in rows_refs], axis=0)
        low0 += lax.dot_general(
            rows, down_ref[:, c : c + STEP], dims, preferred_element_type=jnp.float32
        )
        low1 += lax.dot_general(
            rows, down_ref[:, half + c : half + c + STEP], dims, preferred_element_type=jnp.float32
        )
    zeros = jnp.zeros((16 - SPARE, shape[1]), jnp.float32)
    no_note = jnp.zeros((16 - SPARE, NOTE), jnp.float32)
    lows, notes = [], []
    for a in range(PLANE):
        note = rows_refs[a][:, half : half + NOTE].astype(jnp.float32)
        for b in range(planes):
            s = 2 * SPARE * b
            m = a * each + s
            lows += [low0[m : m + SPARE] + low1[m + SPARE : m + 2 * SPARE], zeros]
            notes += [note[s : s + SPARE], no_note]
    low = jnp.concatenate(lows, axis=0)
    note = jnp.concatenate(notes, axis=0)[:, :1]
    delta = low_delta(low, note, first_ref[0], rank, up_ref[...]).astype(jnp.bfloat16)
    for a, out in enumerate(outs):
        out[...] = delta[16 * planes * a : 16 * planes * (a + 1)]


def final_body(at_ref, base_ref, back_ref, *refs):
    *overs, out = refs
    back = jnp.concatenate([back_ref[...]] + [o[...] for o in overs], axis=0)
    main_rows, size = back_ref.shape[0], overs[0].shape[0]
    row = lax.broadcasted_iota(jnp.int32, (back.shape[0], at_ref.shape[1]), 0)
    b, i = (row - main_rows) // size, (row - main_rows) % size
    spare = jnp.where(i < SPARE, main_rows + b * SPARE + i, -2)
    pick = jnp.where(row < main_rows, row, spare) == at_ref[...]
    pick = pick.astype(jnp.float32).astype(jnp.bfloat16)
    delta = lax.dot_general(
        pick, back, (((0,), (0,)), ((), ())), preferred_element_type=jnp.float32
    )
    out[...] = (base_ref[...] + delta).astype(jnp.bfloat16)


def call(body, outs, args, specs, flops, moved, scratch=()):
    return pl.pallas_call(
        body,
        in_specs=specs,
        out_specs=[VMEM] * len(outs),
        out_shape=[jax.ShapeDtypeStruct(s, jnp.bfloat16) for s in outs],
        scratch_shapes=list(scratch),
        compiler_params=pltpu.CompilerParams(vmem_limit_bytes=40 * 2**20),
        cost_estimate=pl.CostEstimate(flops=flops, bytes_accessed=moved, transcendentals=0),
    )(*args)


def swap(x, k):
    count = lax.axis_size("ad")
    return lax.ppermute(x, "ad", [(s, s ^ k) for s in range(count)])


def on_device(tokens, value_weight, adapt_down, adapt_up, tenant_ids, tenant_slot):
    row_count, depth = tokens.shape
    count = lax.axis_size("ad")
    me = lax.axis_index("ad")
    local, _, rank = adapt_down.shape
    width = adapt_up.shape[2]
    tenant = tenant_ids[:, 0]
    tenant_match = tenant[:, None] == jnp.arange(TENANTS, dtype=jnp.int32)[None, :]
    slot = jnp.sum(jnp.where(tenant_match, tenant_slot[None, :], 0), axis=1)
    owner = slot // local
    order = jnp.arange(row_count, dtype=jnp.int32)
    before = order[None, :] < order[:, None]
    place = jnp.sum(((owner[:, None] == owner[None, :]) & before).astype(jnp.int32), axis=1)
    base_value = jnp.dot(tokens, value_weight, preferred_element_type=jnp.float32)
    room = row_count // count
    planes = count // PLANE
    if count != 16 or room != 16 or (depth + NOTE) % WIDE:
        delta = exchange(tokens, slot, owner, place, CAP * local, adapt_down, adapt_up)
        return (base_value + delta).astype(jnp.bfloat16)

    plane = (owner ^ me) // PLANE
    over = place >= room
    over_place = jnp.sum(
        (over[None, :] & (plane[:, None] == plane[None, :]) & before).astype(jnp.int32), axis=1
    )
    main_rows = count * room
    left = over & (over_place >= SPARE)
    at = jnp.where(over, main_rows + plane * SPARE + over_place, owner * room + place)
    at = jnp.where(left, -1, at)[None, :]
    info = jnp.where(jnp.arange(NOTE)[None, :] == 0, slot[:, None] + 1, 0).astype(jnp.bfloat16)
    some_left = jnp.max(left.astype(jnp.int32)).reshape(1)
    groups = lax.axis_size("grp")
    seen = some_left
    for g in range(1, groups):
        other = lax.ppermute(some_left, "grp", [(s, (s + g) % groups) for s in range(groups)])
        seen = jnp.maximum(seen, other)

    spare = call(
        functools.partial(pack_over_body, main_rows, planes),
        [(2 * SPARE, depth // 2 + NOTE)] * planes,
        (at, info, tokens),
        [VMEM, VMEM, pl.BlockSpec(memory_space=pl.ANY)],
        2 * 96 * row_count * depth,
        6 * 2**20,
        [pltpu.VMEM(tokens.shape, jnp.bfloat16), pltpu.SemaphoreType.DMA((depth // STEP,))],
    )
    blocks = pack(main_rows, seen, at, info, tokens)

    first = (me * local).reshape(1)
    down = adapt_down.transpose(0, 2, 1).reshape(local * rank, depth)
    up = adapt_up.reshape(local * rank, width)

    along = jnp.concatenate(
        [spare[0]] + [swap(spare[b], b * PLANE) for b in range(1, planes)], axis=0
    )
    along, blocks, base_value = lax.optimization_barrier((along, blocks, base_value))
    shared = [along] + [swap(along, a) for a in range(1, PLANE)]
    blocks, shared[1] = lax.optimization_barrier((blocks, shared[1]))
    got = lax.all_to_all(
        blocks.reshape(count, room, depth + NOTE), "ad", split_axis=0, concat_axis=0, tiled=True
    ).reshape(main_rows, depth + NOTE)

    over_delta = call(
        functools.partial(adapt_over_body, planes, rank),
        [(16 * planes, width)] * PLANE,
        (first, down, up, *shared),
        [SMEM] + [VMEM] * 6,
        4 * 10**14,
        6 * 2**20,
    )
    over_sum = over_delta[0]
    for a in range(1, PLANE):
        over_sum = over_sum + swap(over_delta[a], a)
    over_back = [over_sum[:16]]
    for b in range(1, planes):
        over_back.append(swap(over_sum[16 * b : 16 * (b + 1)], b * PLANE))

    delta, flags = adapt(rank, first, down, up, got)
    back = lax.all_to_all(
        delta.reshape(count, room, width), "ad", split_axis=0, concat_axis=0, tiled=True
    ).reshape(main_rows, width)

    def finish(base):
        return call(
            final_body,
            [(row_count, width)],
            (at, base, back, *over_back),
            [VMEM] * (3 + planes),
            2 * row_count * width * 320,
            2**20,
        )[0]

    def more():
        extra = exchange(
            tokens,
            slot,
            owner,
            jnp.where(left, place - room, -1),
            CAP * local - room,
            adapt_down,
            adapt_up,
        )
        return finish(base_value + extra)

    return lax.cond(flags[0, 1] > 0, more, lambda: finish(base_value))


def solution(mesh):
    placed = (
        P(("grp", "ad"), None),
        P(),
        P(("grp", "ad"), None, None),
        P(("grp", "ad"), None, None),
        P(("grp", "ad"), None),
        P("grp"),
    )
    return jax.shard_map(
        on_device, mesh=mesh, in_specs=placed, out_specs=P(("grp", "ad"), None), check_vma=False
    )
```

```python
import functools

import jax
import jax.numpy as jnp
from jax import lax
from jax.experimental import pallas as pl
from jax.experimental.pallas import tpu as pltpu
from jax.sharding import PartitionSpec as P

TENANTS = 256
CAP = 2
PLANE = 4
SPARE = 12
NOTE = 128
STEP = 1024
WIDE = 1664
VMEM = pl.BlockSpec(memory_space=pltpu.VMEM)
ANY = pl.BlockSpec(memory_space=pl.ANY)
SMEM = pl.BlockSpec(memory_space=pltpu.SMEM)


def exchange(tokens, slot, owner, place, room, down, up):
    count = lax.axis_size("ad")
    local, depth, rank = down.shape
    width = up.shape[2]
    at = jnp.where((place >= 0) & (place < room), owner * room + place, -1)
    hits = at[None, :] == jnp.arange(count * room, dtype=jnp.int32)[:, None]
    slots = jnp.sum(jnp.where(hits, slot[None, :] + 1, 0), axis=1) - 1
    pick = hits.astype(jnp.bfloat16)
    sent = jnp.dot(pick, tokens, preferred_element_type=jnp.float32).astype(jnp.bfloat16)
    got = lax.all_to_all(
        sent.reshape(count, room, depth), "ad", split_axis=0, concat_axis=0, tiled=True
    ).reshape(count * room, depth)
    got_slots = lax.all_to_all(
        slots.reshape(count, room), "ad", split_axis=0, concat_axis=0, tiled=True
    ).reshape(count * room)
    low_rank = jnp.einsum("td,ldr->tlr", got, down, preferred_element_type=jnp.float32)
    own = (got_slots - lax.axis_index("ad") * local)[:, None] == jnp.arange(local)[None, :]
    low_rank = jnp.where(own[:, :, None], low_rank, 0.0).astype(jnp.bfloat16)
    delta = jnp.dot(
        low_rank.reshape(count * room, local * rank),
        up.reshape(local * rank, width),
        preferred_element_type=jnp.float32,
    ).astype(jnp.bfloat16)
    back = lax.all_to_all(
        delta.reshape(count, room, width), "ad", split_axis=0, concat_axis=0, tiled=True
    )
    return jnp.dot(
        pick.T, back.reshape(count * room, width), preferred_element_type=jnp.float32
    )


def one_hot(hit):
    return hit.astype(jnp.float32).astype(jnp.bfloat16)


def earlier(hit, until):
    counts = jnp.dot(one_hot(hit), until, preferred_element_type=jnp.float32)
    return jnp.sum(jnp.where(hit, counts, 0.0), axis=0, keepdims=True).astype(jnp.int32)


def route_body(room, local, me_ref, tenant_ref, slot_ref, tokens_hbm, *refs):
    *outs, at_ref, note_ref, left_ref, tokens_ref, sems = refs
    half = tokens_ref.shape[1] // 2
    spans = [slice(h + c, h + c + STEP) for c in range(0, half, STEP) for h in (0, half)]
    copies = [
        pltpu.make_async_copy(tokens_hbm.at[:, span], tokens_ref.at[:, span], sems.at[i])
        for i, span in enumerate(spans)
    ]
    for copy in copies:
        copy.start()
    tenant = tenant_ref[...]
    rows = tenant.shape[1]
    planes = len(outs)
    main_rows = planes * PLANE * room

    def iota(size, axis=0):
        return lax.broadcasted_iota(jnp.int32, (size, rows), axis)

    table = jnp.broadcast_to(slot_ref[...].astype(jnp.float32), (16, TENANTS)).astype(jnp.bfloat16)
    slot = jnp.dot(table, one_hot(iota(TENANTS) == tenant), preferred_element_type=jnp.float32)[:1]
    owner = slot.astype(jnp.int32) // local
    until = one_hot(iota(rows) < iota(rows, 1))
    place = earlier(iota(planes * PLANE) == owner, until)
    plane = (owner ^ me_ref[0]) // PLANE
    over = place >= room
    over_place = earlier((iota(16) == plane) & over, until)
    left = over & (over_place >= SPARE)
    at = jnp.where(over, main_rows + plane * SPARE + over_place, owner * room + place)
    at = jnp.where(left, -1, at)
    at_ref[...] = at
    most = jnp.max(left.astype(jnp.float32), axis=1, keepdims=True).astype(jnp.int32)
    left_ref[...] = jnp.broadcast_to(most, left_ref.shape)
    note = jnp.where(iota(NOTE) == 0, slot + 1.0, 0.0).astype(jnp.bfloat16)
    note_ref[...] = note

    row = iota(2 * SPARE)
    upper = row >= SPARE
    ids = jnp.where(upper, row - SPARE, row)
    ids = jnp.concatenate([ids + main_rows + b * SPARE for b in range(planes)], axis=0)
    upper = jnp.concatenate([upper] * planes, axis=0)
    hit = ids == at
    first, second = one_hot(hit & ~upper), one_hot(hit & upper)

    def put(value, columns):
        for b in range(planes):
            outs[b][:, columns] = value[2 * SPARE * b : 2 * SPARE * (b + 1)].astype(jnp.bfloat16)

    put(notes_of(one_hot(hit), note), slice(half, half + NOTE))
    for i, c in enumerate(range(0, half, STEP)):
        copies[2 * i].wait()
        copies[2 * i + 1].wait()
        put(
            jnp.dot(first, tokens_ref[:, c : c + STEP], preferred_element_type=jnp.float32)
            + jnp.dot(
                second,
                tokens_ref[:, half + c : half + c + STEP],
                preferred_element_type=jnp.float32,
            ),
            slice(c, c + STEP),
        )


def notes_of(pick, note):
    return lax.dot_general(
        pick, note, (((1,), (1,)), ((), ())), preferred_element_type=jnp.float32
    )


def pack_body(last, flag_ref, at_ref, note_ref, tokens_ref, out):
    shape = (out.shape[0], at_ref.shape[1])
    pick = lax.broadcasted_iota(jnp.int32, shape, 0) == at_ref[...]
    pick = pick.astype(jnp.float32).astype(jnp.bfloat16)

    @pl.when(pl.program_id(0) < pl.num_programs(0) - 1)
    def _():
        out[...] = jnp.dot(
            pick, tokens_ref[...], preferred_element_type=jnp.float32
        ).astype(jnp.bfloat16)

    @pl.when(pl.program_id(0) == pl.num_programs(0) - 1)
    def _():
        out[:, :last] = jnp.dot(
            pick, tokens_ref[:, :last], preferred_element_type=jnp.float32
        ).astype(jnp.bfloat16)
        note = notes_of(pick, note_ref[...])
        column = lax.broadcasted_iota(jnp.int32, note.shape, 1)
        flag = jnp.where(column == 1, flag_ref[...].astype(jnp.float32), 0.0)
        out[:, last:] = (note + flag).astype(jnp.bfloat16)


def pack(main_rows, flag, at, note, tokens):
    rows, depth = tokens.shape
    steps = (depth + NOTE) // WIDE
    return pl.pallas_call(
        functools.partial(pack_body, WIDE - NOTE),
        grid=(steps,),
        in_specs=[
            pl.BlockSpec(flag.shape, lambda i: (0, 0)),
            pl.BlockSpec(at.shape, lambda i: (0, 0)),
            pl.BlockSpec(note.shape, lambda i: (0, 0)),
            pl.BlockSpec((rows, WIDE), lambda i: (0, i)),
        ],
        out_specs=pl.BlockSpec((main_rows, WIDE), lambda i: (0, i)),
        out_shape=jax.ShapeDtypeStruct((main_rows, depth + NOTE), jnp.bfloat16),
        compiler_params=pltpu.CompilerParams(vmem_limit_bytes=56 * 2**20),
        cost_estimate=pl.CostEstimate(
            flops=2 * main_rows * rows * depth, bytes_accessed=8 * 2**20, transcendentals=0
        ),
    )(flag, at, note, tokens)


def low_delta(low, note, first, rank, up):
    column = lax.broadcasted_iota(jnp.int32, low.shape, 1) // rank + (first + 1)
    low = jnp.where(note.astype(jnp.float32) == column.astype(jnp.float32), low, 0.0)
    return jnp.dot(low.astype(jnp.bfloat16), up, preferred_element_type=jnp.float32)


def adapt_body(rank, first_ref, down_hbm, up_ref, rows_hbm, out, flag_out, *scratch):
    down_ref, rows_ref, down_sems, sems = scratch
    depth = down_ref.shape[1]
    spans = [slice(c, min(c + WIDE, depth + NOTE)) for c in range(0, depth + NOTE, WIDE)]
    copies = []
    for i, span in enumerate(spans):
        kept = slice(span.start, min(span.stop, depth))
        copies.append(
            (
                pltpu.make_async_copy(rows_hbm.at[:, span], rows_ref.at[:, span], sems.at[i]),
                pltpu.make_async_copy(down_hbm.at[:, kept], down_ref.at[:, kept], down_sems.at[i]),
            )
        )
    for pair in copies:
        pair[0].start()
        pair[1].start()
    low = jnp.zeros((rows_ref.shape[0], down_ref.shape[0]), jnp.float32)
    for pair, span in zip(copies, spans, strict=True):
        pair[0].wait()
        pair[1].wait()
        span = slice(span.start, min(span.stop, depth))
        low += lax.dot_general(
            rows_ref[:, span],
            down_ref[:, span],
            (((1,), (1,)), ((), ())),
            preferred_element_type=jnp.float32,
        )
    note = rows_ref[:, depth:].astype(jnp.float32)
    out[...] = low_delta(low, note[:, :1], first_ref[0], rank, up_ref[...]).astype(jnp.bfloat16)
    most = jnp.max(note, axis=0, keepdims=True)
    flag_out[...] = jnp.broadcast_to(most, flag_out.shape).astype(jnp.bfloat16)


def adapt(rank, first, down, up, got):
    rows, width = got.shape[0], up.shape[1]
    return pl.pallas_call(
        functools.partial(adapt_body, rank),
        in_specs=[SMEM, ANY, VMEM, ANY],
        out_specs=[VMEM, VMEM],
        out_shape=[
            jax.ShapeDtypeStruct((rows, width), jnp.bfloat16),
            jax.ShapeDtypeStruct((16, NOTE), jnp.bfloat16),
        ],
        scratch_shapes=[
            pltpu.VMEM(down.shape, jnp.bfloat16),
            pltpu.VMEM(got.shape, jnp.bfloat16),
            pltpu.SemaphoreType.DMA((pl.cdiv(got.shape[1], WIDE),)),
            pltpu.SemaphoreType.DMA((pl.cdiv(got.shape[1], WIDE),)),
        ],
        compiler_params=pltpu.CompilerParams(vmem_limit_bytes=24 * 2**20),
        cost_estimate=pl.CostEstimate(
            flops=2 * rows * down.size, bytes_accessed=8 * 2**20, transcendentals=0
        ),
    )(first, down, up, got)


def adapt_over_body(planes, rank, first_ref, down_hbm, up_ref, *refs):
    rows_refs, outs = refs[:PLANE], refs[PLANE : 2 * PLANE]
    down_ref, sems = refs[2 * PLANE :]
    half = down_ref.shape[1] // 2
    spans = [slice(h + c, h + c + STEP) for c in range(0, half, STEP) for h in (0, half)]
    copies = [
        pltpu.make_async_copy(down_hbm.at[:, span], down_ref.at[:, span], sems.at[i])
        for i, span in enumerate(spans)
    ]
    for copy in copies:
        copy.start()
    each = rows_refs[0].shape[0]
    shape = (PLANE * each, down_ref.shape[0])
    dims = (((1,), (1,)), ((), ()))
    low0, low1 = jnp.zeros(shape, jnp.float32), jnp.zeros(shape, jnp.float32)
    for i, c in enumerate(range(0, half, STEP)):
        copies[2 * i].wait()
        copies[2 * i + 1].wait()
        rows = jnp.concatenate([r[:, c : c + STEP] for r in rows_refs], axis=0)
        low0 += lax.dot_general(
            rows, down_ref[:, c : c + STEP], dims, preferred_element_type=jnp.float32
        )
        low1 += lax.dot_general(
            rows, down_ref[:, half + c : half + c + STEP], dims, preferred_element_type=jnp.float32
        )
    zeros = jnp.zeros((16 - SPARE, shape[1]), jnp.float32)
    no_note = jnp.zeros((16 - SPARE, NOTE), jnp.float32)
    lows, notes = [], []
    for a in range(PLANE):
        note = rows_refs[a][:, half : half + NOTE].astype(jnp.float32)
        for b in range(planes):
            s = 2 * SPARE * b
            m = a * each + s
            lows += [low0[m : m + SPARE] + low1[m + SPARE : m + 2 * SPARE], zeros]
            notes += [note[s : s + SPARE], no_note]
    low = jnp.concatenate(lows, axis=0)
    note = jnp.concatenate(notes, axis=0)[:, :1]
    delta = low_delta(low, note, first_ref[0], rank, up_ref[...]).astype(jnp.bfloat16)
    for a, out in enumerate(outs):
        out[...] = delta[16 * planes * a : 16 * planes * (a + 1)]


def final_body(at_ref, base_ref, back_ref, *refs):
    *overs, out = refs
    back = jnp.concatenate([back_ref[...]] + [o[...] for o in overs], axis=0)
    main_rows, size = back_ref.shape[0], overs[0].shape[0]
    row = lax.broadcasted_iota(jnp.int32, (back.shape[0], at_ref.shape[1]), 0)
    b, i = (row - main_rows) // size, (row - main_rows) % size
    spare = jnp.where(i < SPARE, main_rows + b * SPARE + i, -2)
    pick = jnp.where(row < main_rows, row, spare) == at_ref[...]
    pick = pick.astype(jnp.float32).astype(jnp.bfloat16)
    delta = lax.dot_general(
        pick, back, (((0,), (0,)), ((), ())), preferred_element_type=jnp.float32
    )
    out[...] = (base_ref[...] + delta).astype(jnp.bfloat16)


def call(body, outs, args, specs, flops, moved, scratch=()):
    return pl.pallas_call(
        body,
        in_specs=specs,
        out_specs=[VMEM] * len(outs),
        out_shape=[jax.ShapeDtypeStruct(s, jnp.bfloat16) for s in outs],
        scratch_shapes=list(scratch),
        compiler_params=pltpu.CompilerParams(vmem_limit_bytes=40 * 2**20),
        cost_estimate=pl.CostEstimate(flops=flops, bytes_accessed=moved, transcendentals=0),
    )(*args)


def swap(x, k):
    count = lax.axis_size("ad")
    return lax.ppermute(x, "ad", [(s, s ^ k) for s in range(count)])


def route(tenant_ids, tenant_slot, local):
    tenant = tenant_ids[:, 0]
    tenant_match = tenant[:, None] == jnp.arange(TENANTS, dtype=jnp.int32)[None, :]
    slot = jnp.sum(jnp.where(tenant_match, tenant_slot[None, :], 0), axis=1)
    owner = slot // local
    order = jnp.arange(tenant.shape[0], dtype=jnp.int32)
    before = order[None, :] < order[:, None]
    place = jnp.sum(((owner[:, None] == owner[None, :]) & before).astype(jnp.int32), axis=1)
    return slot, owner, place


def on_device(tokens, value_weight, adapt_down, adapt_up, tenant_ids, tenant_slot):
    row_count, depth = tokens.shape
    count = lax.axis_size("ad")
    me = lax.axis_index("ad")
    local, _, rank = adapt_down.shape
    width = adapt_up.shape[2]
    base_value = jnp.dot(tokens, value_weight, preferred_element_type=jnp.float32)
    room = row_count // count
    planes = count // PLANE
    if count != 16 or room != 16 or (depth + NOTE) % WIDE or depth % (2 * STEP):
        slot, owner, place = route(tenant_ids, tenant_slot, local)
        delta = exchange(tokens, slot, owner, place, CAP * local, adapt_down, adapt_up)
        return (base_value + delta).astype(jnp.bfloat16)

    main_rows = count * room
    *spare, at, note, left = pl.pallas_call(
        functools.partial(route_body, room, local),
        in_specs=[SMEM, VMEM, VMEM, ANY],
        out_specs=[VMEM] * (planes + 3),
        out_shape=[jax.ShapeDtypeStruct((2 * SPARE, depth // 2 + NOTE), jnp.bfloat16)] * planes
        + [
            jax.ShapeDtypeStruct((1, row_count), jnp.int32),
            jax.ShapeDtypeStruct((NOTE, row_count), jnp.bfloat16),
            jax.ShapeDtypeStruct((1, NOTE), jnp.int32),
        ],
        scratch_shapes=[
            pltpu.VMEM(tokens.shape, jnp.bfloat16),
            pltpu.SemaphoreType.DMA((depth // STEP,)),
        ],
        compiler_params=pltpu.CompilerParams(vmem_limit_bytes=24 * 2**20),
        cost_estimate=pl.CostEstimate(
            flops=4 * 96 * row_count * depth, bytes_accessed=6 * 2**20, transcendentals=0
        ),
    )(me.reshape(1), tenant_ids.reshape(1, row_count), tenant_slot.reshape(1, TENANTS), tokens)

    along = [spare[0]] + [swap(spare[b], b * PLANE) for b in range(1, planes)]

    groups = lax.axis_size("grp")
    along[1], left = lax.optimization_barrier((along[1], left))
    flag = left
    for g in range(1, groups):
        other = lax.ppermute(left, "grp", [(s, (s + g) % groups) for s in range(groups)])
        flag = jnp.maximum(flag, other)
    blocks = pack(main_rows, flag, at, note, tokens)

    along = jnp.concatenate(along, axis=0)
    along, blocks, base_value = lax.optimization_barrier((along, blocks, base_value))
    shared = [along] + [swap(along, a) for a in range(1, PLANE)]

    blocks, shared[1] = lax.optimization_barrier((blocks, shared[1]))
    got = lax.all_to_all(
        blocks.reshape(count, room, depth + NOTE), "ad", split_axis=0, concat_axis=0, tiled=True
    ).reshape(main_rows, depth + NOTE)

    first = (me * local).reshape(1)
    down = adapt_down.transpose(0, 2, 1).reshape(local * rank, depth)
    up = adapt_up.reshape(local * rank, width)

    over_delta = call(
        functools.partial(adapt_over_body, planes, rank),
        [(16 * planes, width)] * PLANE,
        (first, down, up, *shared),
        [SMEM, ANY] + [VMEM] * 5,
        4 * 10**14,
        6 * 2**20,
        [pltpu.VMEM(down.shape, jnp.bfloat16), pltpu.SemaphoreType.DMA((depth // STEP,))],
    )
    over_sum = over_delta[0]
    for a in range(1, PLANE):
        over_sum = over_sum + swap(over_delta[a], a)
    over_back = [over_sum[:16]]
    for b in range(1, planes):
        over_back.append(swap(over_sum[16 * b : 16 * (b + 1)], b * PLANE))

    got, *over_back = lax.optimization_barrier((got, *over_back))
    delta, flags = adapt(rank, first, down, up, got)
    back = lax.all_to_all(
        delta.reshape(count, room, width), "ad", split_axis=0, concat_axis=0, tiled=True
    ).reshape(main_rows, width)

    def finish(base):
        return call(
            final_body,
            [(row_count, width)],
            (at, base, back, *over_back),
            [VMEM] * (3 + planes),
            2 * row_count * width * 320,
            2**20,
        )[0]

    def more():
        slot, owner, place = route(tenant_ids, tenant_slot, local)
        extra = exchange(
            tokens,
            slot,
            owner,
            jnp.where(at[0] < 0, place - room, -1),
            CAP * local - room,
            adapt_down,
            adapt_up,
        )
        return finish(base_value + extra)

    return lax.cond(flags[0, 1] > 0, more, lambda: finish(base_value))


def solution(mesh):
    placed = (
        P(("grp", "ad"), None),
        P(),
        P(("grp", "ad"), None, None),
        P(("grp", "ad"), None, None),
        P(("grp", "ad"), None),
        P("grp"),
    )
    return jax.shard_map(
        on_device, mesh=mesh, in_specs=placed, out_specs=P(("grp", "ad"), None), check_vma=False
    )
```

```python
import functools

import jax
import jax.numpy as jnp
from jax import lax
from jax.experimental import pallas as pl
from jax.experimental.pallas import tpu as pltpu
from jax.sharding import PartitionSpec as P

TENANTS = 256
CAP = 2
PLANE = 4
SPARE = 12
NOTE = 128
STEP = 1024
WIDE = 1664
VMEM = pl.BlockSpec(memory_space=pltpu.VMEM)
ANY = pl.BlockSpec(memory_space=pl.ANY)
SMEM = pl.BlockSpec(memory_space=pltpu.SMEM)


def exchange(tokens, slot, owner, place, room, down, up):
    count = lax.axis_size("ad")
    local, depth, rank = down.shape
    width = up.shape[2]
    at = jnp.where((place >= 0) & (place < room), owner * room + place, -1)
    hits = at[None, :] == jnp.arange(count * room, dtype=jnp.int32)[:, None]
    slots = jnp.sum(jnp.where(hits, slot[None, :] + 1, 0), axis=1) - 1
    pick = hits.astype(jnp.bfloat16)
    sent = jnp.dot(pick, tokens, preferred_element_type=jnp.float32).astype(jnp.bfloat16)
    got = lax.all_to_all(
        sent.reshape(count, room, depth), "ad", split_axis=0, concat_axis=0, tiled=True
    ).reshape(count * room, depth)
    got_slots = lax.all_to_all(
        slots.reshape(count, room), "ad", split_axis=0, concat_axis=0, tiled=True
    ).reshape(count * room)
    low_rank = jnp.einsum("td,ldr->tlr", got, down, preferred_element_type=jnp.float32)
    own = (got_slots - lax.axis_index("ad") * local)[:, None] == jnp.arange(local)[None, :]
    low_rank = jnp.where(own[:, :, None], low_rank, 0.0).astype(jnp.bfloat16)
    delta = jnp.dot(
        low_rank.reshape(count * room, local * rank),
        up.reshape(local * rank, width),
        preferred_element_type=jnp.float32,
    ).astype(jnp.bfloat16)
    back = lax.all_to_all(
        delta.reshape(count, room, width), "ad", split_axis=0, concat_axis=0, tiled=True
    )
    return jnp.dot(
        pick.T, back.reshape(count * room, width), preferred_element_type=jnp.float32
    )


def one_hot(hit):
    return hit.astype(jnp.float32).astype(jnp.bfloat16)


def earlier(hit, until):
    counts = jnp.dot(one_hot(hit), until, preferred_element_type=jnp.float32)
    return jnp.sum(jnp.where(hit, counts, 0.0), axis=0, keepdims=True).astype(jnp.int32)


def route_body(room, local, me_ref, tenant_ref, slot_ref, tokens_hbm, *refs):
    *outs, at_ref, note_ref, left_ref, tokens_ref, sems = refs
    half = tokens_ref.shape[1] // 2
    spans = [slice(h + c, h + c + STEP) for c in range(0, half, STEP) for h in (0, half)]
    copies = [
        pltpu.make_async_copy(tokens_hbm.at[:, span], tokens_ref.at[:, span], sems.at[i])
        for i, span in enumerate(spans)
    ]
    for copy in copies:
        copy.start()
    tenant = tenant_ref[...]
    rows = tenant.shape[1]
    planes = len(outs)
    main_rows = planes * PLANE * room

    def iota(size, axis=0):
        return lax.broadcasted_iota(jnp.int32, (size, rows), axis)

    table = jnp.broadcast_to(slot_ref[...].astype(jnp.float32), (16, TENANTS)).astype(jnp.bfloat16)
    slot = jnp.dot(table, one_hot(iota(TENANTS) == tenant), preferred_element_type=jnp.float32)[:1]
    owner = slot.astype(jnp.int32) // local
    until = one_hot(iota(rows) < iota(rows, 1))
    place = earlier(iota(planes * PLANE) == owner, until)
    plane = (owner ^ me_ref[0]) // PLANE
    over = place >= room
    over_place = earlier((iota(16) == plane) & over, until)
    left = over & (over_place >= SPARE)
    at = jnp.where(over, main_rows + plane * SPARE + over_place, owner * room + place)
    at = jnp.where(left, -1, at)
    at_ref[...] = at
    most = jnp.max(left.astype(jnp.float32), axis=1, keepdims=True).astype(jnp.int32)
    left_ref[...] = jnp.broadcast_to(most, left_ref.shape)
    note = jnp.where(iota(NOTE) == 0, slot + 1.0, 0.0).astype(jnp.bfloat16)
    note_ref[...] = note

    row = iota(2 * SPARE)
    upper = row >= SPARE
    ids = jnp.where(upper, row - SPARE, row)
    ids = jnp.concatenate([ids + main_rows + b * SPARE for b in range(planes)], axis=0)
    upper = jnp.concatenate([upper] * planes, axis=0)
    hit = ids == at
    first, second = one_hot(hit & ~upper), one_hot(hit & upper)

    def put(value, columns):
        for b in range(planes):
            outs[b][:, columns] = value[2 * SPARE * b : 2 * SPARE * (b + 1)].astype(jnp.bfloat16)

    put(notes_of(one_hot(hit), note), slice(half, half + NOTE))
    for i, c in enumerate(range(0, half, STEP)):
        copies[2 * i].wait()
        copies[2 * i + 1].wait()
        put(
            jnp.dot(first, tokens_ref[:, c : c + STEP], preferred_element_type=jnp.float32)
            + jnp.dot(
                second,
                tokens_ref[:, half + c : half + c + STEP],
                preferred_element_type=jnp.float32,
            ),
            slice(c, c + STEP),
        )


def notes_of(pick, note):
    return lax.dot_general(
        pick, note, (((1,), (1,)), ((), ())), preferred_element_type=jnp.float32
    )


def pack_body(last, flag_ref, at_ref, note_ref, tokens_ref, out):
    shape = (out.shape[0], at_ref.shape[1])
    pick = lax.broadcasted_iota(jnp.int32, shape, 0) == at_ref[...]
    pick = pick.astype(jnp.float32).astype(jnp.bfloat16)

    @pl.when(pl.program_id(0) < pl.num_programs(0) - 1)
    def _():
        out[...] = jnp.dot(
            pick, tokens_ref[...], preferred_element_type=jnp.float32
        ).astype(jnp.bfloat16)

    @pl.when(pl.program_id(0) == pl.num_programs(0) - 1)
    def _():
        out[:, :last] = jnp.dot(
            pick, tokens_ref[:, :last], preferred_element_type=jnp.float32
        ).astype(jnp.bfloat16)
        note = notes_of(pick, note_ref[...])
        column = lax.broadcasted_iota(jnp.int32, note.shape, 1)
        flag = jnp.where(column == 1, flag_ref[...].astype(jnp.float32), 0.0)
        out[:, last:] = (note + flag).astype(jnp.bfloat16)


def pack(main_rows, flag, at, note, tokens):
    rows, depth = tokens.shape
    steps = (depth + NOTE) // WIDE
    return pl.pallas_call(
        functools.partial(pack_body, WIDE - NOTE),
        grid=(steps,),
        in_specs=[
            pl.BlockSpec(flag.shape, lambda i: (0, 0)),
            pl.BlockSpec(at.shape, lambda i: (0, 0)),
            pl.BlockSpec(note.shape, lambda i: (0, 0)),
            pl.BlockSpec((rows, WIDE), lambda i: (0, i)),
        ],
        out_specs=pl.BlockSpec((main_rows, WIDE), lambda i: (0, i)),
        out_shape=jax.ShapeDtypeStruct((main_rows, depth + NOTE), jnp.bfloat16),
        compiler_params=pltpu.CompilerParams(vmem_limit_bytes=56 * 2**20),
        cost_estimate=pl.CostEstimate(
            flops=2 * main_rows * rows * depth, bytes_accessed=8 * 2**20, transcendentals=0
        ),
    )(flag, at, note, tokens)


def low_delta(low, note, first, rank, up):
    column = lax.broadcasted_iota(jnp.int32, low.shape, 1) // rank + (first + 1)
    low = jnp.where(note.astype(jnp.float32) == column.astype(jnp.float32), low, 0.0)
    return jnp.dot(low.astype(jnp.bfloat16), up, preferred_element_type=jnp.float32)


def adapt_body(rank, first_ref, down_hbm, up_ref, rows_hbm, out, flag_out, *scratch):
    down_ref, rows_ref, down_sems, sems = scratch
    depth = down_ref.shape[1]
    spans = [slice(c, min(c + WIDE, depth + NOTE)) for c in range(0, depth + NOTE, WIDE)]
    copies = []
    for i, span in enumerate(spans):
        kept = slice(span.start, min(span.stop, depth))
        copies.append(
            (
                pltpu.make_async_copy(rows_hbm.at[:, span], rows_ref.at[:, span], sems.at[i]),
                pltpu.make_async_copy(down_hbm.at[:, kept], down_ref.at[:, kept], down_sems.at[i]),
            )
        )
    for pair in copies:
        pair[0].start()
        pair[1].start()
    low = jnp.zeros((rows_ref.shape[0], down_ref.shape[0]), jnp.float32)
    for pair, span in zip(copies, spans, strict=True):
        pair[0].wait()
        pair[1].wait()
        span = slice(span.start, min(span.stop, depth))
        low += lax.dot_general(
            rows_ref[:, span],
            down_ref[:, span],
            (((1,), (1,)), ((), ())),
            preferred_element_type=jnp.float32,
        )
    note = rows_ref[:, depth:].astype(jnp.float32)
    out[...] = low_delta(low, note[:, :1], first_ref[0], rank, up_ref[...]).astype(jnp.bfloat16)
    most = jnp.max(note, axis=0, keepdims=True)
    flag_out[...] = jnp.broadcast_to(most, flag_out.shape).astype(jnp.bfloat16)


def adapt(rank, first, down, up, got):
    rows, width = got.shape[0], up.shape[1]
    return pl.pallas_call(
        functools.partial(adapt_body, rank),
        in_specs=[SMEM, ANY, VMEM, ANY],
        out_specs=[VMEM, VMEM],
        out_shape=[
            jax.ShapeDtypeStruct((rows, width), jnp.bfloat16),
            jax.ShapeDtypeStruct((16, NOTE), jnp.bfloat16),
        ],
        scratch_shapes=[
            pltpu.VMEM(down.shape, jnp.bfloat16),
            pltpu.VMEM(got.shape, jnp.bfloat16),
            pltpu.SemaphoreType.DMA((pl.cdiv(got.shape[1], WIDE),)),
            pltpu.SemaphoreType.DMA((pl.cdiv(got.shape[1], WIDE),)),
        ],
        compiler_params=pltpu.CompilerParams(vmem_limit_bytes=24 * 2**20),
        cost_estimate=pl.CostEstimate(
            flops=2 * rows * down.size, bytes_accessed=8 * 2**20, transcendentals=0
        ),
    )(first, down, up, got)


def adapt_over_body(planes, rank, first_ref, down_hbm, up_ref, *refs):
    rows_refs, outs = refs[:PLANE], refs[PLANE : 2 * PLANE]
    down_ref, sems = refs[2 * PLANE :]
    half = down_ref.shape[1] // 2
    spans = [slice(h + c, h + c + STEP) for c in range(0, half, STEP) for h in (0, half)]
    copies = [
        pltpu.make_async_copy(down_hbm.at[:, span], down_ref.at[:, span], sems.at[i])
        for i, span in enumerate(spans)
    ]
    for copy in copies:
        copy.start()
    each = rows_refs[0].shape[0]
    shape = (PLANE * each, down_ref.shape[0])
    dims = (((1,), (1,)), ((), ()))
    low0, low1 = jnp.zeros(shape, jnp.float32), jnp.zeros(shape, jnp.float32)
    for i, c in enumerate(range(0, half, STEP)):
        copies[2 * i].wait()
        copies[2 * i + 1].wait()
        rows = jnp.concatenate([r[:, c : c + STEP] for r in rows_refs], axis=0)
        low0 += lax.dot_general(
            rows, down_ref[:, c : c + STEP], dims, preferred_element_type=jnp.float32
        )
        low1 += lax.dot_general(
            rows, down_ref[:, half + c : half + c + STEP], dims, preferred_element_type=jnp.float32
        )
    zeros = jnp.zeros((16 - SPARE, shape[1]), jnp.float32)
    no_note = jnp.zeros((16 - SPARE, NOTE), jnp.float32)
    lows, notes = [], []
    for a in range(PLANE):
        note = rows_refs[a][:, half : half + NOTE].astype(jnp.float32)
        for b in range(planes):
            s = 2 * SPARE * b
            m = a * each + s
            lows += [low0[m : m + SPARE] + low1[m + SPARE : m + 2 * SPARE], zeros]
            notes += [note[s : s + SPARE], no_note]
    low = jnp.concatenate(lows, axis=0)
    note = jnp.concatenate(notes, axis=0)[:, :1]
    delta = low_delta(low, note, first_ref[0], rank, up_ref[...]).astype(jnp.bfloat16)
    for a, out in enumerate(outs):
        out[...] = delta[16 * planes * a : 16 * planes * (a + 1)]


def final_body(at_ref, base_ref, back_ref, *refs):
    *overs, out = refs
    back = jnp.concatenate([back_ref[...]] + [o[...] for o in overs], axis=0)
    main_rows, size = back_ref.shape[0], overs[0].shape[0]
    row = lax.broadcasted_iota(jnp.int32, (back.shape[0], at_ref.shape[1]), 0)
    b, i = (row - main_rows) // size, (row - main_rows) % size
    spare = jnp.where(i < SPARE, main_rows + b * SPARE + i, -2)
    pick = jnp.where(row < main_rows, row, spare) == at_ref[...]
    pick = pick.astype(jnp.float32).astype(jnp.bfloat16)
    delta = lax.dot_general(
        pick, back, (((0,), (0,)), ((), ())), preferred_element_type=jnp.float32
    )
    out[...] = (base_ref[...] + delta).astype(jnp.bfloat16)


def call(body, outs, args, specs, flops, moved, scratch=()):
    return pl.pallas_call(
        body,
        in_specs=specs,
        out_specs=[VMEM] * len(outs),
        out_shape=[jax.ShapeDtypeStruct(s, jnp.bfloat16) for s in outs],
        scratch_shapes=list(scratch),
        compiler_params=pltpu.CompilerParams(vmem_limit_bytes=40 * 2**20),
        cost_estimate=pl.CostEstimate(flops=flops, bytes_accessed=moved, transcendentals=0),
    )(*args)


def swap(x, k):
    count = lax.axis_size("ad")
    return lax.ppermute(x, "ad", [(s, s ^ k) for s in range(count)])


def route(tenant_ids, tenant_slot, local):
    tenant = tenant_ids[:, 0]
    tenant_match = tenant[:, None] == jnp.arange(TENANTS, dtype=jnp.int32)[None, :]
    slot = jnp.sum(jnp.where(tenant_match, tenant_slot[None, :], 0), axis=1)
    owner = slot // local
    order = jnp.arange(tenant.shape[0], dtype=jnp.int32)
    before = order[None, :] < order[:, None]
    place = jnp.sum(((owner[:, None] == owner[None, :]) & before).astype(jnp.int32), axis=1)
    return slot, owner, place


def on_device(tokens, value_weight, adapt_down, adapt_up, tenant_ids, tenant_slot):
    row_count, depth = tokens.shape
    count = lax.axis_size("ad")
    me = lax.axis_index("ad")
    local, _, rank = adapt_down.shape
    width = adapt_up.shape[2]
    base_value = jnp.dot(tokens, value_weight, preferred_element_type=jnp.float32)
    room = row_count // count
    planes = count // PLANE
    if count != 16 or room != 16 or (depth + NOTE) % WIDE or depth % (2 * STEP):
        slot, owner, place = route(tenant_ids, tenant_slot, local)
        delta = exchange(tokens, slot, owner, place, CAP * local, adapt_down, adapt_up)
        return (base_value + delta).astype(jnp.bfloat16)

    main_rows = count * room
    *spare, at, note, left = pl.pallas_call(
        functools.partial(route_body, room, local),
        in_specs=[SMEM, VMEM, VMEM, ANY],
        out_specs=[VMEM] * (planes + 3),
        out_shape=[jax.ShapeDtypeStruct((2 * SPARE, depth // 2 + NOTE), jnp.bfloat16)] * planes
        + [
            jax.ShapeDtypeStruct((1, row_count), jnp.int32),
            jax.ShapeDtypeStruct((NOTE, row_count), jnp.bfloat16),
            jax.ShapeDtypeStruct((1, NOTE), jnp.int32),
        ],
        scratch_shapes=[
            pltpu.VMEM(tokens.shape, jnp.bfloat16),
            pltpu.SemaphoreType.DMA((depth // STEP,)),
        ],
        compiler_params=pltpu.CompilerParams(vmem_limit_bytes=24 * 2**20),
        cost_estimate=pl.CostEstimate(
            flops=4 * 96 * row_count * depth, bytes_accessed=6 * 2**20, transcendentals=0
        ),
    )(me.reshape(1), tenant_ids.reshape(1, row_count), tenant_slot.reshape(1, TENANTS), tokens)

    along = [spare[0]] + [swap(spare[b], b * PLANE) for b in range(1, planes)]

    blocks = pack(main_rows, left, at, note, tokens)

    along = jnp.concatenate(along, axis=0)
    shared = [along] + [swap(along, a) for a in range(1, PLANE)]

    got = lax.all_to_all(
        blocks.reshape(count, room, depth + NOTE), "ad", split_axis=0, concat_axis=0, tiled=True
    ).reshape(main_rows, depth + NOTE)

    first = (me * local).reshape(1)
    down = adapt_down.transpose(0, 2, 1).reshape(local * rank, depth)
    up = adapt_up.reshape(local * rank, width)

    over_delta = call(
        functools.partial(adapt_over_body, planes, rank),
        [(16 * planes, width)] * PLANE,
        (first, down, up, *shared),
        [SMEM, ANY] + [VMEM] * 5,
        10**12,
        6 * 2**20,
        [pltpu.VMEM(down.shape, jnp.bfloat16), pltpu.SemaphoreType.DMA((depth // STEP,))],
    )
    got, base_value, *over_delta = lax.optimization_barrier((got, base_value, *over_delta))
    over_sum = over_delta[0]
    for a in range(1, PLANE):
        over_sum = over_sum + swap(over_delta[a], a)
    over_back = [over_sum[:16]]
    for b in range(1, planes):
        over_back.append(swap(over_sum[16 * b : 16 * (b + 1)], b * PLANE))

    delta, flags = adapt(rank, first, down, up, got)
    back = lax.all_to_all(
        delta.reshape(count, room, width), "ad", split_axis=0, concat_axis=0, tiled=True
    ).reshape(main_rows, width)

    groups = lax.axis_size("grp")
    own = flags[0, 1].astype(jnp.int32)
    seen = own
    for g in range(1, groups):
        other = lax.ppermute(own, "grp", [(s, (s + g) % groups) for s in range(groups)])
        seen = jnp.maximum(seen, other)

    def finish(base):
        return call(
            final_body,
            [(row_count, width)],
            (at, base, back, *over_back),
            [VMEM] * (3 + planes),
            2 * row_count * width * 320,
            2**20,
        )[0]

    def more():
        slot, owner, place = route(tenant_ids, tenant_slot, local)
        extra = exchange(
            tokens,
            slot,
            owner,
            jnp.where(at[0] < 0, place - room, -1),
            CAP * local - room,
            adapt_down,
            adapt_up,
        )
        return finish(base_value + extra)

    return lax.cond(seen > 0, more, lambda: finish(base_value))


def solution(mesh):
    placed = (
        P(("grp", "ad"), None),
        P(),
        P(("grp", "ad"), None, None),
        P(("grp", "ad"), None, None),
        P(("grp", "ad"), None),
        P("grp"),
    )
    return jax.shard_map(
        on_device, mesh=mesh, in_specs=placed, out_specs=P(("grp", "ad"), None), check_vma=False
    )
```

```python
import functools

import jax
import jax.numpy as jnp
from jax import lax
from jax.experimental import pallas as pl
from jax.experimental.pallas import tpu as pltpu
from jax.sharding import PartitionSpec as P

TENANTS = 256
CAP = 2
PLANE = 4
SPARE = 12
NOTE = 128
STEP = 1024
WIDE = 1664
VMEM = pl.BlockSpec(memory_space=pltpu.VMEM)
ANY = pl.BlockSpec(memory_space=pl.ANY)
SMEM = pl.BlockSpec(memory_space=pltpu.SMEM)


def exchange(tokens, slot, owner, place, room, down, up):
    count = lax.axis_size("ad")
    local, depth, rank = down.shape
    width = up.shape[2]
    at = jnp.where((place >= 0) & (place < room), owner * room + place, -1)
    hits = at[None, :] == jnp.arange(count * room, dtype=jnp.int32)[:, None]
    slots = jnp.sum(jnp.where(hits, slot[None, :] + 1, 0), axis=1) - 1
    pick = hits.astype(jnp.bfloat16)
    sent = jnp.dot(pick, tokens, preferred_element_type=jnp.float32).astype(jnp.bfloat16)
    got = lax.all_to_all(
        sent.reshape(count, room, depth), "ad", split_axis=0, concat_axis=0, tiled=True
    ).reshape(count * room, depth)
    got_slots = lax.all_to_all(
        slots.reshape(count, room), "ad", split_axis=0, concat_axis=0, tiled=True
    ).reshape(count * room)
    low_rank = jnp.einsum("td,ldr->tlr", got, down, preferred_element_type=jnp.float32)
    own = (got_slots - lax.axis_index("ad") * local)[:, None] == jnp.arange(local)[None, :]
    low_rank = jnp.where(own[:, :, None], low_rank, 0.0).astype(jnp.bfloat16)
    delta = jnp.dot(
        low_rank.reshape(count * room, local * rank),
        up.reshape(local * rank, width),
        preferred_element_type=jnp.float32,
    ).astype(jnp.bfloat16)
    back = lax.all_to_all(
        delta.reshape(count, room, width), "ad", split_axis=0, concat_axis=0, tiled=True
    )
    return jnp.dot(
        pick.T, back.reshape(count * room, width), preferred_element_type=jnp.float32
    )


def one_hot(hit):
    return hit.astype(jnp.float32).astype(jnp.bfloat16)


def earlier(hit, until):
    counts = jnp.dot(one_hot(hit), until, preferred_element_type=jnp.float32)
    return jnp.sum(jnp.where(hit, counts, 0.0), axis=0, keepdims=True).astype(jnp.int32)


def route_body(room, local, me_ref, tenant_ref, slot_ref, tokens_hbm, *refs):
    *outs, at_ref, note_ref, left_ref, tokens_ref, sems = refs
    half = tokens_ref.shape[1] // 2
    spans = [slice(h + c, h + c + STEP) for c in range(0, half, STEP) for h in (0, half)]
    copies = [
        pltpu.make_async_copy(tokens_hbm.at[:, span], tokens_ref.at[:, span], sems.at[i])
        for i, span in enumerate(spans)
    ]
    for copy in copies:
        copy.start()
    tenant = tenant_ref[...]
    rows = tenant.shape[1]
    planes = len(outs)
    main_rows = planes * PLANE * room

    def iota(size, axis=0):
        return lax.broadcasted_iota(jnp.int32, (size, rows), axis)

    table = jnp.broadcast_to(slot_ref[...].astype(jnp.float32), (16, TENANTS)).astype(jnp.bfloat16)
    slot = jnp.dot(table, one_hot(iota(TENANTS) == tenant), preferred_element_type=jnp.float32)[:1]
    owner = slot.astype(jnp.int32) // local
    until = one_hot(iota(rows) < iota(rows, 1))
    place = earlier(iota(planes * PLANE) == owner, until)
    plane = (owner ^ me_ref[0]) // PLANE
    over = place >= room
    over_place = earlier((iota(16) == plane) & over, until)
    left = over & (over_place >= SPARE)
    at = jnp.where(over, main_rows + plane * SPARE + over_place, owner * room + place)
    at = jnp.where(left, -1, at)
    at_ref[...] = at
    most = jnp.max(left.astype(jnp.float32), axis=1, keepdims=True).astype(jnp.int32)
    left_ref[...] = jnp.broadcast_to(most, left_ref.shape)
    note = jnp.where(iota(NOTE) == 0, slot + 1.0, 0.0).astype(jnp.bfloat16)
    note_ref[...] = note

    row = iota(2 * SPARE)
    upper = row >= SPARE
    ids = jnp.where(upper, row - SPARE, row)
    ids = jnp.concatenate([ids + main_rows + b * SPARE for b in range(planes)], axis=0)
    upper = jnp.concatenate([upper] * planes, axis=0)
    hit = ids == at
    first, second = one_hot(hit & ~upper), one_hot(hit & upper)

    def put(value, columns):
        for b in range(planes):
            outs[b][:, columns] = value[2 * SPARE * b : 2 * SPARE * (b + 1)].astype(jnp.bfloat16)

    put(notes_of(one_hot(hit), note), slice(half, half + NOTE))
    for i, c in enumerate(range(0, half, STEP)):
        copies[2 * i].wait()
        copies[2 * i + 1].wait()
        put(
            jnp.dot(first, tokens_ref[:, c : c + STEP], preferred_element_type=jnp.float32)
            + jnp.dot(
                second,
                tokens_ref[:, half + c : half + c + STEP],
                preferred_element_type=jnp.float32,
            ),
            slice(c, c + STEP),
        )


def notes_of(pick, note):
    return lax.dot_general(
        pick, note, (((1,), (1,)), ((), ())), preferred_element_type=jnp.float32
    )


def pack_body(at_ref, note_ref, tokens_hbm, out_hbm, tokens_ref, out_ref, sems, out_sems):
    depth = tokens_ref.shape[1]
    spans = [slice(c, c + STEP) for c in range(0, depth, STEP)]
    loads = [
        pltpu.make_async_copy(tokens_hbm.at[:, span], tokens_ref.at[:, span], sems.at[i])
        for i, span in enumerate(spans)
    ]
    for load in loads:
        load.start()
    pick = lax.broadcasted_iota(jnp.int32, (out_ref.shape[0], at_ref.shape[1]), 0) == at_ref[...]
    pick = one_hot(pick)
    out_ref[:, depth:] = notes_of(pick, note_ref[...]).astype(jnp.bfloat16)
    stores = []
    for i, span in enumerate(spans):
        loads[i].wait()
        out_ref[:, span] = jnp.dot(
            pick, tokens_ref[:, span], preferred_element_type=jnp.float32
        ).astype(jnp.bfloat16)
        ready = slice(span.start, span.stop if i + 1 < len(spans) else depth + NOTE)
        store = pltpu.make_async_copy(out_ref.at[:, ready], out_hbm.at[:, ready], out_sems.at[i])
        store.start()
        stores.append(store)
    for store in stores:
        store.wait()


def pack(main_rows, at, note, tokens):
    rows, depth = tokens.shape
    out = jax.ShapeDtypeStruct((main_rows, depth + NOTE), jnp.bfloat16)
    return pl.pallas_call(
        pack_body,
        in_specs=[VMEM, VMEM, ANY],
        out_specs=pl.BlockSpec(memory_space=pltpu.HBM),
        out_shape=out,
        scratch_shapes=[
            pltpu.VMEM(tokens.shape, jnp.bfloat16),
            pltpu.VMEM(out.shape, jnp.bfloat16),
            pltpu.SemaphoreType.DMA((depth // STEP,)),
            pltpu.SemaphoreType.DMA((depth // STEP,)),
        ],
        compiler_params=pltpu.CompilerParams(vmem_limit_bytes=52 * 2**20),
        cost_estimate=pl.CostEstimate(
            flops=2 * main_rows * rows * depth, bytes_accessed=8 * 2**20, transcendentals=0
        ),
    )(at, note, tokens)


def low_delta(low, note, first, rank, up):
    column = lax.broadcasted_iota(jnp.int32, low.shape, 1) // rank + (first + 1)
    low = jnp.where(note.astype(jnp.float32) == column.astype(jnp.float32), low, 0.0)
    return jnp.dot(low.astype(jnp.bfloat16), up, preferred_element_type=jnp.float32)


def adapt_body(rank, first_ref, down_hbm, up_ref, rows_hbm, out, *scratch):
    down_ref, rows_ref, down_sems, sems = scratch
    depth = down_ref.shape[1]
    spans = [slice(c, min(c + WIDE, depth + NOTE)) for c in range(0, depth + NOTE, WIDE)]
    copies = []
    for i, span in enumerate(spans):
        kept = slice(span.start, min(span.stop, depth))
        copies.append(
            (
                pltpu.make_async_copy(rows_hbm.at[:, span], rows_ref.at[:, span], sems.at[i]),
                pltpu.make_async_copy(down_hbm.at[:, kept], down_ref.at[:, kept], down_sems.at[i]),
            )
        )
    for pair in copies:
        pair[0].start()
        pair[1].start()
    low = jnp.zeros((rows_ref.shape[0], down_ref.shape[0]), jnp.float32)
    for pair, span in zip(copies, spans, strict=True):
        pair[0].wait()
        pair[1].wait()
        span = slice(span.start, min(span.stop, depth))
        low += lax.dot_general(
            rows_ref[:, span],
            down_ref[:, span],
            (((1,), (1,)), ((), ())),
            preferred_element_type=jnp.float32,
        )
    note = rows_ref[:, depth:].astype(jnp.float32)
    out[...] = low_delta(low, note[:, :1], first_ref[0], rank, up_ref[...]).astype(jnp.bfloat16)


def adapt(rank, first, down, up, got):
    rows, width = got.shape[0], up.shape[1]
    return pl.pallas_call(
        functools.partial(adapt_body, rank),
        in_specs=[SMEM, ANY, VMEM, ANY],
        out_specs=VMEM,
        out_shape=jax.ShapeDtypeStruct((rows, width), jnp.bfloat16),
        scratch_shapes=[
            pltpu.VMEM(down.shape, jnp.bfloat16),
            pltpu.VMEM(got.shape, jnp.bfloat16),
            pltpu.SemaphoreType.DMA((pl.cdiv(got.shape[1], WIDE),)),
            pltpu.SemaphoreType.DMA((pl.cdiv(got.shape[1], WIDE),)),
        ],
        compiler_params=pltpu.CompilerParams(vmem_limit_bytes=24 * 2**20),
        cost_estimate=pl.CostEstimate(
            flops=2 * rows * down.size, bytes_accessed=8 * 2**20, transcendentals=0
        ),
    )(first, down, up, got)


def adapt_over_body(planes, rank, first_ref, down_hbm, up_ref, flag_ref, *refs):
    rows_refs, outs = refs[:PLANE], refs[PLANE : 2 * PLANE]
    down_ref, sems = refs[2 * PLANE :]
    half = down_ref.shape[1] // 2
    spans = [slice(h + c, h + c + STEP) for c in range(0, half, STEP) for h in (0, half)]
    copies = [
        pltpu.make_async_copy(down_hbm.at[:, span], down_ref.at[:, span], sems.at[i])
        for i, span in enumerate(spans)
    ]
    for copy in copies:
        copy.start()
    each = rows_refs[0].shape[0]
    shape = (PLANE * each, down_ref.shape[0])
    dims = (((1,), (1,)), ((), ()))
    low0, low1 = jnp.zeros(shape, jnp.float32), jnp.zeros(shape, jnp.float32)
    for i, c in enumerate(range(0, half, STEP)):
        copies[2 * i].wait()
        copies[2 * i + 1].wait()
        rows = jnp.concatenate([r[:, c : c + STEP] for r in rows_refs], axis=0)
        low0 += lax.dot_general(
            rows, down_ref[:, c : c + STEP], dims, preferred_element_type=jnp.float32
        )
        low1 += lax.dot_general(
            rows, down_ref[:, half + c : half + c + STEP], dims, preferred_element_type=jnp.float32
        )
    zeros = jnp.zeros((16 - SPARE, shape[1]), jnp.float32)
    no_note = jnp.zeros((16 - SPARE, NOTE), jnp.float32)
    lows, notes = [], []
    for a in range(PLANE):
        note = rows_refs[a][:, half : half + NOTE].astype(jnp.float32)
        for b in range(planes):
            s = 2 * SPARE * b
            m = a * each + s
            lows += [low0[m : m + SPARE] + low1[m + SPARE : m + 2 * SPARE], zeros]
            notes += [note[s : s + SPARE], no_note]
    low = jnp.concatenate(lows, axis=0)
    note = jnp.concatenate(notes, axis=0)[:, :1]
    delta = low_delta(low, note, first_ref[0], rank, up_ref[...])
    row = lax.broadcasted_iota(jnp.int32, delta.shape, 0) % 16
    flag = flag_ref[...][:, :1].astype(jnp.float32)
    delta = jnp.where(row == SPARE, flag, delta).astype(jnp.bfloat16)
    for a, out in enumerate(outs):
        out[...] = delta[16 * planes * a : 16 * planes * (a + 1)]


def final_body(at_ref, base_ref, back_ref, *refs):
    *overs, out, seen_ref = refs
    seen = sum(o[...][SPARE:, :1].astype(jnp.float32) for o in overs)
    seen_ref[0] = jnp.max(seen).astype(jnp.int32)
    back = jnp.concatenate([back_ref[...]] + [o[...] for o in overs], axis=0)
    main_rows, size = back_ref.shape[0], overs[0].shape[0]
    row = lax.broadcasted_iota(jnp.int32, (back.shape[0], at_ref.shape[1]), 0)
    b, i = (row - main_rows) // size, (row - main_rows) % size
    spare = jnp.where(i < SPARE, main_rows + b * SPARE + i, -2)
    pick = jnp.where(row < main_rows, row, spare) == at_ref[...]
    pick = pick.astype(jnp.float32).astype(jnp.bfloat16)
    delta = lax.dot_general(
        pick, back, (((0,), (0,)), ((), ())), preferred_element_type=jnp.float32
    )
    out[...] = (base_ref[...] + delta).astype(jnp.bfloat16)


def call(body, outs, args, specs, flops, moved, scratch=()):
    return pl.pallas_call(
        body,
        in_specs=specs,
        out_specs=[VMEM] * len(outs),
        out_shape=[jax.ShapeDtypeStruct(s, jnp.bfloat16) for s in outs],
        scratch_shapes=list(scratch),
        compiler_params=pltpu.CompilerParams(vmem_limit_bytes=40 * 2**20),
        cost_estimate=pl.CostEstimate(flops=flops, bytes_accessed=moved, transcendentals=0),
    )(*args)


def swap(x, k):
    count = lax.axis_size("ad")
    return lax.ppermute(x, "ad", [(s, s ^ k) for s in range(count)])


def route(tenant_ids, tenant_slot, local):
    tenant = tenant_ids[:, 0]
    tenant_match = tenant[:, None] == jnp.arange(TENANTS, dtype=jnp.int32)[None, :]
    slot = jnp.sum(jnp.where(tenant_match, tenant_slot[None, :], 0), axis=1)
    owner = slot // local
    order = jnp.arange(tenant.shape[0], dtype=jnp.int32)
    before = order[None, :] < order[:, None]
    place = jnp.sum(((owner[:, None] == owner[None, :]) & before).astype(jnp.int32), axis=1)
    return slot, owner, place


def on_device(tokens, value_weight, adapt_down, adapt_up, tenant_ids, tenant_slot):
    row_count, depth = tokens.shape
    count = lax.axis_size("ad")
    me = lax.axis_index("ad")
    local, _, rank = adapt_down.shape
    width = adapt_up.shape[2]
    base_value = jnp.dot(tokens, value_weight, preferred_element_type=jnp.float32)
    room = row_count // count
    planes = count // PLANE
    if count != 16 or room != 16 or (depth + NOTE) % WIDE or depth % (2 * STEP):
        slot, owner, place = route(tenant_ids, tenant_slot, local)
        delta = exchange(tokens, slot, owner, place, CAP * local, adapt_down, adapt_up)
        return (base_value + delta).astype(jnp.bfloat16)

    main_rows = count * room
    *spare, at, note, left = pl.pallas_call(
        functools.partial(route_body, room, local),
        in_specs=[SMEM, VMEM, VMEM, ANY],
        out_specs=[VMEM] * (planes + 3),
        out_shape=[jax.ShapeDtypeStruct((2 * SPARE, depth // 2 + NOTE), jnp.bfloat16)] * planes
        + [
            jax.ShapeDtypeStruct((1, row_count), jnp.int32),
            jax.ShapeDtypeStruct((NOTE, row_count), jnp.bfloat16),
            jax.ShapeDtypeStruct((1, NOTE), jnp.int32),
        ],
        scratch_shapes=[
            pltpu.VMEM(tokens.shape, jnp.bfloat16),
            pltpu.SemaphoreType.DMA((depth // STEP,)),
        ],
        compiler_params=pltpu.CompilerParams(vmem_limit_bytes=24 * 2**20),
        cost_estimate=pl.CostEstimate(
            flops=4 * 96 * row_count * depth, bytes_accessed=6 * 2**20, transcendentals=0
        ),
    )(me.reshape(1), tenant_ids.reshape(1, row_count), tenant_slot.reshape(1, TENANTS), tokens)

    along = [spare[0]] + [swap(spare[b], b * PLANE) for b in range(1, planes)]

    blocks = pack(main_rows, at, note, tokens)

    groups = lax.axis_size("grp")
    flag = left
    for g in range(1, groups):
        other = lax.ppermute(left, "grp", [(s, (s + g) % groups) for s in range(groups)])
        flag = jnp.maximum(flag, other)


    along = jnp.concatenate(along, axis=0)
    shared = [along] + [swap(along, a) for a in range(1, PLANE)]

    got = lax.all_to_all(
        blocks.reshape(count, room, depth + NOTE), "ad", split_axis=0, concat_axis=0, tiled=True
    ).reshape(main_rows, depth + NOTE)

    first = (me * local).reshape(1)
    down = adapt_down.transpose(0, 2, 1).reshape(local * rank, depth)
    up = adapt_up.reshape(local * rank, width)

    over_delta = call(
        functools.partial(adapt_over_body, planes, rank),
        [(16 * planes, width)] * PLANE,
        (first, down, up, flag, *shared),
        [SMEM, ANY] + [VMEM] * 6,
        10**12,
        6 * 2**20,
        [pltpu.VMEM(down.shape, jnp.bfloat16), pltpu.SemaphoreType.DMA((depth // STEP,))],
    )
    got, base_value = lax.optimization_barrier((got, base_value))
    delta = adapt(rank, first, down, up, got)
    delta, *over_delta = lax.optimization_barrier((delta, *over_delta))
    over_sum = over_delta[0]
    for a in range(1, PLANE):
        over_sum = over_sum + swap(over_delta[a], a)
    over_back = [over_sum[:16]]
    for b in range(1, planes):
        over_back.append(swap(over_sum[16 * b : 16 * (b + 1)], b * PLANE))
    back = lax.all_to_all(
        delta.reshape(count, room, width), "ad", split_axis=0, concat_axis=0, tiled=True
    ).reshape(main_rows, width)

    def finish(base):
        return pl.pallas_call(
            final_body,
            in_specs=[VMEM] * (3 + planes),
            out_specs=[VMEM, SMEM],
            out_shape=[
                jax.ShapeDtypeStruct((row_count, width), jnp.bfloat16),
                jax.ShapeDtypeStruct((1,), jnp.int32),
            ],
        )(at, base, back, *over_back)

    out, seen = finish(base_value)

    def more():
        slot, owner, place = route(tenant_ids, tenant_slot, local)
        extra = exchange(
            tokens,
            slot,
            owner,
            jnp.where(at[0] < 0, place - room, -1),
            CAP * local - room,
            adapt_down,
            adapt_up,
        )
        return finish(base_value + extra)[0]

    return lax.cond(seen[0] > 0, more, lambda: out)


def solution(mesh):
    placed = (
        P(("grp", "ad"), None),
        P(),
        P(("grp", "ad"), None, None),
        P(("grp", "ad"), None, None),
        P(("grp", "ad"), None),
        P("grp"),
    )
    return jax.shard_map(
        on_device, mesh=mesh, in_specs=placed, out_specs=P(("grp", "ad"), None), check_vma=False
    )
```

```python
import functools

import jax
import jax.numpy as jnp
from jax import lax
from jax.experimental import pallas as pl
from jax.experimental.pallas import tpu as pltpu
from jax.sharding import PartitionSpec as P

TENANTS = 256
CAP = 2
PLANE = 4
SPARE = 12
NOTE = 128
STEP = 1024
WIDE = 1664
VMEM = pl.BlockSpec(memory_space=pltpu.VMEM)
ANY = pl.BlockSpec(memory_space=pl.ANY)
SMEM = pl.BlockSpec(memory_space=pltpu.SMEM)


def exchange(tokens, slot, owner, place, room, down, up):
    count = lax.axis_size("ad")
    local, depth, rank = down.shape
    width = up.shape[2]
    at = jnp.where((place >= 0) & (place < room), owner * room + place, -1)
    hits = at[None, :] == jnp.arange(count * room, dtype=jnp.int32)[:, None]
    slots = jnp.sum(jnp.where(hits, slot[None, :] + 1, 0), axis=1) - 1
    pick = hits.astype(jnp.bfloat16)
    sent = jnp.dot(pick, tokens, preferred_element_type=jnp.float32).astype(jnp.bfloat16)
    got = lax.all_to_all(
        sent.reshape(count, room, depth), "ad", split_axis=0, concat_axis=0, tiled=True
    ).reshape(count * room, depth)
    got_slots = lax.all_to_all(
        slots.reshape(count, room), "ad", split_axis=0, concat_axis=0, tiled=True
    ).reshape(count * room)
    low_rank = jnp.einsum("td,ldr->tlr", got, down, preferred_element_type=jnp.float32)
    own = (got_slots - lax.axis_index("ad") * local)[:, None] == jnp.arange(local)[None, :]
    low_rank = jnp.where(own[:, :, None], low_rank, 0.0).astype(jnp.bfloat16)
    delta = jnp.dot(
        low_rank.reshape(count * room, local * rank),
        up.reshape(local * rank, width),
        preferred_element_type=jnp.float32,
    ).astype(jnp.bfloat16)
    back = lax.all_to_all(
        delta.reshape(count, room, width), "ad", split_axis=0, concat_axis=0, tiled=True
    )
    return jnp.dot(
        pick.T, back.reshape(count * room, width), preferred_element_type=jnp.float32
    )


def one_hot(hit):
    return hit.astype(jnp.float32).astype(jnp.bfloat16)


def earlier(hit, until):
    counts = jnp.dot(one_hot(hit), until, preferred_element_type=jnp.float32)
    return jnp.sum(jnp.where(hit, counts, 0.0), axis=0, keepdims=True).astype(jnp.int32)


def route_body(room, local, me_ref, tenant_ref, slot_ref, tokens_hbm, *refs):
    *outs, at_ref, note_ref, left_ref, tokens_ref, sems = refs
    half = tokens_ref.shape[1] // 2
    spans = [slice(h + c, h + c + STEP) for c in range(0, half, STEP) for h in (0, half)]
    copies = [
        pltpu.make_async_copy(tokens_hbm.at[:, span], tokens_ref.at[:, span], sems.at[i])
        for i, span in enumerate(spans)
    ]
    for copy in copies:
        copy.start()
    tenant = tenant_ref[...]
    rows = tenant.shape[1]
    planes = len(outs)
    main_rows = planes * PLANE * room

    def iota(size, axis=0):
        return lax.broadcasted_iota(jnp.int32, (size, rows), axis)

    table = jnp.broadcast_to(slot_ref[...].astype(jnp.float32), (16, TENANTS)).astype(jnp.bfloat16)
    slot = jnp.dot(table, one_hot(iota(TENANTS) == tenant), preferred_element_type=jnp.float32)[:1]
    owner = slot.astype(jnp.int32) // local
    until = one_hot(iota(rows) < iota(rows, 1))
    place = earlier(iota(planes * PLANE) == owner, until)
    plane = (owner ^ me_ref[0]) // PLANE
    over = place >= room
    over_place = earlier((iota(16) == plane) & over, until)
    left = over & (over_place >= SPARE)
    at = jnp.where(over, main_rows + plane * SPARE + over_place, owner * room + place)
    at = jnp.where(left, -1, at)
    at_ref[...] = at
    most = jnp.max(left.astype(jnp.float32), axis=1, keepdims=True).astype(jnp.int32)
    left_ref[...] = jnp.broadcast_to(most, left_ref.shape)
    note = jnp.where(iota(NOTE) == 0, slot + 1.0, 0.0).astype(jnp.bfloat16)
    note_ref[...] = note

    row = iota(2 * SPARE)
    upper = row >= SPARE
    ids = jnp.where(upper, row - SPARE, row)
    ids = jnp.concatenate([ids + main_rows + b * SPARE for b in range(planes)], axis=0)
    upper = jnp.concatenate([upper] * planes, axis=0)
    hit = ids == at
    first, second = one_hot(hit & ~upper), one_hot(hit & upper)

    def put(value, columns):
        for b in range(planes):
            outs[b][:, columns] = value[2 * SPARE * b : 2 * SPARE * (b + 1)].astype(jnp.bfloat16)

    put(notes_of(one_hot(hit), note), slice(half, half + NOTE))
    for i, c in enumerate(range(0, half, STEP)):
        copies[2 * i].wait()
        copies[2 * i + 1].wait()
        put(
            jnp.dot(first, tokens_ref[:, c : c + STEP], preferred_element_type=jnp.float32)
            + jnp.dot(
                second,
                tokens_ref[:, half + c : half + c + STEP],
                preferred_element_type=jnp.float32,
            ),
            slice(c, c + STEP),
        )


def notes_of(pick, note):
    return lax.dot_general(
        pick, note, (((1,), (1,)), ((), ())), preferred_element_type=jnp.float32
    )


def pack_body(at_ref, note_ref, tokens_hbm, out_hbm, tokens_ref, out_ref, sems, out_sems):
    depth = tokens_ref.shape[1]
    spans = [slice(c, c + STEP) for c in range(0, depth, STEP)]
    loads = [
        pltpu.make_async_copy(tokens_hbm.at[:, span], tokens_ref.at[:, span], sems.at[i])
        for i, span in enumerate(spans)
    ]
    for load in loads:
        load.start()
    pick = lax.broadcasted_iota(jnp.int32, (out_ref.shape[0], at_ref.shape[1]), 0) == at_ref[...]
    pick = one_hot(pick)
    out_ref[:, depth:] = notes_of(pick, note_ref[...]).astype(jnp.bfloat16)
    stores = []
    for i, span in enumerate(spans):
        loads[i].wait()
        out_ref[:, span] = jnp.dot(
            pick, tokens_ref[:, span], preferred_element_type=jnp.float32
        ).astype(jnp.bfloat16)
        ready = slice(span.start, span.stop if i + 1 < len(spans) else depth + NOTE)
        store = pltpu.make_async_copy(out_ref.at[:, ready], out_hbm.at[:, ready], out_sems.at[i])
        store.start()
        stores.append(store)
    for store in stores:
        store.wait()


def pack(main_rows, at, note, tokens):
    rows, depth = tokens.shape
    out = jax.ShapeDtypeStruct((main_rows, depth + NOTE), jnp.bfloat16)
    return pl.pallas_call(
        pack_body,
        in_specs=[VMEM, VMEM, ANY],
        out_specs=pl.BlockSpec(memory_space=pltpu.HBM),
        out_shape=out,
        scratch_shapes=[
            pltpu.VMEM(tokens.shape, jnp.bfloat16),
            pltpu.VMEM(out.shape, jnp.bfloat16),
            pltpu.SemaphoreType.DMA((depth // STEP,)),
            pltpu.SemaphoreType.DMA((depth // STEP,)),
        ],
        compiler_params=pltpu.CompilerParams(vmem_limit_bytes=52 * 2**20),
        cost_estimate=pl.CostEstimate(
            flops=2 * main_rows * rows * depth, bytes_accessed=8 * 2**20, transcendentals=0
        ),
    )(at, note, tokens)


def low_delta(low, note, first, rank, up):
    column = lax.broadcasted_iota(jnp.int32, low.shape, 1) // rank + (first + 1)
    low = jnp.where(note.astype(jnp.float32) == column.astype(jnp.float32), low, 0.0)
    return jnp.dot(low.astype(jnp.bfloat16), up, preferred_element_type=jnp.float32)


def adapt_body(rank, first_ref, down_hbm, up_ref, rows_hbm, out, *scratch):
    down_ref, rows_ref, down_sems, sems = scratch
    depth = down_ref.shape[1]
    spans = [slice(c, min(c + WIDE, depth + NOTE)) for c in range(0, depth + NOTE, WIDE)]
    copies = []
    for i, span in enumerate(spans):
        kept = slice(span.start, min(span.stop, depth))
        copies.append(
            (
                pltpu.make_async_copy(rows_hbm.at[:, span], rows_ref.at[:, span], sems.at[i]),
                pltpu.make_async_copy(down_hbm.at[:, kept], down_ref.at[:, kept], down_sems.at[i]),
            )
        )
    for pair in copies:
        pair[0].start()
        pair[1].start()
    low = jnp.zeros((rows_ref.shape[0], down_ref.shape[0]), jnp.float32)
    for pair, span in zip(copies, spans, strict=True):
        pair[0].wait()
        pair[1].wait()
        span = slice(span.start, min(span.stop, depth))
        low += lax.dot_general(
            rows_ref[:, span],
            down_ref[:, span],
            (((1,), (1,)), ((), ())),
            preferred_element_type=jnp.float32,
        )
    note = rows_ref[:, depth:].astype(jnp.float32)
    out[...] = low_delta(low, note[:, :1], first_ref[0], rank, up_ref[...]).astype(jnp.bfloat16)


def adapt(rank, first, down, up, got):
    rows, width = got.shape[0], up.shape[1]
    return pl.pallas_call(
        functools.partial(adapt_body, rank),
        in_specs=[SMEM, ANY, VMEM, ANY],
        out_specs=VMEM,
        out_shape=jax.ShapeDtypeStruct((rows, width), jnp.bfloat16),
        scratch_shapes=[
            pltpu.VMEM(down.shape, jnp.bfloat16),
            pltpu.VMEM(got.shape, jnp.bfloat16),
            pltpu.SemaphoreType.DMA((pl.cdiv(got.shape[1], WIDE),)),
            pltpu.SemaphoreType.DMA((pl.cdiv(got.shape[1], WIDE),)),
        ],
        compiler_params=pltpu.CompilerParams(vmem_limit_bytes=24 * 2**20),
        cost_estimate=pl.CostEstimate(
            flops=2 * rows * down.size, bytes_accessed=8 * 2**20, transcendentals=0
        ),
    )(first, down, up, got)


def adapt_over_body(planes, rank, first_ref, down_hbm, up_ref, flag_ref, *refs):
    rows_refs, outs = refs[:PLANE], refs[PLANE : 2 * PLANE]
    down_ref, sems = refs[2 * PLANE :]
    half = down_ref.shape[1] // 2
    spans = [slice(h + c, h + c + STEP) for c in range(0, half, STEP) for h in (0, half)]
    copies = [
        pltpu.make_async_copy(down_hbm.at[:, span], down_ref.at[:, span], sems.at[i])
        for i, span in enumerate(spans)
    ]
    for copy in copies:
        copy.start()
    each = rows_refs[0].shape[0]
    shape = (PLANE * each, down_ref.shape[0])
    dims = (((1,), (1,)), ((), ()))
    low0, low1 = jnp.zeros(shape, jnp.float32), jnp.zeros(shape, jnp.float32)
    for i, c in enumerate(range(0, half, STEP)):
        copies[2 * i].wait()
        copies[2 * i + 1].wait()
        rows = jnp.concatenate([r[:, c : c + STEP] for r in rows_refs], axis=0)
        low0 += lax.dot_general(
            rows, down_ref[:, c : c + STEP], dims, preferred_element_type=jnp.float32
        )
        low1 += lax.dot_general(
            rows, down_ref[:, half + c : half + c + STEP], dims, preferred_element_type=jnp.float32
        )
    zeros = jnp.zeros((16 - SPARE, shape[1]), jnp.float32)
    no_note = jnp.zeros((16 - SPARE, NOTE), jnp.float32)
    lows, notes = [], []
    for a in range(PLANE):
        note = rows_refs[a][:, half : half + NOTE].astype(jnp.float32)
        for b in range(planes):
            s = 2 * SPARE * b
            m = a * each + s
            lows += [low0[m : m + SPARE] + low1[m + SPARE : m + 2 * SPARE], zeros]
            notes += [note[s : s + SPARE], no_note]
    low = jnp.concatenate(lows, axis=0)
    note = jnp.concatenate(notes, axis=0)[:, :1]
    delta = low_delta(low, note, first_ref[0], rank, up_ref[...])
    row = lax.broadcasted_iota(jnp.int32, delta.shape, 0) % 16
    flag = flag_ref[...][:, :1].astype(jnp.float32)
    delta = jnp.where(row == SPARE, flag, delta).astype(jnp.bfloat16)
    for a, out in enumerate(outs):
        out[...] = delta[16 * planes * a : 16 * planes * (a + 1)]


def final_body(at_ref, base_ref, back_ref, *refs):
    *overs, out, seen_ref = refs
    seen = sum(o[...][SPARE:, :1].astype(jnp.float32) for o in overs)
    seen_ref[0] = jnp.max(seen).astype(jnp.int32)
    back = jnp.concatenate([back_ref[...]] + [o[...] for o in overs], axis=0)
    main_rows, size = back_ref.shape[0], overs[0].shape[0]
    row = lax.broadcasted_iota(jnp.int32, (back.shape[0], at_ref.shape[1]), 0)
    b, i = (row - main_rows) // size, (row - main_rows) % size
    spare = jnp.where(i < SPARE, main_rows + b * SPARE + i, -2)
    pick = jnp.where(row < main_rows, row, spare) == at_ref[...]
    pick = pick.astype(jnp.float32).astype(jnp.bfloat16)
    delta = lax.dot_general(
        pick, back, (((0,), (0,)), ((), ())), preferred_element_type=jnp.float32
    )
    out[...] = (base_ref[...] + delta).astype(jnp.bfloat16)


def call(body, outs, args, specs, flops, moved, scratch=()):
    return pl.pallas_call(
        body,
        in_specs=specs,
        out_specs=[VMEM] * len(outs),
        out_shape=[jax.ShapeDtypeStruct(s, jnp.bfloat16) for s in outs],
        scratch_shapes=list(scratch),
        compiler_params=pltpu.CompilerParams(vmem_limit_bytes=40 * 2**20),
        cost_estimate=pl.CostEstimate(flops=flops, bytes_accessed=moved, transcendentals=0),
    )(*args)


def swap(x, k):
    count = lax.axis_size("ad")
    return lax.ppermute(x, "ad", [(s, s ^ k) for s in range(count)])


def route(tenant_ids, tenant_slot, local):
    tenant = tenant_ids[:, 0]
    tenant_match = tenant[:, None] == jnp.arange(TENANTS, dtype=jnp.int32)[None, :]
    slot = jnp.sum(jnp.where(tenant_match, tenant_slot[None, :], 0), axis=1)
    owner = slot // local
    order = jnp.arange(tenant.shape[0], dtype=jnp.int32)
    before = order[None, :] < order[:, None]
    place = jnp.sum(((owner[:, None] == owner[None, :]) & before).astype(jnp.int32), axis=1)
    return slot, owner, place


def on_device(tokens, value_weight, adapt_down, adapt_up, tenant_ids, tenant_slot):
    row_count, depth = tokens.shape
    count = lax.axis_size("ad")
    me = lax.axis_index("ad")
    local, _, rank = adapt_down.shape
    width = adapt_up.shape[2]
    base_value = jnp.dot(tokens, value_weight, preferred_element_type=jnp.float32)
    room = row_count // count
    planes = count // PLANE
    if count != 16 or room != 16 or (depth + NOTE) % WIDE or depth % (2 * STEP):
        slot, owner, place = route(tenant_ids, tenant_slot, local)
        delta = exchange(tokens, slot, owner, place, CAP * local, adapt_down, adapt_up)
        return (base_value + delta).astype(jnp.bfloat16)

    main_rows = count * room
    *spare, at, note, left = pl.pallas_call(
        functools.partial(route_body, room, local),
        in_specs=[SMEM, VMEM, VMEM, ANY],
        out_specs=[VMEM] * (planes + 3),
        out_shape=[jax.ShapeDtypeStruct((2 * SPARE, depth // 2 + NOTE), jnp.bfloat16)] * planes
        + [
            jax.ShapeDtypeStruct((1, row_count), jnp.int32),
            jax.ShapeDtypeStruct((NOTE, row_count), jnp.bfloat16),
            jax.ShapeDtypeStruct((1, NOTE), jnp.int32),
        ],
        scratch_shapes=[
            pltpu.VMEM(tokens.shape, jnp.bfloat16),
            pltpu.SemaphoreType.DMA((depth // STEP,)),
        ],
        compiler_params=pltpu.CompilerParams(vmem_limit_bytes=24 * 2**20),
        cost_estimate=pl.CostEstimate(
            flops=4 * 96 * row_count * depth, bytes_accessed=6 * 2**20, transcendentals=0
        ),
    )(me.reshape(1), tenant_ids.reshape(1, row_count), tenant_slot.reshape(1, TENANTS), tokens)

    along = [spare[0]] + [swap(spare[b], b * PLANE) for b in range(1, planes)]

    blocks = pack(main_rows, at, note, tokens)

    along = jnp.concatenate(along, axis=0)
    along, left = lax.optimization_barrier((along, left))
    groups = lax.axis_size("grp")
    flag = left
    for g in range(1, groups):
        other = lax.ppermute(left, "grp", [(s, (s + g) % groups) for s in range(groups)])
        flag = jnp.maximum(flag, other)
    shared = [along] + [swap(along, a) for a in range(1, PLANE)]

    got = lax.all_to_all(
        blocks.reshape(count, room, depth + NOTE), "ad", split_axis=0, concat_axis=0, tiled=True
    ).reshape(main_rows, depth + NOTE)

    first = (me * local).reshape(1)
    down = adapt_down.transpose(0, 2, 1).reshape(local * rank, depth)
    up = adapt_up.reshape(local * rank, width)

    over_delta = call(
        functools.partial(adapt_over_body, planes, rank),
        [(16 * planes, width)] * PLANE,
        (first, down, up, flag, *shared),
        [SMEM, ANY] + [VMEM] * 6,
        2 * 384 * depth * local * rank,
        6 * 2**20,
        [pltpu.VMEM(down.shape, jnp.bfloat16), pltpu.SemaphoreType.DMA((depth // STEP,))],
    )
    got, base_value, *over_delta = lax.optimization_barrier((got, base_value, *over_delta))
    delta = adapt(rank, first, down, up, got)
    delta, *over_delta = lax.optimization_barrier((delta, *over_delta))
    over_sum = over_delta[0]
    for a in range(1, PLANE):
        over_sum = over_sum + swap(over_delta[a], a)
    over_back = [over_sum[:16]]
    for b in range(1, planes):
        over_back.append(swap(over_sum[16 * b : 16 * (b + 1)], b * PLANE))
    back = lax.all_to_all(
        delta.reshape(count, room, width), "ad", split_axis=0, concat_axis=0, tiled=True
    ).reshape(main_rows, width)

    def finish(base):
        return pl.pallas_call(
            final_body,
            in_specs=[VMEM] * (3 + planes),
            out_specs=[VMEM, SMEM],
            out_shape=[
                jax.ShapeDtypeStruct((row_count, width), jnp.bfloat16),
                jax.ShapeDtypeStruct((1,), jnp.int32),
            ],
        )(at, base, back, *over_back)

    out, seen = finish(base_value)

    def more():
        slot, owner, place = route(tenant_ids, tenant_slot, local)
        extra = exchange(
            tokens,
            slot,
            owner,
            jnp.where(at[0] < 0, place - room, -1),
            CAP * local - room,
            adapt_down,
            adapt_up,
        )
        return finish(base_value + extra)[0]

    return lax.cond(seen[0] > 0, more, lambda: out)


def solution(mesh):
    placed = (
        P(("grp", "ad"), None),
        P(),
        P(("grp", "ad"), None, None),
        P(("grp", "ad"), None, None),
        P(("grp", "ad"), None),
        P("grp"),
    )
    return jax.shard_map(
        on_device, mesh=mesh, in_specs=placed, out_specs=P(("grp", "ad"), None), check_vma=False
    )
```

```python
import functools

import jax
import jax.numpy as jnp
from jax import lax
from jax.experimental import pallas as pl
from jax.experimental.pallas import tpu as pltpu
from jax.sharding import PartitionSpec as P

TENANTS = 256
CAP = 2
PLANE = 4
SPARE = 12
NOTE = 128
STEP = 1024
WIDE = 1664
VMEM = pl.BlockSpec(memory_space=pltpu.VMEM)
ANY = pl.BlockSpec(memory_space=pl.ANY)
SMEM = pl.BlockSpec(memory_space=pltpu.SMEM)


def exchange(tokens, slot, owner, place, room, down, up):
    count = lax.axis_size("ad")
    local, depth, rank = down.shape
    width = up.shape[2]
    at = jnp.where((place >= 0) & (place < room), owner * room + place, -1)
    hits = at[None, :] == jnp.arange(count * room, dtype=jnp.int32)[:, None]
    slots = jnp.sum(jnp.where(hits, slot[None, :] + 1, 0), axis=1) - 1
    pick = hits.astype(jnp.bfloat16)
    sent = jnp.dot(pick, tokens, preferred_element_type=jnp.float32).astype(jnp.bfloat16)
    got = lax.all_to_all(
        sent.reshape(count, room, depth), "ad", split_axis=0, concat_axis=0, tiled=True
    ).reshape(count * room, depth)
    got_slots = lax.all_to_all(
        slots.reshape(count, room), "ad", split_axis=0, concat_axis=0, tiled=True
    ).reshape(count * room)
    low_rank = jnp.einsum("td,ldr->tlr", got, down, preferred_element_type=jnp.float32)
    own = (got_slots - lax.axis_index("ad") * local)[:, None] == jnp.arange(local)[None, :]
    low_rank = jnp.where(own[:, :, None], low_rank, 0.0).astype(jnp.bfloat16)
    delta = jnp.dot(
        low_rank.reshape(count * room, local * rank),
        up.reshape(local * rank, width),
        preferred_element_type=jnp.float32,
    ).astype(jnp.bfloat16)
    back = lax.all_to_all(
        delta.reshape(count, room, width), "ad", split_axis=0, concat_axis=0, tiled=True
    )
    return jnp.dot(
        pick.T, back.reshape(count * room, width), preferred_element_type=jnp.float32
    )


def one_hot(hit):
    return hit.astype(jnp.float32).astype(jnp.bfloat16)


def earlier(hit, until):
    counts = jnp.dot(one_hot(hit), until, preferred_element_type=jnp.float32)
    return jnp.sum(jnp.where(hit, counts, 0.0), axis=0, keepdims=True).astype(jnp.int32)


def route_body(room, local, me_ref, tenant_ref, slot_ref, tokens_hbm, *refs):
    *outs, at_ref, note_ref, left_ref, tokens_ref, sems = refs
    half = tokens_ref.shape[1] // 2
    spans = [slice(h + c, h + c + STEP) for c in range(0, half, STEP) for h in (0, half)]
    copies = [
        pltpu.make_async_copy(tokens_hbm.at[:, span], tokens_ref.at[:, span], sems.at[i])
        for i, span in enumerate(spans)
    ]
    for copy in copies:
        copy.start()
    tenant = tenant_ref[...]
    rows = tenant.shape[1]
    planes = len(outs)
    main_rows = planes * PLANE * room

    def iota(size, axis=0):
        return lax.broadcasted_iota(jnp.int32, (size, rows), axis)

    table = jnp.broadcast_to(slot_ref[...].astype(jnp.float32), (16, TENANTS)).astype(jnp.bfloat16)
    slot = jnp.dot(table, one_hot(iota(TENANTS) == tenant), preferred_element_type=jnp.float32)[:1]
    owner = slot.astype(jnp.int32) // local
    until = one_hot(iota(rows) < iota(rows, 1))
    place = earlier(iota(planes * PLANE) == owner, until)
    plane = (owner ^ me_ref[0]) // PLANE
    over = place >= room
    over_place = earlier((iota(16) == plane) & over, until)
    left = over & (over_place >= SPARE)
    at = jnp.where(over, main_rows + plane * SPARE + over_place, owner * room + place)
    at = jnp.where(left, -1, at)
    at_ref[...] = at
    most = jnp.max(left.astype(jnp.float32), axis=1, keepdims=True).astype(jnp.int32)
    left_ref[...] = jnp.broadcast_to(most, left_ref.shape)
    note = jnp.where(iota(NOTE) == 0, slot + 1.0, 0.0).astype(jnp.bfloat16)
    note_ref[...] = note

    row = iota(2 * SPARE)
    upper = row >= SPARE
    ids = jnp.where(upper, row - SPARE, row)
    ids = jnp.concatenate([ids + main_rows + b * SPARE for b in range(planes)], axis=0)
    upper = jnp.concatenate([upper] * planes, axis=0)
    hit = ids == at
    first, second = one_hot(hit & ~upper), one_hot(hit & upper)

    def put(value, columns):
        for b in range(planes):
            outs[b][:, columns] = value[2 * SPARE * b : 2 * SPARE * (b + 1)].astype(jnp.bfloat16)

    put(notes_of(one_hot(hit), note), slice(half, half + NOTE))
    for i, c in enumerate(range(0, half, STEP)):
        copies[2 * i].wait()
        copies[2 * i + 1].wait()
        put(
            jnp.dot(first, tokens_ref[:, c : c + STEP], preferred_element_type=jnp.float32)
            + jnp.dot(
                second,
                tokens_ref[:, half + c : half + c + STEP],
                preferred_element_type=jnp.float32,
            ),
            slice(c, c + STEP),
        )


def notes_of(pick, note):
    return lax.dot_general(
        pick, note, (((1,), (1,)), ((), ())), preferred_element_type=jnp.float32
    )


def pack_body(at_ref, note_ref, tokens_hbm, out_hbm, tokens_ref, out_ref, sems, out_sems):
    depth = tokens_ref.shape[1]
    spans = [slice(c, c + STEP) for c in range(0, depth, STEP)]
    loads = [
        pltpu.make_async_copy(tokens_hbm.at[:, span], tokens_ref.at[:, span], sems.at[i])
        for i, span in enumerate(spans)
    ]
    for load in loads:
        load.start()
    pick = lax.broadcasted_iota(jnp.int32, (out_ref.shape[0], at_ref.shape[1]), 0) == at_ref[...]
    pick = one_hot(pick)
    out_ref[:, depth:] = notes_of(pick, note_ref[...]).astype(jnp.bfloat16)
    stores = []
    for i, span in enumerate(spans):
        loads[i].wait()
        out_ref[:, span] = jnp.dot(
            pick, tokens_ref[:, span], preferred_element_type=jnp.float32
        ).astype(jnp.bfloat16)
        ready = slice(span.start, span.stop if i + 1 < len(spans) else depth + NOTE)
        store = pltpu.make_async_copy(out_ref.at[:, ready], out_hbm.at[:, ready], out_sems.at[i])
        store.start()
        stores.append(store)
    for store in stores:
        store.wait()


def pack(main_rows, at, note, tokens):
    rows, depth = tokens.shape
    out = jax.ShapeDtypeStruct((main_rows, depth + NOTE), jnp.bfloat16)
    return pl.pallas_call(
        pack_body,
        in_specs=[VMEM, VMEM, ANY],
        out_specs=pl.BlockSpec(memory_space=pltpu.HBM),
        out_shape=out,
        scratch_shapes=[
            pltpu.VMEM(tokens.shape, jnp.bfloat16),
            pltpu.VMEM(out.shape, jnp.bfloat16),
            pltpu.SemaphoreType.DMA((depth // STEP,)),
            pltpu.SemaphoreType.DMA((depth // STEP,)),
        ],
        compiler_params=pltpu.CompilerParams(vmem_limit_bytes=52 * 2**20),
        cost_estimate=pl.CostEstimate(
            flops=2 * main_rows * rows * depth, bytes_accessed=8 * 2**20, transcendentals=0
        ),
    )(at, note, tokens)


def low_delta(low, note, first, rank, up):
    column = lax.broadcasted_iota(jnp.int32, low.shape, 1) // rank + (first + 1)
    low = jnp.where(note.astype(jnp.float32) == column.astype(jnp.float32), low, 0.0)
    return jnp.dot(low.astype(jnp.bfloat16), up, preferred_element_type=jnp.float32)


def adapt_body(rank, first_ref, down_hbm, up_ref, rows_hbm, out, *scratch):
    down_ref, rows_ref, down_sems, sems = scratch
    depth = down_ref.shape[1]
    spans = [slice(c, min(c + WIDE, depth + NOTE)) for c in range(0, depth + NOTE, WIDE)]
    copies = []
    for i, span in enumerate(spans):
        kept = slice(span.start, min(span.stop, depth))
        copies.append(
            (
                pltpu.make_async_copy(rows_hbm.at[:, span], rows_ref.at[:, span], sems.at[i]),
                pltpu.make_async_copy(down_hbm.at[:, kept], down_ref.at[:, kept], down_sems.at[i]),
            )
        )
    for pair in copies:
        pair[0].start()
        pair[1].start()
    low = jnp.zeros((rows_ref.shape[0], down_ref.shape[0]), jnp.float32)
    for pair, span in zip(copies, spans, strict=True):
        pair[0].wait()
        pair[1].wait()
        span = slice(span.start, min(span.stop, depth))
        low += lax.dot_general(
            rows_ref[:, span],
            down_ref[:, span],
            (((1,), (1,)), ((), ())),
            preferred_element_type=jnp.float32,
        )
    note = rows_ref[:, depth:].astype(jnp.float32)
    out[...] = low_delta(low, note[:, :1], first_ref[0], rank, up_ref[...]).astype(jnp.bfloat16)


def adapt(rank, first, down, up, got):
    rows, width = got.shape[0], up.shape[1]
    return pl.pallas_call(
        functools.partial(adapt_body, rank),
        in_specs=[SMEM, ANY, VMEM, ANY],
        out_specs=VMEM,
        out_shape=jax.ShapeDtypeStruct((rows, width), jnp.bfloat16),
        scratch_shapes=[
            pltpu.VMEM(down.shape, jnp.bfloat16),
            pltpu.VMEM(got.shape, jnp.bfloat16),
            pltpu.SemaphoreType.DMA((pl.cdiv(got.shape[1], WIDE),)),
            pltpu.SemaphoreType.DMA((pl.cdiv(got.shape[1], WIDE),)),
        ],
        compiler_params=pltpu.CompilerParams(vmem_limit_bytes=24 * 2**20),
        cost_estimate=pl.CostEstimate(
            flops=2 * rows * down.size, bytes_accessed=8 * 2**20, transcendentals=0
        ),
    )(first, down, up, got)


def adapt_over_body(planes, rank, first_ref, down_hbm, up_ref, flag_ref, *refs):
    rows_refs, outs = refs[:PLANE], refs[PLANE : 2 * PLANE]
    down_ref, sems = refs[2 * PLANE :]
    half = down_ref.shape[1] // 2
    spans = [slice(h + c, h + c + STEP) for c in range(0, half, STEP) for h in (0, half)]
    copies = [
        pltpu.make_async_copy(down_hbm.at[:, span], down_ref.at[:, span], sems.at[i])
        for i, span in enumerate(spans)
    ]
    for copy in copies:
        copy.start()
    each = rows_refs[0].shape[0]
    shape = (PLANE * each, down_ref.shape[0])
    dims = (((1,), (1,)), ((), ()))
    low0, low1 = jnp.zeros(shape, jnp.float32), jnp.zeros(shape, jnp.float32)
    for i, c in enumerate(range(0, half, STEP)):
        copies[2 * i].wait()
        copies[2 * i + 1].wait()
        rows = jnp.concatenate([r[:, c : c + STEP] for r in rows_refs], axis=0)
        low0 += lax.dot_general(
            rows, down_ref[:, c : c + STEP], dims, preferred_element_type=jnp.float32
        )
        low1 += lax.dot_general(
            rows, down_ref[:, half + c : half + c + STEP], dims, preferred_element_type=jnp.float32
        )
    zeros = jnp.zeros((16 - SPARE, shape[1]), jnp.float32)
    no_note = jnp.zeros((16 - SPARE, NOTE), jnp.float32)
    lows, notes = [], []
    for a in range(PLANE):
        note = rows_refs[a][:, half : half + NOTE].astype(jnp.float32)
        for b in range(planes):
            s = 2 * SPARE * b
            m = a * each + s
            lows += [low0[m : m + SPARE] + low1[m + SPARE : m + 2 * SPARE], zeros]
            notes += [note[s : s + SPARE], no_note]
    low = jnp.concatenate(lows, axis=0)
    note = jnp.concatenate(notes, axis=0)[:, :1]
    delta = low_delta(low, note, first_ref[0], rank, up_ref[...])
    row = lax.broadcasted_iota(jnp.int32, delta.shape, 0) % 16
    flag = flag_ref[...][:, :1].astype(jnp.float32)
    delta = jnp.where(row == SPARE, flag, delta).astype(jnp.bfloat16)
    for a, out in enumerate(outs):
        out[...] = delta[16 * planes * a : 16 * planes * (a + 1)]


def final_body(at_ref, base_ref, back_ref, *refs):
    *overs, out, seen_ref = refs
    seen = sum(o[...][SPARE:, :1].astype(jnp.float32) for o in overs)
    seen_ref[0] = jnp.max(seen).astype(jnp.int32)
    back = jnp.concatenate([back_ref[...]] + [o[...] for o in overs], axis=0)
    main_rows, size = back_ref.shape[0], overs[0].shape[0]
    row = lax.broadcasted_iota(jnp.int32, (back.shape[0], at_ref.shape[1]), 0)
    b, i = (row - main_rows) // size, (row - main_rows) % size
    spare = jnp.where(i < SPARE, main_rows + b * SPARE + i, -2)
    pick = jnp.where(row < main_rows, row, spare) == at_ref[...]
    pick = pick.astype(jnp.float32).astype(jnp.bfloat16)
    delta = lax.dot_general(
        pick, back, (((0,), (0,)), ((), ())), preferred_element_type=jnp.float32
    )
    out[...] = (base_ref[...] + delta).astype(jnp.bfloat16)


def call(body, outs, args, specs, flops, moved, scratch=()):
    return pl.pallas_call(
        body,
        in_specs=specs,
        out_specs=[VMEM] * len(outs),
        out_shape=[jax.ShapeDtypeStruct(s, jnp.bfloat16) for s in outs],
        scratch_shapes=list(scratch),
        compiler_params=pltpu.CompilerParams(vmem_limit_bytes=40 * 2**20),
        cost_estimate=pl.CostEstimate(flops=flops, bytes_accessed=moved, transcendentals=0),
    )(*args)


def swap(x, k):
    count = lax.axis_size("ad")
    return lax.ppermute(x, "ad", [(s, s ^ k) for s in range(count)])


def route(tenant_ids, tenant_slot, local):
    tenant = tenant_ids[:, 0]
    tenant_match = tenant[:, None] == jnp.arange(TENANTS, dtype=jnp.int32)[None, :]
    slot = jnp.sum(jnp.where(tenant_match, tenant_slot[None, :], 0), axis=1)
    owner = slot // local
    order = jnp.arange(tenant.shape[0], dtype=jnp.int32)
    before = order[None, :] < order[:, None]
    place = jnp.sum(((owner[:, None] == owner[None, :]) & before).astype(jnp.int32), axis=1)
    return slot, owner, place


def on_device(tokens, value_weight, adapt_down, adapt_up, tenant_ids, tenant_slot):
    row_count, depth = tokens.shape
    count = lax.axis_size("ad")
    me = lax.axis_index("ad")
    local, _, rank = adapt_down.shape
    width = adapt_up.shape[2]
    base_value = jnp.dot(tokens, value_weight, preferred_element_type=jnp.float32)
    room = row_count // count
    planes = count // PLANE
    if count != 16 or room != 16 or (depth + NOTE) % WIDE or depth % (2 * STEP):
        slot, owner, place = route(tenant_ids, tenant_slot, local)
        delta = exchange(tokens, slot, owner, place, CAP * local, adapt_down, adapt_up)
        return (base_value + delta).astype(jnp.bfloat16)

    main_rows = count * room
    *spare, at, note, left = pl.pallas_call(
        functools.partial(route_body, room, local),
        in_specs=[SMEM, VMEM, VMEM, ANY],
        out_specs=[VMEM] * (planes + 3),
        out_shape=[jax.ShapeDtypeStruct((2 * SPARE, depth // 2 + NOTE), jnp.bfloat16)] * planes
        + [
            jax.ShapeDtypeStruct((1, row_count), jnp.int32),
            jax.ShapeDtypeStruct((NOTE, row_count), jnp.bfloat16),
            jax.ShapeDtypeStruct((1, NOTE), jnp.int32),
        ],
        scratch_shapes=[
            pltpu.VMEM(tokens.shape, jnp.bfloat16),
            pltpu.SemaphoreType.DMA((depth // STEP,)),
        ],
        compiler_params=pltpu.CompilerParams(vmem_limit_bytes=24 * 2**20),
        cost_estimate=pl.CostEstimate(
            flops=4 * 96 * row_count * depth, bytes_accessed=6 * 2**20, transcendentals=0
        ),
    )(me.reshape(1), tenant_ids.reshape(1, row_count), tenant_slot.reshape(1, TENANTS), tokens)

    along = [spare[0]] + [swap(spare[b], b * PLANE) for b in range(1, planes)]

    blocks = pack(main_rows, at, note, tokens)

    along = jnp.concatenate(along, axis=0)
    along, left = lax.optimization_barrier((along, left))
    groups = lax.axis_size("grp")
    flag = left
    for g in range(1, groups):
        other = lax.ppermute(left, "grp", [(s, (s + g) % groups) for s in range(groups)])
        flag = jnp.maximum(flag, other)
    shared = [along] + [swap(along, a) for a in range(1, PLANE)]

    got = lax.all_to_all(
        blocks.reshape(count, room, depth + NOTE), "ad", split_axis=0, concat_axis=0, tiled=True
    ).reshape(main_rows, depth + NOTE)

    first = (me * local).reshape(1)
    down = adapt_down.transpose(0, 2, 1).reshape(local * rank, depth)
    up = adapt_up.reshape(local * rank, width)

    over_delta = call(
        functools.partial(adapt_over_body, planes, rank),
        [(16 * planes, width)] * PLANE,
        (first, down, up, flag, *shared),
        [SMEM, ANY] + [VMEM] * 6,
        10**12,
        6 * 2**20,
        [pltpu.VMEM(down.shape, jnp.bfloat16), pltpu.SemaphoreType.DMA((depth // STEP,))],
    )
    got, base_value, *over_delta = lax.optimization_barrier((got, base_value, *over_delta))
    delta = adapt(rank, first, down, up, got)
    delta, *over_delta = lax.optimization_barrier((delta, *over_delta))
    over_sum = over_delta[0]
    for a in range(1, PLANE):
        over_sum = over_sum + swap(over_delta[a], a)
    over_back = [over_sum[:16]]
    for b in range(1, planes):
        over_back.append(swap(over_sum[16 * b : 16 * (b + 1)], b * PLANE))
    back = lax.all_to_all(
        delta.reshape(count, room, width), "ad", split_axis=0, concat_axis=0, tiled=True
    ).reshape(main_rows, width)

    def finish(base):
        return pl.pallas_call(
            final_body,
            in_specs=[VMEM] * (3 + planes),
            out_specs=[VMEM, SMEM],
            out_shape=[
                jax.ShapeDtypeStruct((row_count, width), jnp.bfloat16),
                jax.ShapeDtypeStruct((1,), jnp.int32),
            ],
        )(at, base, back, *over_back)

    out, seen = finish(base_value)

    def more():
        slot, owner, place = route(tenant_ids, tenant_slot, local)
        extra = exchange(
            tokens,
            slot,
            owner,
            jnp.where(at[0] < 0, place - room, -1),
            CAP * local - room,
            adapt_down,
            adapt_up,
        )
        return finish(base_value + extra)[0]

    return lax.cond(seen[0] > 0, more, lambda: out)


def solution(mesh):
    placed = (
        P(("grp", "ad"), None),
        P(),
        P(("grp", "ad"), None, None),
        P(("grp", "ad"), None, None),
        P(("grp", "ad"), None),
        P("grp"),
    )
    return jax.shard_map(
        on_device, mesh=mesh, in_specs=placed, out_specs=P(("grp", "ad"), None), check_vma=False
    )
```

```python
import functools

import jax
import jax.numpy as jnp
from jax import lax
from jax.experimental import pallas as pl
from jax.experimental.pallas import tpu as pltpu
from jax.sharding import PartitionSpec as P

TENANTS = 256
CAP = 2
PLANE = 4
SPARE = 12
NOTE = 128
STEP = 1024
PARTS = 8
VMEM = pl.BlockSpec(memory_space=pltpu.VMEM)
ANY = pl.BlockSpec(memory_space=pl.ANY)
SMEM = pl.BlockSpec(memory_space=pltpu.SMEM)


def exchange(tokens, slot, owner, place, room, down, up):
    count = lax.axis_size("ad")
    local, depth, rank = down.shape
    width = up.shape[2]
    at = jnp.where((place >= 0) & (place < room), owner * room + place, -1)
    hits = at[None, :] == jnp.arange(count * room, dtype=jnp.int32)[:, None]
    slots = jnp.sum(jnp.where(hits, slot[None, :] + 1, 0), axis=1) - 1
    pick = hits.astype(jnp.bfloat16)
    sent = jnp.dot(pick, tokens, preferred_element_type=jnp.float32).astype(jnp.bfloat16)
    got = lax.all_to_all(
        sent.reshape(count, room, depth), "ad", split_axis=0, concat_axis=0, tiled=True
    ).reshape(count * room, depth)
    got_slots = lax.all_to_all(
        slots.reshape(count, room), "ad", split_axis=0, concat_axis=0, tiled=True
    ).reshape(count * room)
    low_rank = jnp.einsum("td,ldr->tlr", got, down, preferred_element_type=jnp.float32)
    own = (got_slots - lax.axis_index("ad") * local)[:, None] == jnp.arange(local)[None, :]
    low_rank = jnp.where(own[:, :, None], low_rank, 0.0).astype(jnp.bfloat16)
    delta = jnp.dot(
        low_rank.reshape(count * room, local * rank),
        up.reshape(local * rank, width),
        preferred_element_type=jnp.float32,
    ).astype(jnp.bfloat16)
    back = lax.all_to_all(
        delta.reshape(count, room, width), "ad", split_axis=0, concat_axis=0, tiled=True
    )
    return jnp.dot(
        pick.T, back.reshape(count * room, width), preferred_element_type=jnp.float32
    )


def row_copies(source, target, sems, parts):
    rows = target.shape[0] // parts
    return [
        pltpu.make_async_copy(
            source.at[i * rows : (i + 1) * rows], target.at[i * rows : (i + 1) * rows], sems.at[i]
        )
        for i in range(parts)
    ]


def one_hot(hit):
    return hit.astype(jnp.float32).astype(jnp.bfloat16)


def earlier(hit, until):
    counts = jnp.dot(one_hot(hit), until, preferred_element_type=jnp.float32)
    return jnp.sum(jnp.where(hit, counts, 0.0), axis=0, keepdims=True).astype(jnp.int32)


def route_body(room, local, me_ref, tenant_ref, slot_ref, tokens_hbm, *refs):
    *outs, at_ref, note_ref, left_ref, tokens_ref, sems = refs
    half = tokens_ref.shape[1] // 2
    copies = row_copies(tokens_hbm, tokens_ref, sems, PARTS)
    for copy in copies:
        copy.start()
    tenant = tenant_ref[...]
    rows = tenant.shape[1]
    planes = len(outs)
    main_rows = planes * PLANE * room

    def iota(size, axis=0):
        return lax.broadcasted_iota(jnp.int32, (size, rows), axis)

    table = jnp.broadcast_to(slot_ref[...].astype(jnp.float32), (16, TENANTS)).astype(jnp.bfloat16)
    slot = jnp.dot(table, one_hot(iota(TENANTS) == tenant), preferred_element_type=jnp.float32)[:1]
    owner = slot.astype(jnp.int32) // local
    until = one_hot(iota(rows) < iota(rows, 1))
    place = earlier(iota(planes * PLANE) == owner, until)
    plane = (owner ^ me_ref[0]) // PLANE
    over = place >= room
    over_place = earlier((iota(16) == plane) & over, until)
    left = over & (over_place >= SPARE)
    at = jnp.where(over, main_rows + plane * SPARE + over_place, owner * room + place)
    at = jnp.where(left, -1, at)
    at_ref[...] = at
    most = jnp.max(left.astype(jnp.float32), axis=1, keepdims=True).astype(jnp.int32)
    left_ref[...] = jnp.broadcast_to(most, left_ref.shape)
    note = jnp.where(iota(NOTE) == 0, slot + 1.0, 0.0).astype(jnp.bfloat16)
    note_ref[...] = note

    row = iota(2 * SPARE)
    upper = row >= SPARE
    ids = jnp.where(upper, row - SPARE, row)
    ids = jnp.concatenate([ids + main_rows + b * SPARE for b in range(planes)], axis=0)
    upper = jnp.concatenate([upper] * planes, axis=0)
    hit = ids == at
    first, second = one_hot(hit & ~upper), one_hot(hit & upper)

    def put(value, columns):
        for b in range(planes):
            outs[b][:, columns] = value[2 * SPARE * b : 2 * SPARE * (b + 1)].astype(jnp.bfloat16)

    put(notes_of(one_hot(hit), note), slice(half, half + NOTE))
    for copy in copies:
        copy.wait()
    for c in range(0, half, STEP):
        put(
            jnp.dot(first, tokens_ref[:, c : c + STEP], preferred_element_type=jnp.float32)
            + jnp.dot(
                second,
                tokens_ref[:, half + c : half + c + STEP],
                preferred_element_type=jnp.float32,
            ),
            slice(c, c + STEP),
        )


def notes_of(pick, note):
    return lax.dot_general(
        pick, note, (((1,), (1,)), ((), ())), preferred_element_type=jnp.float32
    )


def pack_body(at_ref, note_ref, tokens_ref, out_hbm, out_ref, sems):
    depth = tokens_ref.shape[1]
    stores = row_copies(out_ref, out_hbm, sems, PARTS)
    half = out_ref.shape[0] // 2
    row = lax.broadcasted_iota(jnp.int32, (half, at_ref.shape[1]), 0)
    for h in range(2):
        own = slice(h * half, (h + 1) * half)
        pick = one_hot(row + h * half == at_ref[...])
        for c in range(0, depth, STEP):
            out_ref[own, c : c + STEP] = jnp.dot(
                pick, tokens_ref[:, c : c + STEP], preferred_element_type=jnp.float32
            ).astype(jnp.bfloat16)
        out_ref[own, depth:] = notes_of(pick, note_ref[...]).astype(jnp.bfloat16)
        for store in stores[h * PARTS // 2 : (h + 1) * PARTS // 2]:
            store.start()
    for store in stores:
        store.wait()


def pack(main_rows, at, note, tokens):
    rows, depth = tokens.shape
    out = jax.ShapeDtypeStruct((main_rows, depth + NOTE), jnp.bfloat16)
    return pl.pallas_call(
        pack_body,
        in_specs=[VMEM, VMEM, VMEM],
        out_specs=pl.BlockSpec(memory_space=pltpu.HBM),
        out_shape=out,
        scratch_shapes=[
            pltpu.VMEM(out.shape, jnp.bfloat16),
            pltpu.SemaphoreType.DMA((PARTS,)),
        ],
        compiler_params=pltpu.CompilerParams(vmem_limit_bytes=52 * 2**20),
        cost_estimate=pl.CostEstimate(
            flops=2 * main_rows * rows * depth, bytes_accessed=8 * 2**20, transcendentals=0
        ),
    )(at, note, tokens)


def low_delta(low, note, first, rank, up):
    column = lax.broadcasted_iota(jnp.int32, low.shape, 1) // rank + (first + 1)
    low = jnp.where(note.astype(jnp.float32) == column.astype(jnp.float32), low, 0.0)
    return jnp.dot(low.astype(jnp.bfloat16), up, preferred_element_type=jnp.float32)


def adapt_body(rank, first_ref, down_hbm, up_ref, rows_hbm, out, *scratch):
    down_ref, rows_ref, down_sems, sems = scratch
    depth = down_ref.shape[1]
    factors = row_copies(down_hbm, down_ref, down_sems, PARTS)
    copies = row_copies(rows_hbm, rows_ref, sems, PARTS)
    for copy in factors + copies:
        copy.start()
    for copy in factors:
        copy.wait()
    half = rows_ref.shape[0] // 2
    for h in range(2):
        for copy in copies[h * PARTS // 2 : (h + 1) * PARTS // 2]:
            copy.wait()
        own = slice(h * half, (h + 1) * half)
        low = jnp.zeros((half, down_ref.shape[0]), jnp.float32)
        for c in range(0, depth, STEP):
            low += lax.dot_general(
                rows_ref[own, c : c + STEP],
                down_ref[:, c : c + STEP],
                (((1,), (1,)), ((), ())),
                preferred_element_type=jnp.float32,
            )
        note = rows_ref[own, depth:].astype(jnp.float32)[:, :1]
        out[own] = low_delta(low, note, first_ref[0], rank, up_ref[...]).astype(jnp.bfloat16)


def adapt(rank, first, down, up, got):
    rows, width = got.shape[0], up.shape[1]
    return pl.pallas_call(
        functools.partial(adapt_body, rank),
        in_specs=[SMEM, ANY, VMEM, ANY],
        out_specs=VMEM,
        out_shape=jax.ShapeDtypeStruct((rows, width), jnp.bfloat16),
        scratch_shapes=[
            pltpu.VMEM(down.shape, jnp.bfloat16),
            pltpu.VMEM(got.shape, jnp.bfloat16),
            pltpu.SemaphoreType.DMA((PARTS,)),
            pltpu.SemaphoreType.DMA((PARTS,)),
        ],
        compiler_params=pltpu.CompilerParams(vmem_limit_bytes=24 * 2**20),
        cost_estimate=pl.CostEstimate(
            flops=2 * rows * down.size, bytes_accessed=8 * 2**20, transcendentals=0
        ),
    )(first, down, up, got)


def adapt_over_body(planes, rank, first_ref, down_hbm, up_ref, flag_ref, *refs):
    rows_refs, outs = refs[:PLANE], refs[PLANE : 2 * PLANE]
    down_ref, sems = refs[2 * PLANE :]
    half = down_ref.shape[1] // 2
    copies = row_copies(down_hbm, down_ref, sems, PARTS)
    for copy in copies:
        copy.start()
    each = rows_refs[0].shape[0]
    shape = (PLANE * each, down_ref.shape[0])
    dims = (((1,), (1,)), ((), ()))
    low0, low1 = jnp.zeros(shape, jnp.float32), jnp.zeros(shape, jnp.float32)
    for copy in copies:
        copy.wait()
    for c in range(0, half, STEP):
        rows = jnp.concatenate([r[:, c : c + STEP] for r in rows_refs], axis=0)
        low0 += lax.dot_general(
            rows, down_ref[:, c : c + STEP], dims, preferred_element_type=jnp.float32
        )
        low1 += lax.dot_general(
            rows, down_ref[:, half + c : half + c + STEP], dims, preferred_element_type=jnp.float32
        )
    zeros = jnp.zeros((16 - SPARE, shape[1]), jnp.float32)
    no_note = jnp.zeros((16 - SPARE, NOTE), jnp.float32)
    lows, notes = [], []
    for a in range(PLANE):
        note = rows_refs[a][:, half : half + NOTE].astype(jnp.float32)
        for b in range(planes):
            s = 2 * SPARE * b
            m = a * each + s
            lows += [low0[m : m + SPARE] + low1[m + SPARE : m + 2 * SPARE], zeros]
            notes += [note[s : s + SPARE], no_note]
    low = jnp.concatenate(lows, axis=0)
    note = jnp.concatenate(notes, axis=0)[:, :1]
    delta = low_delta(low, note, first_ref[0], rank, up_ref[...])
    row = lax.broadcasted_iota(jnp.int32, delta.shape, 0) % 16
    flag = flag_ref[...][:, :1].astype(jnp.float32)
    delta = jnp.where(row == SPARE, flag, delta).astype(jnp.bfloat16)
    for a, out in enumerate(outs):
        out[...] = delta[16 * planes * a : 16 * planes * (a + 1)]


def final_body(at_ref, base_ref, back_ref, *refs):
    *overs, out, seen_ref = refs
    seen = sum(o[...][SPARE:, :1].astype(jnp.float32) for o in overs)
    seen_ref[0] = jnp.max(seen).astype(jnp.int32)
    back = jnp.concatenate([back_ref[...]] + [o[...] for o in overs], axis=0)
    main_rows, size = back_ref.shape[0], overs[0].shape[0]
    row = lax.broadcasted_iota(jnp.int32, (back.shape[0], at_ref.shape[1]), 0)
    b, i = (row - main_rows) // size, (row - main_rows) % size
    spare = jnp.where(i < SPARE, main_rows + b * SPARE + i, -2)
    pick = jnp.where(row < main_rows, row, spare) == at_ref[...]
    pick = pick.astype(jnp.float32).astype(jnp.bfloat16)
    delta = lax.dot_general(
        pick, back, (((0,), (0,)), ((), ())), preferred_element_type=jnp.float32
    )
    out[...] = (base_ref[...] + delta).astype(jnp.bfloat16)


def call(body, outs, args, specs, flops, moved, scratch=()):
    return pl.pallas_call(
        body,
        in_specs=specs,
        out_specs=[VMEM] * len(outs),
        out_shape=[jax.ShapeDtypeStruct(s, jnp.bfloat16) for s in outs],
        scratch_shapes=list(scratch),
        compiler_params=pltpu.CompilerParams(vmem_limit_bytes=40 * 2**20),
        cost_estimate=pl.CostEstimate(flops=flops, bytes_accessed=moved, transcendentals=0),
    )(*args)


def swap(x, k):
    count = lax.axis_size("ad")
    return lax.ppermute(x, "ad", [(s, s ^ k) for s in range(count)])


def route(tenant_ids, tenant_slot, local):
    tenant = tenant_ids[:, 0]
    tenant_match = tenant[:, None] == jnp.arange(TENANTS, dtype=jnp.int32)[None, :]
    slot = jnp.sum(jnp.where(tenant_match, tenant_slot[None, :], 0), axis=1)
    owner = slot // local
    order = jnp.arange(tenant.shape[0], dtype=jnp.int32)
    before = order[None, :] < order[:, None]
    place = jnp.sum(((owner[:, None] == owner[None, :]) & before).astype(jnp.int32), axis=1)
    return slot, owner, place


def on_device(tokens, value_weight, adapt_down, adapt_up, tenant_ids, tenant_slot):
    row_count, depth = tokens.shape
    count = lax.axis_size("ad")
    me = lax.axis_index("ad")
    local, _, rank = adapt_down.shape
    width = adapt_up.shape[2]
    base_value = jnp.dot(tokens, value_weight, preferred_element_type=jnp.float32)
    room = row_count // count
    planes = count // PLANE
    if count != 16 or room != 16 or depth % (2 * STEP):
        slot, owner, place = route(tenant_ids, tenant_slot, local)
        delta = exchange(tokens, slot, owner, place, CAP * local, adapt_down, adapt_up)
        return (base_value + delta).astype(jnp.bfloat16)

    main_rows = count * room
    *spare, at, note, left = pl.pallas_call(
        functools.partial(route_body, room, local),
        in_specs=[SMEM, VMEM, VMEM, ANY],
        out_specs=[VMEM] * (planes + 3),
        out_shape=[jax.ShapeDtypeStruct((2 * SPARE, depth // 2 + NOTE), jnp.bfloat16)] * planes
        + [
            jax.ShapeDtypeStruct((1, row_count), jnp.int32),
            jax.ShapeDtypeStruct((NOTE, row_count), jnp.bfloat16),
            jax.ShapeDtypeStruct((1, NOTE), jnp.int32),
        ],
        scratch_shapes=[
            pltpu.VMEM(tokens.shape, jnp.bfloat16),
            pltpu.SemaphoreType.DMA((PARTS,)),
        ],
        compiler_params=pltpu.CompilerParams(vmem_limit_bytes=24 * 2**20),
        cost_estimate=pl.CostEstimate(
            flops=4 * 96 * row_count * depth, bytes_accessed=6 * 2**20, transcendentals=0
        ),
    )(me.reshape(1), tenant_ids.reshape(1, row_count), tenant_slot.reshape(1, TENANTS), tokens)

    along = [spare[0]] + [swap(spare[b], b * PLANE) for b in range(1, planes)]

    blocks = pack(main_rows, at, note, tokens)

    along = jnp.concatenate(along, axis=0)
    along, left = lax.optimization_barrier((along, left))
    groups = lax.axis_size("grp")
    flag = left
    for g in range(1, groups):
        other = lax.ppermute(left, "grp", [(s, (s + g) % groups) for s in range(groups)])
        flag = jnp.maximum(flag, other)
    shared = [along] + [swap(along, a) for a in range(1, PLANE)]

    got = lax.all_to_all(
        blocks.reshape(count, room, depth + NOTE), "ad", split_axis=0, concat_axis=0, tiled=True
    ).reshape(main_rows, depth + NOTE)

    first = (me * local).reshape(1)
    down = adapt_down.transpose(0, 2, 1).reshape(local * rank, depth)
    up = adapt_up.reshape(local * rank, width)

    flag, base_value = lax.optimization_barrier((flag, base_value))
    over_delta = call(
        functools.partial(adapt_over_body, planes, rank),
        [(16 * planes, width)] * PLANE,
        (first, down, up, flag, *shared),
        [SMEM, ANY] + [VMEM] * 6,
        10**12,
        6 * 2**20,
        [pltpu.VMEM(down.shape, jnp.bfloat16), pltpu.SemaphoreType.DMA((PARTS,))],
    )
    over_sum = over_delta[0]
    for a in range(1, PLANE):
        over_sum = over_sum + swap(over_delta[a], a)
    got, over_sum = lax.optimization_barrier((got, over_sum))
    delta = adapt(rank, first, down, up, got)
    delta, over_sum = lax.optimization_barrier((delta, over_sum))
    over_back = [over_sum[:16]]
    for b in range(1, planes):
        over_back.append(swap(over_sum[16 * b : 16 * (b + 1)], b * PLANE))
    back = lax.all_to_all(
        delta.reshape(count, room, width), "ad", split_axis=0, concat_axis=0, tiled=True
    ).reshape(main_rows, width)

    def finish(base):
        return pl.pallas_call(
            final_body,
            in_specs=[VMEM] * (3 + planes),
            out_specs=[VMEM, SMEM],
            out_shape=[
                jax.ShapeDtypeStruct((row_count, width), jnp.bfloat16),
                jax.ShapeDtypeStruct((1,), jnp.int32),
            ],
        )(at, base, back, *over_back)

    out, seen = finish(base_value)

    def more():
        slot, owner, place = route(tenant_ids, tenant_slot, local)
        extra = exchange(
            tokens,
            slot,
            owner,
            jnp.where(at[0] < 0, place - room, -1),
            CAP * local - room,
            adapt_down,
            adapt_up,
        )
        return finish(base_value + extra)[0]

    return lax.cond(seen[0] > 0, more, lambda: out)


def solution(mesh):
    placed = (
        P(("grp", "ad"), None),
        P(),
        P(("grp", "ad"), None, None),
        P(("grp", "ad"), None, None),
        P(("grp", "ad"), None),
        P("grp"),
    )
    return jax.shard_map(
        on_device, mesh=mesh, in_specs=placed, out_specs=P(("grp", "ad"), None), check_vma=False
    )
```

```python
import functools

import jax
import jax.numpy as jnp
from jax import lax
from jax.experimental import pallas as pl
from jax.experimental.pallas import tpu as pltpu
from jax.sharding import PartitionSpec as P

TENANTS = 256
CAP = 2
PLANE = 4
SPARE = 12
EXTRA = 8
NOTE = 128
STEP = 1024
WIDE = 1664
PARTS = 8
VMEM = pl.BlockSpec(memory_space=pltpu.VMEM)
ANY = pl.BlockSpec(memory_space=pl.ANY)
SMEM = pl.BlockSpec(memory_space=pltpu.SMEM)


def exchange(tokens, slot, owner, place, room, down, up):
    count = lax.axis_size("ad")
    local, depth, rank = down.shape
    width = up.shape[2]
    at = jnp.where((place >= 0) & (place < room), owner * room + place, -1)
    hits = at[None, :] == jnp.arange(count * room, dtype=jnp.int32)[:, None]
    slots = jnp.sum(jnp.where(hits, slot[None, :] + 1, 0), axis=1) - 1
    pick = hits.astype(jnp.bfloat16)
    sent = jnp.dot(pick, tokens, preferred_element_type=jnp.float32).astype(jnp.bfloat16)
    got = lax.all_to_all(
        sent.reshape(count, room, depth), "ad", split_axis=0, concat_axis=0, tiled=True
    ).reshape(count * room, depth)
    got_slots = lax.all_to_all(
        slots.reshape(count, room), "ad", split_axis=0, concat_axis=0, tiled=True
    ).reshape(count * room)
    low_rank = jnp.einsum("td,ldr->tlr", got, down, preferred_element_type=jnp.float32)
    own = (got_slots - lax.axis_index("ad") * local)[:, None] == jnp.arange(local)[None, :]
    low_rank = jnp.where(own[:, :, None], low_rank, 0.0).astype(jnp.bfloat16)
    delta = jnp.dot(
        low_rank.reshape(count * room, local * rank),
        up.reshape(local * rank, width),
        preferred_element_type=jnp.float32,
    ).astype(jnp.bfloat16)
    back = lax.all_to_all(
        delta.reshape(count, room, width), "ad", split_axis=0, concat_axis=0, tiled=True
    )
    return jnp.dot(
        pick.T, back.reshape(count * room, width), preferred_element_type=jnp.float32
    )


def row_copies(source, target, sems, parts):
    rows = target.shape[0] // parts
    return [
        pltpu.make_async_copy(
            source.at[i * rows : (i + 1) * rows], target.at[i * rows : (i + 1) * rows], sems.at[i]
        )
        for i in range(parts)
    ]


def one_hot(hit):
    return hit.astype(jnp.float32).astype(jnp.bfloat16)


def earlier(hit, until):
    counts = jnp.dot(one_hot(hit), until, preferred_element_type=jnp.float32)
    return jnp.sum(jnp.where(hit, counts, 0.0), axis=0, keepdims=True).astype(jnp.int32)


def route_body(room, local, me_ref, tenant_ref, slot_ref, tokens_hbm, *refs):
    *outs, at_ref, back_ref, note_ref, tokens_ref, sems = refs
    half = tokens_ref.shape[1] // 2
    copies = row_copies(tokens_hbm, tokens_ref, sems, PARTS)
    for copy in copies:
        copy.start()
    tenant = tenant_ref[...]
    rows = tenant.shape[1]
    planes = len(outs)
    main_rows = planes * PLANE * room

    def iota(size, axis=0):
        return lax.broadcasted_iota(jnp.int32, (size, rows), axis)

    table = jnp.broadcast_to(slot_ref[...].astype(jnp.float32), (16, TENANTS)).astype(jnp.bfloat16)
    slot = jnp.dot(table, one_hot(iota(TENANTS) == tenant), preferred_element_type=jnp.float32)[:1]
    owner = slot.astype(jnp.int32) // local
    until = one_hot(iota(rows) < iota(rows, 1))
    place = earlier(iota(planes * PLANE) == owner, until)
    plane = (owner ^ me_ref[0]) // PLANE
    over = place >= room
    over_place = earlier((iota(16) == plane) & over, until)
    left = over & ((over_place >= SPARE) | (place >= room + EXTRA))
    at = jnp.where(over, main_rows + plane * SPARE + over_place, owner * room + place)
    at = jnp.where(left, -1, at)
    at_ref[...] = at
    back_ref[...] = jnp.where(left, -1, owner * (room + EXTRA) + place)
    note = jnp.where(iota(NOTE) == 0, slot + 1.0, 0.0)
    note = jnp.where(iota(NOTE) == 1, place.astype(jnp.float32), note).astype(jnp.bfloat16)
    note_ref[...] = note
    most = jnp.max(left.astype(jnp.float32), axis=1, keepdims=True)

    row = iota(2 * SPARE)
    upper = row >= SPARE
    ids = jnp.where(upper, row - SPARE, row)
    ids = jnp.concatenate([ids + main_rows + b * SPARE for b in range(planes)], axis=0)
    upper = jnp.concatenate([upper] * planes, axis=0)
    hit = ids == at
    first, second = one_hot(hit & ~upper), one_hot(hit & upper)

    def put(value, columns):
        for b in range(planes):
            outs[b][:, columns] = value[2 * SPARE * b : 2 * SPARE * (b + 1)].astype(jnp.bfloat16)

    notes = notes_of(one_hot(hit), note)
    flag = lax.broadcasted_iota(jnp.int32, notes.shape, 1) == 2
    put(jnp.where(flag, most, notes), slice(half, half + NOTE))
    for copy in copies:
        copy.wait()
    for c in range(0, half, STEP):
        put(
            jnp.dot(first, tokens_ref[:, c : c + STEP], preferred_element_type=jnp.float32)
            + jnp.dot(
                second,
                tokens_ref[:, half + c : half + c + STEP],
                preferred_element_type=jnp.float32,
            ),
            slice(c, c + STEP),
        )


def notes_of(pick, note):
    return lax.dot_general(
        pick, note, (((1,), (1,)), ((), ())), preferred_element_type=jnp.float32
    )


def pack_body(at_ref, note_ref, tokens_ref, out_hbm, out_ref, sems):
    depth = tokens_ref.shape[1]
    stores = row_copies(out_ref, out_hbm, sems, PARTS)
    half = out_ref.shape[0] // 2
    row = lax.broadcasted_iota(jnp.int32, (half, at_ref.shape[1]), 0)
    for h in range(2):
        own = slice(h * half, (h + 1) * half)
        pick = one_hot(row + h * half == at_ref[...])
        for c in range(0, depth, STEP):
            out_ref[own, c : c + STEP] = jnp.dot(
                pick, tokens_ref[:, c : c + STEP], preferred_element_type=jnp.float32
            ).astype(jnp.bfloat16)
        out_ref[own, depth:] = notes_of(pick, note_ref[...]).astype(jnp.bfloat16)
        for store in stores[h * PARTS // 2 : (h + 1) * PARTS // 2]:
            store.start()
    for store in stores:
        store.wait()


def pack(main_rows, at, note, tokens):
    rows, depth = tokens.shape
    out = jax.ShapeDtypeStruct((main_rows, depth + NOTE), jnp.bfloat16)
    return pl.pallas_call(
        pack_body,
        in_specs=[VMEM, VMEM, VMEM],
        out_specs=pl.BlockSpec(memory_space=pltpu.HBM),
        out_shape=out,
        scratch_shapes=[
            pltpu.VMEM(out.shape, jnp.bfloat16),
            pltpu.SemaphoreType.DMA((PARTS,)),
        ],
        compiler_params=pltpu.CompilerParams(vmem_limit_bytes=52 * 2**20),
        cost_estimate=pl.CostEstimate(
            flops=2 * main_rows * rows * depth, bytes_accessed=8 * 2**20, transcendentals=0
        ),
    )(at, note, tokens)


def low_delta(low, note, first, rank, up):
    column = lax.broadcasted_iota(jnp.int32, low.shape, 1) // rank + (first + 1)
    low = jnp.where(note.astype(jnp.float32) == column.astype(jnp.float32), low, 0.0)
    return jnp.dot(low.astype(jnp.bfloat16), up, preferred_element_type=jnp.float32)


def adapt_body(rank, me_ref, down_hbm, up_ref, rows_hbm, extra_ref, out, *scratch):
    down_ref, rows_ref, down_sems, sems = scratch
    depth = down_ref.shape[1]
    spans = [slice(c, min(c + WIDE, depth + NOTE)) for c in range(0, depth + NOTE, WIDE)]
    copies = []
    for i, span in enumerate(spans):
        kept = slice(span.start, min(span.stop, depth))
        copies.append(
            (
                pltpu.make_async_copy(rows_hbm.at[:, span], rows_ref.at[:, span], sems.at[i]),
                pltpu.make_async_copy(down_hbm.at[:, kept], down_ref.at[:, kept], down_sems.at[i]),
            )
        )
    for pair in copies:
        pair[0].start()
        pair[1].start()
    low = jnp.zeros((rows_ref.shape[0], down_ref.shape[0]), jnp.float32)
    for pair, span in zip(copies, spans, strict=True):
        pair[0].wait()
        pair[1].wait()
        span = slice(span.start, min(span.stop, depth))
        low += lax.dot_general(
            rows_ref[:, span],
            down_ref[:, span],
            (((1,), (1,)), ((), ())),
            preferred_element_type=jnp.float32,
        )
    note = rows_ref[:, depth:].astype(jnp.float32)
    sources = out.shape[0]
    first = me_ref[0] * (down_ref.shape[0] // rank)
    delta = low_delta(low, note[:, :1], first, rank, up_ref[...])
    room = delta.shape[0] // sources
    for s in range(sources):
        k = me_ref[0] ^ s
        extra = extra_ref[(k % PLANE) * (sources // PLANE) + k // PLANE]
        rows = jnp.concatenate([delta[s * room : (s + 1) * room], extra], axis=0)
        out[s] = rows.astype(jnp.bfloat16)


def adapt(rank, me, down, up, got, extra):
    rows, width = got.shape[0], up.shape[1]
    count = extra.shape[0]
    return pl.pallas_call(
        functools.partial(adapt_body, rank),
        in_specs=[SMEM, ANY, VMEM, ANY, VMEM],
        out_specs=VMEM,
        out_shape=jax.ShapeDtypeStruct((count, rows // count + EXTRA, width), jnp.bfloat16),
        scratch_shapes=[
            pltpu.VMEM(down.shape, jnp.bfloat16),
            pltpu.VMEM(got.shape, jnp.bfloat16),
            pltpu.SemaphoreType.DMA((pl.cdiv(got.shape[1], WIDE),)),
            pltpu.SemaphoreType.DMA((pl.cdiv(got.shape[1], WIDE),)),
        ],
        compiler_params=pltpu.CompilerParams(vmem_limit_bytes=24 * 2**20),
        cost_estimate=pl.CostEstimate(
            flops=2 * rows * down.size, bytes_accessed=8 * 2**20, transcendentals=0
        ),
    )(me, down, up, got, extra)


def adapt_over_body(planes, rank, first_ref, down_hbm, up_ref, *refs):
    rows_refs = refs[:PLANE]
    out, flag_out, down_ref, sems = refs[PLANE:]
    half = down_ref.shape[1] // 2
    copies = row_copies(down_hbm, down_ref, sems, PARTS)
    for copy in copies:
        copy.start()
    each = rows_refs[0].shape[0]
    shape = (PLANE * each, down_ref.shape[0])
    dims = (((1,), (1,)), ((), ()))
    low0, low1 = jnp.zeros(shape, jnp.float32), jnp.zeros(shape, jnp.float32)
    for copy in copies:
        copy.wait()
    for c in range(0, half, STEP):
        rows = jnp.concatenate([r[:, c : c + STEP] for r in rows_refs], axis=0)
        low0 += lax.dot_general(
            rows, down_ref[:, c : c + STEP], dims, preferred_element_type=jnp.float32
        )
        low1 += lax.dot_general(
            rows, down_ref[:, half + c : half + c + STEP], dims, preferred_element_type=jnp.float32
        )
    zeros = jnp.zeros((16 - SPARE, shape[1]), jnp.float32)
    no_note = jnp.zeros((16 - SPARE, NOTE), jnp.float32)
    lows, notes = [], []
    for a in range(PLANE):
        note = rows_refs[a][:, half : half + NOTE].astype(jnp.float32)
        for b in range(planes):
            s = 2 * SPARE * b
            m = a * each + s
            lows += [low0[m : m + SPARE] + low1[m + SPARE : m + 2 * SPARE], zeros]
            notes += [note[s : s + SPARE], no_note]
    low = jnp.concatenate(lows, axis=0)
    note = jnp.concatenate(notes, axis=0)
    delta = low_delta(low, note[:, :1], first_ref[0], rank, up_ref[...]).astype(jnp.bfloat16)
    shape = (delta.shape[0], PLANE * planes * EXTRA)
    row, column = (lax.broadcasted_iota(jnp.int32, shape, axis) for axis in (0, 1))
    own = (note[:, :1].astype(jnp.int32) - 1) // (down_ref.shape[0] // rank) == first_ref[
        0
    ] // (down_ref.shape[0] // rank)
    own = own & (note[:, :1] > 0)
    put = (note[:, 1:2].astype(jnp.int32) == 16 + column % EXTRA) & (row // 16 == column // EXTRA)
    extra = lax.dot_general(
        one_hot(put & own), delta, (((0,), (0,)), ((), ())), preferred_element_type=jnp.float32
    )
    for g in range(PLANE * planes):
        out[g] = extra[g * EXTRA : (g + 1) * EXTRA]
    flags = [jnp.max(r[:, half : half + NOTE].astype(jnp.float32), axis=0) for r in rows_refs]
    most = functools.reduce(jnp.maximum, flags).reshape(1, NOTE)
    flag_out[...] = most.astype(jnp.int32)


def final_body(at_ref, base_ref, back_ref, out):
    row = lax.broadcasted_iota(jnp.int32, (back_ref.shape[0], at_ref.shape[1]), 0)
    delta = lax.dot_general(
        one_hot(row == at_ref[...]),
        back_ref[...],
        (((0,), (0,)), ((), ())),
        preferred_element_type=jnp.float32,
    )
    out[...] = (base_ref[...] + delta).astype(jnp.bfloat16)


def swap(x, k):
    count = lax.axis_size("ad")
    return lax.ppermute(x, "ad", [(s, s ^ k) for s in range(count)])


def route(tenant_ids, tenant_slot, local):
    tenant = tenant_ids[:, 0]
    tenant_match = tenant[:, None] == jnp.arange(TENANTS, dtype=jnp.int32)[None, :]
    slot = jnp.sum(jnp.where(tenant_match, tenant_slot[None, :], 0), axis=1)
    owner = slot // local
    order = jnp.arange(tenant.shape[0], dtype=jnp.int32)
    before = order[None, :] < order[:, None]
    place = jnp.sum(((owner[:, None] == owner[None, :]) & before).astype(jnp.int32), axis=1)
    return slot, owner, place


def on_device(tokens, value_weight, adapt_down, adapt_up, tenant_ids, tenant_slot):
    row_count, depth = tokens.shape
    count = lax.axis_size("ad")
    me = lax.axis_index("ad")
    local, _, rank = adapt_down.shape
    width = adapt_up.shape[2]
    base_value = jnp.dot(tokens, value_weight, preferred_element_type=jnp.float32)
    room = row_count // count
    planes = count // PLANE
    if count != 16 or room != 16 or depth % (2 * STEP):
        slot, owner, place = route(tenant_ids, tenant_slot, local)
        delta = exchange(tokens, slot, owner, place, CAP * local, adapt_down, adapt_up)
        return (base_value + delta).astype(jnp.bfloat16)

    main_rows = count * room
    *spare, at, at_back, note = pl.pallas_call(
        functools.partial(route_body, room, local),
        in_specs=[SMEM, VMEM, VMEM, ANY],
        out_specs=[VMEM] * (planes + 3),
        out_shape=[jax.ShapeDtypeStruct((2 * SPARE, depth // 2 + NOTE), jnp.bfloat16)] * planes
        + [
            jax.ShapeDtypeStruct((1, row_count), jnp.int32),
            jax.ShapeDtypeStruct((1, row_count), jnp.int32),
            jax.ShapeDtypeStruct((NOTE, row_count), jnp.bfloat16),
        ],
        scratch_shapes=[
            pltpu.VMEM(tokens.shape, jnp.bfloat16),
            pltpu.SemaphoreType.DMA((PARTS,)),
        ],
        compiler_params=pltpu.CompilerParams(vmem_limit_bytes=24 * 2**20),
        cost_estimate=pl.CostEstimate(
            flops=4 * 96 * row_count * depth, bytes_accessed=6 * 2**20, transcendentals=0
        ),
    )(me.reshape(1), tenant_ids.reshape(1, row_count), tenant_slot.reshape(1, TENANTS), tokens)

    along = [spare[0]] + [swap(spare[b], b * PLANE) for b in range(1, planes)]

    blocks = pack(main_rows, at, note, tokens)

    along = jnp.concatenate(along, axis=0)
    shared = [along] + [swap(along, a) for a in range(1, PLANE)]

    got = lax.all_to_all(
        blocks.reshape(count, room, depth + NOTE), "ad", split_axis=0, concat_axis=0, tiled=True
    ).reshape(main_rows, depth + NOTE)

    first = (me * local).reshape(1)
    down = adapt_down.transpose(0, 2, 1).reshape(local * rank, depth)
    up = adapt_up.reshape(local * rank, width)

    shared[0], base_value = lax.optimization_barrier((shared[0], base_value))
    extra, flag = pl.pallas_call(
        functools.partial(adapt_over_body, planes, rank),
        in_specs=[SMEM, ANY] + [VMEM] * (1 + PLANE),
        out_specs=[VMEM, VMEM],
        out_shape=[
            jax.ShapeDtypeStruct((count, EXTRA, width), jnp.float32),
            jax.ShapeDtypeStruct((1, NOTE), jnp.int32),
        ],
        scratch_shapes=[pltpu.VMEM(down.shape, jnp.bfloat16), pltpu.SemaphoreType.DMA((PARTS,))],
        compiler_params=pltpu.CompilerParams(vmem_limit_bytes=40 * 2**20),
        cost_estimate=pl.CostEstimate(
            flops=10**12,
            bytes_accessed=6 * 2**20,
            transcendentals=0,
        ),
    )(first, down, up, *shared)

    groups = lax.axis_size("grp")
    own = flag[0, 2]
    seen = own
    for g in range(1, groups):
        other = lax.ppermute(own, "grp", [(s, (s + g) % groups) for s in range(groups)])
        seen = jnp.maximum(seen, other)
    got, extra, seen = lax.optimization_barrier((got, extra, seen))
    delta = adapt(rank, me.reshape(1), down, up, got, extra)
    back = lax.all_to_all(delta, "ad", split_axis=0, concat_axis=0, tiled=True)
    back = back.reshape(count * (room + EXTRA), width)

    def finish(base):
        return pl.pallas_call(
            final_body,
            in_specs=[VMEM] * 3,
            out_specs=VMEM,
            out_shape=jax.ShapeDtypeStruct((row_count, width), jnp.bfloat16),
        )(at_back, base, back)

    def more():
        slot, owner, place = route(tenant_ids, tenant_slot, local)
        extra = exchange(
            tokens,
            slot,
            owner,
            jnp.where(at[0] < 0, place - room, -1),
            CAP * local - room,
            adapt_down,
            adapt_up,
        )
        return finish(base_value + extra)

    return lax.cond(seen > 0, more, lambda: finish(base_value))


def solution(mesh):
    placed = (
        P(("grp", "ad"), None),
        P(),
        P(("grp", "ad"), None, None),
        P(("grp", "ad"), None, None),
        P(("grp", "ad"), None),
        P("grp"),
    )
    return jax.shard_map(
        on_device, mesh=mesh, in_specs=placed, out_specs=P(("grp", "ad"), None), check_vma=False
    )
```

```python
import functools

import jax
import jax.numpy as jnp
from jax import lax
from jax.experimental import pallas as pl
from jax.experimental.pallas import tpu as pltpu
from jax.sharding import PartitionSpec as P

TENANTS = 256
CAP = 2
PLANE = 4
SPARE = 12
EXTRA = 8
NOTE = 128
STEP = 1024
WIDE = 1664
PARTS = 8
VMEM = pl.BlockSpec(memory_space=pltpu.VMEM)
ANY = pl.BlockSpec(memory_space=pl.ANY)
SMEM = pl.BlockSpec(memory_space=pltpu.SMEM)


def exchange(tokens, slot, owner, place, room, down, up):
    count = lax.axis_size("ad")
    local, depth, rank = down.shape
    width = up.shape[2]
    at = jnp.where((place >= 0) & (place < room), owner * room + place, -1)
    hits = at[None, :] == jnp.arange(count * room, dtype=jnp.int32)[:, None]
    slots = jnp.sum(jnp.where(hits, slot[None, :] + 1, 0), axis=1) - 1
    pick = hits.astype(jnp.bfloat16)
    sent = jnp.dot(pick, tokens, preferred_element_type=jnp.float32).astype(jnp.bfloat16)
    got = lax.all_to_all(
        sent.reshape(count, room, depth), "ad", split_axis=0, concat_axis=0, tiled=True
    ).reshape(count * room, depth)
    got_slots = lax.all_to_all(
        slots.reshape(count, room), "ad", split_axis=0, concat_axis=0, tiled=True
    ).reshape(count * room)
    low_rank = jnp.einsum("td,ldr->tlr", got, down, preferred_element_type=jnp.float32)
    own = (got_slots - lax.axis_index("ad") * local)[:, None] == jnp.arange(local)[None, :]
    low_rank = jnp.where(own[:, :, None], low_rank, 0.0).astype(jnp.bfloat16)
    delta = jnp.dot(
        low_rank.reshape(count * room, local * rank),
        up.reshape(local * rank, width),
        preferred_element_type=jnp.float32,
    ).astype(jnp.bfloat16)
    back = lax.all_to_all(
        delta.reshape(count, room, width), "ad", split_axis=0, concat_axis=0, tiled=True
    )
    return jnp.dot(
        pick.T, back.reshape(count * room, width), preferred_element_type=jnp.float32
    )


def row_copies(source, target, sems, parts):
    rows = target.shape[0] // parts
    return [
        pltpu.make_async_copy(
            source.at[i * rows : (i + 1) * rows], target.at[i * rows : (i + 1) * rows], sems.at[i]
        )
        for i in range(parts)
    ]


def one_hot(hit):
    return hit.astype(jnp.float32).astype(jnp.bfloat16)


def earlier(hit, until):
    counts = jnp.dot(one_hot(hit), until, preferred_element_type=jnp.float32)
    return jnp.sum(jnp.where(hit, counts, 0.0), axis=0, keepdims=True).astype(jnp.int32)


def route_body(room, local, me_ref, tenant_ref, slot_ref, tokens_hbm, *refs):
    *outs, at_ref, back_ref, note_ref, tokens_ref, sems = refs
    half = tokens_ref.shape[1] // 2
    copies = row_copies(tokens_hbm, tokens_ref, sems, PARTS)
    for copy in copies:
        copy.start()
    tenant = tenant_ref[...]
    rows = tenant.shape[1]
    planes = len(outs)
    main_rows = planes * PLANE * room

    def iota(size, axis=0):
        return lax.broadcasted_iota(jnp.int32, (size, rows), axis)

    table = jnp.broadcast_to(slot_ref[...].astype(jnp.float32), (16, TENANTS)).astype(jnp.bfloat16)
    slot = jnp.dot(table, one_hot(iota(TENANTS) == tenant), preferred_element_type=jnp.float32)[:1]
    owner = slot.astype(jnp.int32) // local
    until = one_hot(iota(rows) < iota(rows, 1))
    place = earlier(iota(planes * PLANE) == owner, until)
    plane = (owner ^ me_ref[0]) // PLANE
    over = place >= room
    over_place = earlier((iota(16) == plane) & over, until)
    left = over & ((over_place >= SPARE) | (place >= room + EXTRA))
    at = jnp.where(over, main_rows + plane * SPARE + over_place, owner * room + place)
    at = jnp.where(left, -1, at)
    at_ref[...] = at
    back_ref[...] = jnp.where(left, -1, owner * (room + EXTRA) + place)
    note = jnp.where(iota(NOTE) == 0, slot + 1.0, 0.0)
    note = jnp.where(iota(NOTE) == 1, place.astype(jnp.float32), note).astype(jnp.bfloat16)
    note_ref[...] = note
    most = jnp.max(left.astype(jnp.float32), axis=1, keepdims=True)

    row = iota(2 * SPARE)
    upper = row >= SPARE
    ids = jnp.where(upper, row - SPARE, row)
    ids = jnp.concatenate([ids + main_rows + b * SPARE for b in range(planes)], axis=0)
    upper = jnp.concatenate([upper] * planes, axis=0)
    hit = ids == at
    first, second = one_hot(hit & ~upper), one_hot(hit & upper)

    def put(value, columns):
        for b in range(planes):
            outs[b][:, columns] = value[2 * SPARE * b : 2 * SPARE * (b + 1)].astype(jnp.bfloat16)

    notes = notes_of(one_hot(hit), note)
    flag = lax.broadcasted_iota(jnp.int32, notes.shape, 1) == 2
    put(jnp.where(flag, most, notes), slice(half, half + NOTE))
    for copy in copies:
        copy.wait()
    for c in range(0, half, STEP):
        put(
            jnp.dot(first, tokens_ref[:, c : c + STEP], preferred_element_type=jnp.float32)
            + jnp.dot(
                second,
                tokens_ref[:, half + c : half + c + STEP],
                preferred_element_type=jnp.float32,
            ),
            slice(c, c + STEP),
        )


def notes_of(pick, note):
    return lax.dot_general(
        pick, note, (((1,), (1,)), ((), ())), preferred_element_type=jnp.float32
    )


def pack_body(at_ref, note_ref, tokens_ref, out_hbm, out_ref, sems):
    depth = tokens_ref.shape[1]
    stores = row_copies(out_ref, out_hbm, sems, PARTS)
    half = out_ref.shape[0] // 2
    row = lax.broadcasted_iota(jnp.int32, (half, at_ref.shape[1]), 0)
    for h in range(2):
        own = slice(h * half, (h + 1) * half)
        pick = one_hot(row + h * half == at_ref[...])
        for c in range(0, depth, STEP):
            out_ref[own, c : c + STEP] = jnp.dot(
                pick, tokens_ref[:, c : c + STEP], preferred_element_type=jnp.float32
            ).astype(jnp.bfloat16)
        out_ref[own, depth:] = notes_of(pick, note_ref[...]).astype(jnp.bfloat16)
        for store in stores[h * PARTS // 2 : (h + 1) * PARTS // 2]:
            store.start()
    for store in stores:
        store.wait()


def pack(main_rows, at, note, tokens):
    rows, depth = tokens.shape
    out = jax.ShapeDtypeStruct((main_rows, depth + NOTE), jnp.bfloat16)
    return pl.pallas_call(
        pack_body,
        in_specs=[VMEM, VMEM, VMEM],
        out_specs=pl.BlockSpec(memory_space=pltpu.HBM),
        out_shape=out,
        scratch_shapes=[
            pltpu.VMEM(out.shape, jnp.bfloat16),
            pltpu.SemaphoreType.DMA((PARTS,)),
        ],
        compiler_params=pltpu.CompilerParams(vmem_limit_bytes=52 * 2**20),
        cost_estimate=pl.CostEstimate(
            flops=2 * main_rows * rows * depth, bytes_accessed=8 * 2**20, transcendentals=0
        ),
    )(at, note, tokens)


def low_delta(low, note, first, rank, up):
    column = lax.broadcasted_iota(jnp.int32, low.shape, 1) // rank + (first + 1)
    low = jnp.where(note.astype(jnp.float32) == column.astype(jnp.float32), low, 0.0)
    return jnp.dot(low.astype(jnp.bfloat16), up, preferred_element_type=jnp.float32)


def adapt_body(rank, me_ref, down_hbm, up_ref, rows_hbm, extra_ref, out, *scratch):
    down_ref, rows_ref, down_sems, sems = scratch
    depth = down_ref.shape[1]
    spans = [slice(c, min(c + WIDE, depth + NOTE)) for c in range(0, depth + NOTE, WIDE)]
    copies = []
    for i, span in enumerate(spans):
        kept = slice(span.start, min(span.stop, depth))
        copies.append(
            (
                pltpu.make_async_copy(rows_hbm.at[:, span], rows_ref.at[:, span], sems.at[i]),
                pltpu.make_async_copy(down_hbm.at[:, kept], down_ref.at[:, kept], down_sems.at[i]),
            )
        )
    for pair in copies:
        pair[0].start()
        pair[1].start()
    low = jnp.zeros((rows_ref.shape[0], down_ref.shape[0]), jnp.float32)
    for pair, span in zip(copies, spans, strict=True):
        pair[0].wait()
        pair[1].wait()
        span = slice(span.start, min(span.stop, depth))
        low += lax.dot_general(
            rows_ref[:, span],
            down_ref[:, span],
            (((1,), (1,)), ((), ())),
            preferred_element_type=jnp.float32,
        )
    note = rows_ref[:, depth:].astype(jnp.float32)
    sources = out.shape[0]
    first = me_ref[0] * (down_ref.shape[0] // rank)
    delta = low_delta(low, note[:, :1], first, rank, up_ref[...])
    room = delta.shape[0] // sources
    for s in range(sources):
        k = me_ref[0] ^ s
        extra = extra_ref[(k % PLANE) * (sources // PLANE) + k // PLANE]
        rows = jnp.concatenate([delta[s * room : (s + 1) * room], extra], axis=0)
        out[s] = rows.astype(jnp.bfloat16)


def adapt(rank, me, down, up, got, extra):
    rows, width = got.shape[0], up.shape[1]
    count = extra.shape[0]
    return pl.pallas_call(
        functools.partial(adapt_body, rank),
        in_specs=[SMEM, ANY, VMEM, ANY, VMEM],
        out_specs=VMEM,
        out_shape=jax.ShapeDtypeStruct((count, rows // count + EXTRA, width), jnp.bfloat16),
        scratch_shapes=[
            pltpu.VMEM(down.shape, jnp.bfloat16),
            pltpu.VMEM(got.shape, jnp.bfloat16),
            pltpu.SemaphoreType.DMA((pl.cdiv(got.shape[1], WIDE),)),
            pltpu.SemaphoreType.DMA((pl.cdiv(got.shape[1], WIDE),)),
        ],
        compiler_params=pltpu.CompilerParams(vmem_limit_bytes=24 * 2**20),
        cost_estimate=pl.CostEstimate(
            flops=2 * rows * down.size, bytes_accessed=8 * 2**20, transcendentals=0
        ),
    )(me, down, up, got, extra)


def adapt_over_body(planes, rank, first_ref, down_hbm, up_ref, *refs):
    rows_refs = refs[:PLANE]
    out, flag_out, down_ref, sems = refs[PLANE:]
    half = down_ref.shape[1] // 2
    copies = row_copies(down_hbm, down_ref, sems, PARTS)
    for copy in copies:
        copy.start()
    each = rows_refs[0].shape[0]
    shape = (PLANE * each, down_ref.shape[0])
    dims = (((1,), (1,)), ((), ()))
    low0, low1 = jnp.zeros(shape, jnp.float32), jnp.zeros(shape, jnp.float32)
    for copy in copies:
        copy.wait()
    for c in range(0, half, STEP):
        rows = jnp.concatenate([r[:, c : c + STEP] for r in rows_refs], axis=0)
        low0 += lax.dot_general(
            rows, down_ref[:, c : c + STEP], dims, preferred_element_type=jnp.float32
        )
        low1 += lax.dot_general(
            rows, down_ref[:, half + c : half + c + STEP], dims, preferred_element_type=jnp.float32
        )
    zeros = jnp.zeros((16 - SPARE, shape[1]), jnp.float32)
    no_note = jnp.zeros((16 - SPARE, NOTE), jnp.float32)
    lows, notes = [], []
    for a in range(PLANE):
        note = rows_refs[a][:, half : half + NOTE].astype(jnp.float32)
        for b in range(planes):
            s = 2 * SPARE * b
            m = a * each + s
            lows += [low0[m : m + SPARE] + low1[m + SPARE : m + 2 * SPARE], zeros]
            notes += [note[s : s + SPARE], no_note]
    low = jnp.concatenate(lows, axis=0)
    note = jnp.concatenate(notes, axis=0)
    delta = low_delta(low, note[:, :1], first_ref[0], rank, up_ref[...]).astype(jnp.bfloat16)
    shape = (delta.shape[0], PLANE * planes * EXTRA)
    row, column = (lax.broadcasted_iota(jnp.int32, shape, axis) for axis in (0, 1))
    own = (note[:, :1].astype(jnp.int32) - 1) // (down_ref.shape[0] // rank) == first_ref[
        0
    ] // (down_ref.shape[0] // rank)
    own = own & (note[:, :1] > 0)
    put = (note[:, 1:2].astype(jnp.int32) == 16 + column % EXTRA) & (row // 16 == column // EXTRA)
    extra = lax.dot_general(
        one_hot(put & own), delta, (((0,), (0,)), ((), ())), preferred_element_type=jnp.float32
    )
    for g in range(PLANE * planes):
        out[g] = extra[g * EXTRA : (g + 1) * EXTRA]
    flags = [jnp.max(r[:, half : half + NOTE].astype(jnp.float32), axis=0) for r in rows_refs]
    most = functools.reduce(jnp.maximum, flags).reshape(1, NOTE)
    flag_out[...] = most.astype(jnp.int32)


def final_body(at_ref, base_ref, back_ref, out):
    row = lax.broadcasted_iota(jnp.int32, (back_ref.shape[0], at_ref.shape[1]), 0)
    delta = lax.dot_general(
        one_hot(row == at_ref[...]),
        back_ref[...],
        (((0,), (0,)), ((), ())),
        preferred_element_type=jnp.float32,
    )
    out[...] = (base_ref[...] + delta).astype(jnp.bfloat16)


def swap(x, k):
    count = lax.axis_size("ad")
    return lax.ppermute(x, "ad", [(s, s ^ k) for s in range(count)])


def route(tenant_ids, tenant_slot, local):
    tenant = tenant_ids[:, 0]
    tenant_match = tenant[:, None] == jnp.arange(TENANTS, dtype=jnp.int32)[None, :]
    slot = jnp.sum(jnp.where(tenant_match, tenant_slot[None, :], 0), axis=1)
    owner = slot // local
    order = jnp.arange(tenant.shape[0], dtype=jnp.int32)
    before = order[None, :] < order[:, None]
    place = jnp.sum(((owner[:, None] == owner[None, :]) & before).astype(jnp.int32), axis=1)
    return slot, owner, place


def on_device(tokens, value_weight, adapt_down, adapt_up, tenant_ids, tenant_slot):
    row_count, depth = tokens.shape
    count = lax.axis_size("ad")
    me = lax.axis_index("ad")
    local, _, rank = adapt_down.shape
    width = adapt_up.shape[2]
    base_value = jnp.dot(tokens, value_weight, preferred_element_type=jnp.float32)
    room = row_count // count
    planes = count // PLANE
    if count != 16 or room != 16 or depth % (2 * STEP):
        slot, owner, place = route(tenant_ids, tenant_slot, local)
        delta = exchange(tokens, slot, owner, place, CAP * local, adapt_down, adapt_up)
        return (base_value + delta).astype(jnp.bfloat16)

    main_rows = count * room
    *spare, at, at_back, note = pl.pallas_call(
        functools.partial(route_body, room, local),
        in_specs=[SMEM, VMEM, VMEM, ANY],
        out_specs=[VMEM] * (planes + 3),
        out_shape=[jax.ShapeDtypeStruct((2 * SPARE, depth // 2 + NOTE), jnp.bfloat16)] * planes
        + [
            jax.ShapeDtypeStruct((1, row_count), jnp.int32),
            jax.ShapeDtypeStruct((1, row_count), jnp.int32),
            jax.ShapeDtypeStruct((NOTE, row_count), jnp.bfloat16),
        ],
        scratch_shapes=[
            pltpu.VMEM(tokens.shape, jnp.bfloat16),
            pltpu.SemaphoreType.DMA((PARTS,)),
        ],
        compiler_params=pltpu.CompilerParams(vmem_limit_bytes=24 * 2**20),
        cost_estimate=pl.CostEstimate(
            flops=4 * 96 * row_count * depth, bytes_accessed=6 * 2**20, transcendentals=0
        ),
    )(me.reshape(1), tenant_ids.reshape(1, row_count), tenant_slot.reshape(1, TENANTS), tokens)

    along = [swap(spare[b], b * PLANE) for b in range(planes - 1, 0, -1)]
    along = list(lax.optimization_barrier(tuple(along)))
    blocks = pack(main_rows, at, note, tokens)

    along = jnp.concatenate([spare[0]] + along[::-1], axis=0)
    shared = [along] + [swap(along, a) for a in range(1, PLANE)]

    got = lax.all_to_all(
        blocks.reshape(count, room, depth + NOTE), "ad", split_axis=0, concat_axis=0, tiled=True
    ).reshape(main_rows, depth + NOTE)

    first = (me * local).reshape(1)
    down = adapt_down.transpose(0, 2, 1).reshape(local * rank, depth)
    up = adapt_up.reshape(local * rank, width)

    shared[0], base_value = lax.optimization_barrier((shared[0], base_value))
    extra, flag = pl.pallas_call(
        functools.partial(adapt_over_body, planes, rank),
        in_specs=[SMEM, ANY] + [VMEM] * (1 + PLANE),
        out_specs=[VMEM, VMEM],
        out_shape=[
            jax.ShapeDtypeStruct((count, EXTRA, width), jnp.float32),
            jax.ShapeDtypeStruct((1, NOTE), jnp.int32),
        ],
        scratch_shapes=[pltpu.VMEM(down.shape, jnp.bfloat16), pltpu.SemaphoreType.DMA((PARTS,))],
        compiler_params=pltpu.CompilerParams(vmem_limit_bytes=40 * 2**20),
        cost_estimate=pl.CostEstimate(
            flops=10**12,
            bytes_accessed=6 * 2**20,
            transcendentals=0,
        ),
    )(first, down, up, *shared)

    got, extra = lax.optimization_barrier((got, extra))
    delta = adapt(rank, me.reshape(1), down, up, got, extra)
    delta, flag = lax.optimization_barrier((delta, flag))
    back = lax.all_to_all(delta, "ad", split_axis=0, concat_axis=0, tiled=True)
    back = back.reshape(count * (room + EXTRA), width)

    groups = lax.axis_size("grp")
    own = flag[0, 2]
    seen = own
    for g in range(1, groups):
        other = lax.ppermute(own, "grp", [(s, (s + g) % groups) for s in range(groups)])
        seen = jnp.maximum(seen, other)

    def finish(base):
        return pl.pallas_call(
            final_body,
            in_specs=[VMEM] * 3,
            out_specs=VMEM,
            out_shape=jax.ShapeDtypeStruct((row_count, width), jnp.bfloat16),
        )(at_back, base, back)

    def more():
        slot, owner, place = route(tenant_ids, tenant_slot, local)
        extra = exchange(
            tokens,
            slot,
            owner,
            jnp.where(at[0] < 0, place - room, -1),
            CAP * local - room,
            adapt_down,
            adapt_up,
        )
        return finish(base_value + extra)

    return lax.cond(seen > 0, more, lambda: finish(base_value))


def solution(mesh):
    placed = (
        P(("grp", "ad"), None),
        P(),
        P(("grp", "ad"), None, None),
        P(("grp", "ad"), None, None),
        P(("grp", "ad"), None),
        P("grp"),
    )
    return jax.shard_map(
        on_device, mesh=mesh, in_specs=placed, out_specs=P(("grp", "ad"), None), check_vma=False
    )
```

```python
import functools

import jax
import jax.numpy as jnp
from jax import lax
from jax.experimental import pallas as pl
from jax.experimental.pallas import tpu as pltpu
from jax.sharding import PartitionSpec as P

TENANTS = 256
CAP = 2
PLANE = 4
SPARE = 12
EXTRA = 8
NOTE = 128
STEP = 1024
WIDE = 1664
PARTS = 8
VMEM = pl.BlockSpec(memory_space=pltpu.VMEM)
ANY = pl.BlockSpec(memory_space=pl.ANY)
SMEM = pl.BlockSpec(memory_space=pltpu.SMEM)


def exchange(tokens, slot, owner, place, room, down, up):
    count = lax.axis_size("ad")
    local, depth, rank = down.shape
    width = up.shape[2]
    at = jnp.where((place >= 0) & (place < room), owner * room + place, -1)
    hits = at[None, :] == jnp.arange(count * room, dtype=jnp.int32)[:, None]
    slots = jnp.sum(jnp.where(hits, slot[None, :] + 1, 0), axis=1) - 1
    pick = hits.astype(jnp.bfloat16)
    sent = jnp.dot(pick, tokens, preferred_element_type=jnp.float32).astype(jnp.bfloat16)
    got = lax.all_to_all(
        sent.reshape(count, room, depth), "ad", split_axis=0, concat_axis=0, tiled=True
    ).reshape(count * room, depth)
    got_slots = lax.all_to_all(
        slots.reshape(count, room), "ad", split_axis=0, concat_axis=0, tiled=True
    ).reshape(count * room)
    low_rank = jnp.einsum("td,ldr->tlr", got, down, preferred_element_type=jnp.float32)
    own = (got_slots - lax.axis_index("ad") * local)[:, None] == jnp.arange(local)[None, :]
    low_rank = jnp.where(own[:, :, None], low_rank, 0.0).astype(jnp.bfloat16)
    delta = jnp.dot(
        low_rank.reshape(count * room, local * rank),
        up.reshape(local * rank, width),
        preferred_element_type=jnp.float32,
    ).astype(jnp.bfloat16)
    back = lax.all_to_all(
        delta.reshape(count, room, width), "ad", split_axis=0, concat_axis=0, tiled=True
    )
    return jnp.dot(
        pick.T, back.reshape(count * room, width), preferred_element_type=jnp.float32
    )


def row_copies(source, target, sems, parts):
    rows = target.shape[0] // parts
    return [
        pltpu.make_async_copy(
            source.at[i * rows : (i + 1) * rows], target.at[i * rows : (i + 1) * rows], sems.at[i]
        )
        for i in range(parts)
    ]


def one_hot(hit):
    return hit.astype(jnp.float32).astype(jnp.bfloat16)


def earlier(hit, until):
    counts = jnp.dot(one_hot(hit), until, preferred_element_type=jnp.float32)
    return jnp.sum(jnp.where(hit, counts, 0.0), axis=0, keepdims=True).astype(jnp.int32)


def route_body(room, local, me_ref, tenant_ref, slot_ref, tokens_hbm, *refs):
    *outs, at_ref, back_ref, note_ref, tokens_ref, sems = refs
    half = tokens_ref.shape[1] // 2
    copies = row_copies(tokens_hbm, tokens_ref, sems, PARTS)
    for copy in copies:
        copy.start()
    tenant = tenant_ref[...]
    rows = tenant.shape[1]
    planes = len(outs)
    main_rows = planes * PLANE * room

    def iota(size, axis=0):
        return lax.broadcasted_iota(jnp.int32, (size, rows), axis)

    table = jnp.broadcast_to(slot_ref[...].astype(jnp.float32), (16, TENANTS)).astype(jnp.bfloat16)
    slot = jnp.dot(table, one_hot(iota(TENANTS) == tenant), preferred_element_type=jnp.float32)[:1]
    owner = slot.astype(jnp.int32) // local
    until = one_hot(iota(rows) < iota(rows, 1))
    place = earlier(iota(planes * PLANE) == owner, until)
    plane = (owner ^ me_ref[0]) // PLANE
    over = place >= room
    over_place = earlier((iota(16) == plane) & over, until)
    left = over & ((over_place >= SPARE) | (place >= room + EXTRA))
    at = jnp.where(over, main_rows + plane * SPARE + over_place, owner * room + place)
    at = jnp.where(left, -1, at)
    at_ref[...] = at
    back_ref[...] = jnp.where(left, -1, owner * (room + EXTRA) + place)
    note = jnp.where(iota(NOTE) == 0, slot + 1.0, 0.0)
    note = jnp.where(iota(NOTE) == 1, place.astype(jnp.float32), note).astype(jnp.bfloat16)
    note_ref[...] = note
    most = jnp.max(left.astype(jnp.float32), axis=1, keepdims=True)

    row = iota(2 * SPARE)
    upper = row >= SPARE
    ids = jnp.where(upper, row - SPARE, row)
    ids = jnp.concatenate([ids + main_rows + b * SPARE for b in range(planes)], axis=0)
    upper = jnp.concatenate([upper] * planes, axis=0)
    hit = ids == at
    first, second = one_hot(hit & ~upper), one_hot(hit & upper)

    def put(value, columns):
        for b in range(planes):
            outs[b][:, columns] = value[2 * SPARE * b : 2 * SPARE * (b + 1)].astype(jnp.bfloat16)

    notes = notes_of(one_hot(hit), note)
    flag = lax.broadcasted_iota(jnp.int32, notes.shape, 1) == 2
    put(jnp.where(flag, most, notes), slice(half, half + NOTE))
    for copy in copies:
        copy.wait()
    for c in range(0, half, STEP):
        put(
            jnp.dot(first, tokens_ref[:, c : c + STEP], preferred_element_type=jnp.float32)
            + jnp.dot(
                second,
                tokens_ref[:, half + c : half + c + STEP],
                preferred_element_type=jnp.float32,
            ),
            slice(c, c + STEP),
        )


def notes_of(pick, note):
    return lax.dot_general(
        pick, note, (((1,), (1,)), ((), ())), preferred_element_type=jnp.float32
    )


def pack_body(at_ref, note_ref, tokens_ref, out_hbm, out_ref, sems):
    depth = tokens_ref.shape[1]
    stores = row_copies(out_ref, out_hbm, sems, PARTS)
    half = out_ref.shape[0] // 2
    row = lax.broadcasted_iota(jnp.int32, (half, at_ref.shape[1]), 0)
    for h in range(2):
        own = slice(h * half, (h + 1) * half)
        pick = one_hot(row + h * half == at_ref[...])
        for c in range(0, depth, STEP):
            out_ref[own, c : c + STEP] = jnp.dot(
                pick, tokens_ref[:, c : c + STEP], preferred_element_type=jnp.float32
            ).astype(jnp.bfloat16)
        out_ref[own, depth:] = notes_of(pick, note_ref[...]).astype(jnp.bfloat16)
        for store in stores[h * PARTS // 2 : (h + 1) * PARTS // 2]:
            store.start()
    for store in stores:
        store.wait()


def pack(main_rows, at, note, tokens):
    rows, depth = tokens.shape
    out = jax.ShapeDtypeStruct((main_rows, depth + NOTE), jnp.bfloat16)
    return pl.pallas_call(
        pack_body,
        in_specs=[VMEM, VMEM, VMEM],
        out_specs=pl.BlockSpec(memory_space=pltpu.HBM),
        out_shape=out,
        scratch_shapes=[
            pltpu.VMEM(out.shape, jnp.bfloat16),
            pltpu.SemaphoreType.DMA((PARTS,)),
        ],
        compiler_params=pltpu.CompilerParams(vmem_limit_bytes=48 * 2**20),
        cost_estimate=pl.CostEstimate(
            flops=2 * main_rows * rows * depth, bytes_accessed=8 * 2**20, transcendentals=0
        ),
    )(at, note, tokens)


def low_delta(low, note, first, rank, up):
    column = lax.broadcasted_iota(jnp.int32, low.shape, 1) // rank + (first + 1)
    low = jnp.where(note.astype(jnp.float32) == column.astype(jnp.float32), low, 0.0)
    return jnp.dot(low.astype(jnp.bfloat16), up, preferred_element_type=jnp.float32)


def adapt_body(rank, me_ref, down_hbm, up_ref, rows_hbm, extra_ref, out, *scratch):
    down_ref, rows_ref, down_sems, sems = scratch
    depth = down_ref.shape[1]
    spans = [slice(c, min(c + WIDE, depth + NOTE)) for c in range(0, depth + NOTE, WIDE)]
    copies = []
    for i, span in enumerate(spans):
        kept = slice(span.start, min(span.stop, depth))
        copies.append(
            (
                pltpu.make_async_copy(rows_hbm.at[:, span], rows_ref.at[:, span], sems.at[i]),
                pltpu.make_async_copy(down_hbm.at[:, kept], down_ref.at[:, kept], down_sems.at[i]),
            )
        )
    for pair in copies:
        pair[0].start()
        pair[1].start()
    low = jnp.zeros((rows_ref.shape[0], down_ref.shape[0]), jnp.float32)
    for pair, span in zip(copies, spans, strict=True):
        pair[0].wait()
        pair[1].wait()
        span = slice(span.start, min(span.stop, depth))
        low += lax.dot_general(
            rows_ref[:, span],
            down_ref[:, span],
            (((1,), (1,)), ((), ())),
            preferred_element_type=jnp.float32,
        )
    note = rows_ref[:, depth:].astype(jnp.float32)
    sources = out.shape[0]
    first = me_ref[0] * (down_ref.shape[0] // rank)
    delta = low_delta(low, note[:, :1], first, rank, up_ref[...])
    room = delta.shape[0] // sources
    for s in range(sources):
        k = me_ref[0] ^ s
        extra = extra_ref[(k % PLANE) * (sources // PLANE) + k // PLANE]
        rows = jnp.concatenate([delta[s * room : (s + 1) * room], extra], axis=0)
        out[s] = rows.astype(jnp.bfloat16)


def adapt(rank, me, down, up, got, extra):
    rows, width = got.shape[0], up.shape[1]
    count = extra.shape[0]
    return pl.pallas_call(
        functools.partial(adapt_body, rank),
        in_specs=[SMEM, ANY, VMEM, ANY, VMEM],
        out_specs=VMEM,
        out_shape=jax.ShapeDtypeStruct((count, rows // count + EXTRA, width), jnp.bfloat16),
        scratch_shapes=[
            pltpu.VMEM(down.shape, jnp.bfloat16),
            pltpu.VMEM(got.shape, jnp.bfloat16),
            pltpu.SemaphoreType.DMA((pl.cdiv(got.shape[1], WIDE),)),
            pltpu.SemaphoreType.DMA((pl.cdiv(got.shape[1], WIDE),)),
        ],
        compiler_params=pltpu.CompilerParams(vmem_limit_bytes=24 * 2**20),
        cost_estimate=pl.CostEstimate(
            flops=2 * rows * down.size, bytes_accessed=8 * 2**20, transcendentals=0
        ),
    )(me, down, up, got, extra)


def adapt_over_body(planes, rank, first_ref, down_hbm, up_ref, *refs):
    rows_refs = refs[:PLANE]
    out, flag_out, down_ref, sems = refs[PLANE:]
    half = down_ref.shape[1] // 2
    copies = row_copies(down_hbm, down_ref, sems, PARTS)
    for copy in copies:
        copy.start()
    each = rows_refs[0].shape[0]
    shape = (PLANE * each, down_ref.shape[0])
    dims = (((1,), (1,)), ((), ()))
    low0, low1 = jnp.zeros(shape, jnp.float32), jnp.zeros(shape, jnp.float32)
    for copy in copies:
        copy.wait()
    for c in range(0, half, STEP):
        rows = jnp.concatenate([r[:, c : c + STEP] for r in rows_refs], axis=0)
        low0 += lax.dot_general(
            rows, down_ref[:, c : c + STEP], dims, preferred_element_type=jnp.float32
        )
        low1 += lax.dot_general(
            rows, down_ref[:, half + c : half + c + STEP], dims, preferred_element_type=jnp.float32
        )
    zeros = jnp.zeros((16 - SPARE, shape[1]), jnp.float32)
    no_note = jnp.zeros((16 - SPARE, NOTE), jnp.float32)
    lows, notes = [], []
    for a in range(PLANE):
        note = rows_refs[a][:, half : half + NOTE].astype(jnp.float32)
        for b in range(planes):
            s = 2 * SPARE * b
            m = a * each + s
            lows += [low0[m : m + SPARE] + low1[m + SPARE : m + 2 * SPARE], zeros]
            notes += [note[s : s + SPARE], no_note]
    low = jnp.concatenate(lows, axis=0)
    note = jnp.concatenate(notes, axis=0)
    delta = low_delta(low, note[:, :1], first_ref[0], rank, up_ref[...]).astype(jnp.bfloat16)
    shape = (delta.shape[0], PLANE * planes * EXTRA)
    row, column = (lax.broadcasted_iota(jnp.int32, shape, axis) for axis in (0, 1))
    own = (note[:, :1].astype(jnp.int32) - 1) // (down_ref.shape[0] // rank) == first_ref[
        0
    ] // (down_ref.shape[0] // rank)
    own = own & (note[:, :1] > 0)
    put = (note[:, 1:2].astype(jnp.int32) == 16 + column % EXTRA) & (row // 16 == column // EXTRA)
    extra = lax.dot_general(
        one_hot(put & own), delta, (((0,), (0,)), ((), ())), preferred_element_type=jnp.float32
    )
    for g in range(PLANE * planes):
        out[g] = extra[g * EXTRA : (g + 1) * EXTRA]
    flags = [jnp.max(r[:, half : half + NOTE].astype(jnp.float32), axis=0) for r in rows_refs]
    most = functools.reduce(jnp.maximum, flags).reshape(1, NOTE)
    flag_out[...] = most.astype(jnp.int32)


def final_body(at_ref, base_ref, back_ref, out):
    row = lax.broadcasted_iota(jnp.int32, (back_ref.shape[0], at_ref.shape[1]), 0)
    delta = lax.dot_general(
        one_hot(row == at_ref[...]),
        back_ref[...],
        (((0,), (0,)), ((), ())),
        preferred_element_type=jnp.float32,
    )
    out[...] = (base_ref[...] + delta).astype(jnp.bfloat16)


def swap(x, k):
    count = lax.axis_size("ad")
    return lax.ppermute(x, "ad", [(s, s ^ k) for s in range(count)])


def route(tenant_ids, tenant_slot, local):
    tenant = tenant_ids[:, 0]
    tenant_match = tenant[:, None] == jnp.arange(TENANTS, dtype=jnp.int32)[None, :]
    slot = jnp.sum(jnp.where(tenant_match, tenant_slot[None, :], 0), axis=1)
    owner = slot // local
    order = jnp.arange(tenant.shape[0], dtype=jnp.int32)
    before = order[None, :] < order[:, None]
    place = jnp.sum(((owner[:, None] == owner[None, :]) & before).astype(jnp.int32), axis=1)
    return slot, owner, place


def on_device(tokens, value_weight, adapt_down, adapt_up, tenant_ids, tenant_slot):
    row_count, depth = tokens.shape
    count = lax.axis_size("ad")
    me = lax.axis_index("ad")
    local, _, rank = adapt_down.shape
    width = adapt_up.shape[2]
    base_value = jnp.dot(tokens, value_weight, preferred_element_type=jnp.float32)
    room = row_count // count
    planes = count // PLANE
    if count != 16 or room != 16 or depth % (2 * STEP):
        slot, owner, place = route(tenant_ids, tenant_slot, local)
        delta = exchange(tokens, slot, owner, place, CAP * local, adapt_down, adapt_up)
        return (base_value + delta).astype(jnp.bfloat16)

    main_rows = count * room
    *spare, at, at_back, note, near = pl.pallas_call(
        functools.partial(route_body, room, local),
        in_specs=[SMEM, VMEM, VMEM, ANY],
        out_specs=[VMEM] * (planes + 4),
        out_shape=[jax.ShapeDtypeStruct((2 * SPARE, depth // 2 + NOTE), jnp.bfloat16)] * planes
        + [
            jax.ShapeDtypeStruct((1, row_count), jnp.int32),
            jax.ShapeDtypeStruct((1, row_count), jnp.int32),
            jax.ShapeDtypeStruct((NOTE, row_count), jnp.bfloat16),
            jax.ShapeDtypeStruct(tokens.shape, jnp.bfloat16),
        ],
        scratch_shapes=[
            pltpu.SemaphoreType.DMA((PARTS,)),
        ],
        compiler_params=pltpu.CompilerParams(vmem_limit_bytes=24 * 2**20),
        cost_estimate=pl.CostEstimate(
            flops=4 * 96 * row_count * depth, bytes_accessed=6 * 2**20, transcendentals=0
        ),
    )(me.reshape(1), tenant_ids.reshape(1, row_count), tenant_slot.reshape(1, TENANTS), tokens)

    along = [swap(spare[b], b * PLANE) for b in range(planes - 1, 0, -1)]
    along = list(lax.optimization_barrier(tuple(along)))
    blocks = pack(main_rows, at, note, near)

    along = jnp.concatenate([spare[0]] + along[::-1], axis=0)
    shared = [along] + [swap(along, a) for a in range(1, PLANE)]

    got = lax.all_to_all(
        blocks.reshape(count, room, depth + NOTE), "ad", split_axis=0, concat_axis=0, tiled=True
    ).reshape(main_rows, depth + NOTE)

    first = (me * local).reshape(1)
    down = adapt_down.transpose(0, 2, 1).reshape(local * rank, depth)
    up = adapt_up.reshape(local * rank, width)

    shared[0], base_value = lax.optimization_barrier((shared[0], base_value))
    extra, flag = pl.pallas_call(
        functools.partial(adapt_over_body, planes, rank),
        in_specs=[SMEM, ANY] + [VMEM] * (1 + PLANE),
        out_specs=[VMEM, VMEM],
        out_shape=[
            jax.ShapeDtypeStruct((count, EXTRA, width), jnp.float32),
            jax.ShapeDtypeStruct((1, NOTE), jnp.int32),
        ],
        scratch_shapes=[pltpu.VMEM(down.shape, jnp.bfloat16), pltpu.SemaphoreType.DMA((PARTS,))],
        compiler_params=pltpu.CompilerParams(vmem_limit_bytes=40 * 2**20),
        cost_estimate=pl.CostEstimate(
            flops=10**12,
            bytes_accessed=6 * 2**20,
            transcendentals=0,
        ),
    )(first, down, up, *shared)

    got, extra = lax.optimization_barrier((got, extra))
    delta = adapt(rank, me.reshape(1), down, up, got, extra)
    delta, flag = lax.optimization_barrier((delta, flag))
    back = lax.all_to_all(delta, "ad", split_axis=0, concat_axis=0, tiled=True)
    back = back.reshape(count * (room + EXTRA), width)

    groups = lax.axis_size("grp")
    own = flag[0, 2]
    seen = own
    for g in range(1, groups):
        other = lax.ppermute(own, "grp", [(s, (s + g) % groups) for s in range(groups)])
        seen = jnp.maximum(seen, other)

    def finish(base):
        return pl.pallas_call(
            final_body,
            in_specs=[VMEM] * 3,
            out_specs=VMEM,
            out_shape=jax.ShapeDtypeStruct((row_count, width), jnp.bfloat16),
        )(at_back, base, back)

    def more():
        slot, owner, place = route(tenant_ids, tenant_slot, local)
        extra = exchange(
            tokens,
            slot,
            owner,
            jnp.where(at[0] < 0, place - room, -1),
            CAP * local - room,
            adapt_down,
            adapt_up,
        )
        return finish(base_value + extra)

    return lax.cond(seen > 0, more, lambda: finish(base_value))


def solution(mesh):
    placed = (
        P(("grp", "ad"), None),
        P(),
        P(("grp", "ad"), None, None),
        P(("grp", "ad"), None, None),
        P(("grp", "ad"), None),
        P("grp"),
    )
    return jax.shard_map(
        on_device, mesh=mesh, in_specs=placed, out_specs=P(("grp", "ad"), None), check_vma=False
    )
```

```python
import functools

import jax
import jax.numpy as jnp
from jax import lax
from jax.experimental import pallas as pl
from jax.experimental.pallas import tpu as pltpu
from jax.sharding import PartitionSpec as P

TENANTS = 256
CAP = 2
PLANE = 4
SPARE = 12
EXTRA = 8
NOTE = 128
STEP = 1024
PARTS = 8
VMEM = pl.BlockSpec(memory_space=pltpu.VMEM)
ANY = pl.BlockSpec(memory_space=pl.ANY)
SMEM = pl.BlockSpec(memory_space=pltpu.SMEM)


def exchange(tokens, slot, owner, place, room, down, up):
    count = lax.axis_size("ad")
    local, depth, rank = down.shape
    width = up.shape[2]
    at = jnp.where((place >= 0) & (place < room), owner * room + place, -1)
    hits = at[None, :] == jnp.arange(count * room, dtype=jnp.int32)[:, None]
    slots = jnp.sum(jnp.where(hits, slot[None, :] + 1, 0), axis=1) - 1
    pick = hits.astype(jnp.bfloat16)
    sent = jnp.dot(pick, tokens, preferred_element_type=jnp.float32).astype(jnp.bfloat16)
    got = lax.all_to_all(
        sent.reshape(count, room, depth), "ad", split_axis=0, concat_axis=0, tiled=True
    ).reshape(count * room, depth)
    got_slots = lax.all_to_all(
        slots.reshape(count, room), "ad", split_axis=0, concat_axis=0, tiled=True
    ).reshape(count * room)
    low_rank = jnp.einsum("td,ldr->tlr", got, down, preferred_element_type=jnp.float32)
    own = (got_slots - lax.axis_index("ad") * local)[:, None] == jnp.arange(local)[None, :]
    low_rank = jnp.where(own[:, :, None], low_rank, 0.0).astype(jnp.bfloat16)
    delta = jnp.dot(
        low_rank.reshape(count * room, local * rank),
        up.reshape(local * rank, width),
        preferred_element_type=jnp.float32,
    ).astype(jnp.bfloat16)
    back = lax.all_to_all(
        delta.reshape(count, room, width), "ad", split_axis=0, concat_axis=0, tiled=True
    )
    return jnp.dot(
        pick.T, back.reshape(count * room, width), preferred_element_type=jnp.float32
    )


def row_copies(source, target, sems, parts):
    rows = target.shape[0] // parts
    return [
        pltpu.make_async_copy(
            source.at[i * rows : (i + 1) * rows], target.at[i * rows : (i + 1) * rows], sems.at[i]
        )
        for i in range(parts)
    ]


def one_hot(hit):
    return hit.astype(jnp.float32).astype(jnp.bfloat16)


def earlier(hit, until):
    counts = jnp.dot(one_hot(hit), until, preferred_element_type=jnp.float32)
    return jnp.sum(jnp.where(hit, counts, 0.0), axis=0, keepdims=True).astype(jnp.int32)


def route_body(room, local, me_ref, tenant_ref, slot_ref, tokens_hbm, *refs):
    *outs, at_ref, back_ref, note_ref, tokens_ref, sems = refs
    half = tokens_ref.shape[1] // 2
    copies = row_copies(tokens_hbm, tokens_ref, sems, PARTS)
    for copy in copies:
        copy.start()
    tenant = tenant_ref[...]
    rows = tenant.shape[1]
    planes = len(outs)
    main_rows = planes * PLANE * room

    def iota(size, axis=0):
        return lax.broadcasted_iota(jnp.int32, (size, rows), axis)

    table = jnp.broadcast_to(slot_ref[...].astype(jnp.float32), (16, TENANTS)).astype(jnp.bfloat16)
    slot = jnp.dot(table, one_hot(iota(TENANTS) == tenant), preferred_element_type=jnp.float32)[:1]
    owner = slot.astype(jnp.int32) // local
    until = one_hot(iota(rows) < iota(rows, 1))
    place = earlier(iota(planes * PLANE) == owner, until)
    plane = (owner ^ me_ref[0]) // PLANE
    over = place >= room
    over_place = earlier((iota(16) == plane) & over, until)
    left = over & ((over_place >= SPARE) | (place >= room + EXTRA))
    at = jnp.where(over, main_rows + plane * SPARE + over_place, owner * room + place)
    at = jnp.where(left, -1, at)
    at_ref[...] = at
    back_ref[...] = jnp.where(left, -1, owner * (room + EXTRA) + place)
    note = jnp.where(iota(NOTE) == 0, slot + 1.0, 0.0)
    note = jnp.where(iota(NOTE) == 1, place.astype(jnp.float32), note).astype(jnp.bfloat16)
    note_ref[...] = note
    most = jnp.max(left.astype(jnp.float32), axis=1, keepdims=True)

    row = iota(2 * SPARE)
    upper = row >= SPARE
    ids = jnp.where(upper, row - SPARE, row)
    ids = jnp.concatenate([ids + main_rows + b * SPARE for b in range(planes)], axis=0)
    upper = jnp.concatenate([upper] * planes, axis=0)
    hit = ids == at
    first, second = one_hot(hit & ~upper), one_hot(hit & upper)

    def put(value, columns):
        for b in range(planes):
            outs[b][:, columns] = value[2 * SPARE * b : 2 * SPARE * (b + 1)].astype(jnp.bfloat16)

    notes = notes_of(one_hot(hit), note)
    flag = lax.broadcasted_iota(jnp.int32, notes.shape, 1) == 2
    put(jnp.where(flag, most, notes), slice(half, half + NOTE))
    for copy in copies:
        copy.wait()
    for c in range(0, half, STEP):
        put(
            jnp.dot(first, tokens_ref[:, c : c + STEP], preferred_element_type=jnp.float32)
            + jnp.dot(
                second,
                tokens_ref[:, half + c : half + c + STEP],
                preferred_element_type=jnp.float32,
            ),
            slice(c, c + STEP),
        )


def notes_of(pick, note):
    return lax.dot_general(
        pick, note, (((1,), (1,)), ((), ())), preferred_element_type=jnp.float32
    )


def pack_body(at_ref, note_ref, tokens_ref, out_hbm, out_ref, sems):
    depth = tokens_ref.shape[1]
    stores = row_copies(out_ref, out_hbm, sems, PARTS)
    half = out_ref.shape[0] // 2
    row = lax.broadcasted_iota(jnp.int32, (half, at_ref.shape[1]), 0)
    for h in range(2):
        own = slice(h * half, (h + 1) * half)
        pick = one_hot(row + h * half == at_ref[...])
        for c in range(0, depth, STEP):
            out_ref[own, c : c + STEP] = jnp.dot(
                pick, tokens_ref[:, c : c + STEP], preferred_element_type=jnp.float32
            ).astype(jnp.bfloat16)
        out_ref[own, depth:] = notes_of(pick, note_ref[...]).astype(jnp.bfloat16)
        for store in stores[h * PARTS // 2 : (h + 1) * PARTS // 2]:
            store.start()
    for store in stores:
        store.wait()


def pack(main_rows, at, note, tokens):
    rows, depth = tokens.shape
    out = jax.ShapeDtypeStruct((main_rows, depth + NOTE), jnp.bfloat16)
    return pl.pallas_call(
        pack_body,
        in_specs=[VMEM, VMEM, VMEM],
        out_specs=pl.BlockSpec(memory_space=pltpu.HBM),
        out_shape=out,
        scratch_shapes=[
            pltpu.VMEM(out.shape, jnp.bfloat16),
            pltpu.SemaphoreType.DMA((PARTS,)),
        ],
        compiler_params=pltpu.CompilerParams(vmem_limit_bytes=52 * 2**20),
        cost_estimate=pl.CostEstimate(
            flops=2 * main_rows * rows * depth, bytes_accessed=8 * 2**20, transcendentals=0
        ),
    )(at, note, tokens)


def low_delta(low, note, first, rank, up):
    column = lax.broadcasted_iota(jnp.int32, low.shape, 1) // rank + (first + 1)
    low = jnp.where(note.astype(jnp.float32) == column.astype(jnp.float32), low, 0.0)
    return jnp.dot(low.astype(jnp.bfloat16), up, preferred_element_type=jnp.float32)


def adapt_body(rank, me_ref, down_hbm, up_ref, rows_hbm, extra_ref, out, *scratch):
    down_ref, rows_ref, down_sems, sems = scratch
    depth = down_ref.shape[1]
    copies = row_copies(down_hbm, down_ref, down_sems, PARTS)
    copies += row_copies(rows_hbm, rows_ref, sems, PARTS)
    for copy in copies:
        copy.start()
    for copy in copies:
        copy.wait()
    low = jnp.zeros((rows_ref.shape[0], down_ref.shape[0]), jnp.float32)
    for c in range(0, depth, STEP):
        low += lax.dot_general(
            rows_ref[:, c : c + STEP],
            down_ref[:, c : c + STEP],
            (((1,), (1,)), ((), ())),
            preferred_element_type=jnp.float32,
        )
    note = rows_ref[:, depth:].astype(jnp.float32)
    sources = out.shape[0]
    first = me_ref[0] * (down_ref.shape[0] // rank)
    delta = low_delta(low, note[:, :1], first, rank, up_ref[...])
    room = delta.shape[0] // sources
    for s in range(sources):
        k = me_ref[0] ^ s
        extra = extra_ref[(k % PLANE) * (sources // PLANE) + k // PLANE]
        rows = jnp.concatenate([delta[s * room : (s + 1) * room], extra], axis=0)
        out[s] = rows.astype(jnp.bfloat16)


def adapt(rank, me, down, up, got, extra):
    rows, width = got.shape[0], up.shape[1]
    count = extra.shape[0]
    return pl.pallas_call(
        functools.partial(adapt_body, rank),
        in_specs=[SMEM, ANY, VMEM, ANY, VMEM],
        out_specs=VMEM,
        out_shape=jax.ShapeDtypeStruct((count, rows // count + EXTRA, width), jnp.bfloat16),
        scratch_shapes=[
            pltpu.VMEM(down.shape, jnp.bfloat16),
            pltpu.VMEM(got.shape, jnp.bfloat16),
            pltpu.SemaphoreType.DMA((PARTS,)),
            pltpu.SemaphoreType.DMA((PARTS,)),
        ],
        compiler_params=pltpu.CompilerParams(vmem_limit_bytes=24 * 2**20),
        cost_estimate=pl.CostEstimate(
            flops=2 * rows * down.size, bytes_accessed=8 * 2**20, transcendentals=0
        ),
    )(me, down, up, got, extra)


def adapt_over_body(planes, rank, first_ref, down_hbm, up_ref, *refs):
    rows_refs = refs[:PLANE]
    out, flag_out, down_ref, sems = refs[PLANE:]
    half = down_ref.shape[1] // 2
    copies = row_copies(down_hbm, down_ref, sems, PARTS)
    for copy in copies:
        copy.start()
    each = rows_refs[0].shape[0]
    shape = (PLANE * each, down_ref.shape[0])
    dims = (((1,), (1,)), ((), ()))
    low0, low1 = jnp.zeros(shape, jnp.float32), jnp.zeros(shape, jnp.float32)
    for copy in copies:
        copy.wait()
    for c in range(0, half, STEP):
        rows = jnp.concatenate([r[:, c : c + STEP] for r in rows_refs], axis=0)
        low0 += lax.dot_general(
            rows, down_ref[:, c : c + STEP], dims, preferred_element_type=jnp.float32
        )
        low1 += lax.dot_general(
            rows, down_ref[:, half + c : half + c + STEP], dims, preferred_element_type=jnp.float32
        )
    zeros = jnp.zeros((16 - SPARE, shape[1]), jnp.float32)
    no_note = jnp.zeros((16 - SPARE, NOTE), jnp.float32)
    lows, notes = [], []
    for a in range(PLANE):
        note = rows_refs[a][:, half : half + NOTE].astype(jnp.float32)
        for b in range(planes):
            s = 2 * SPARE * b
            m = a * each + s
            lows += [low0[m : m + SPARE] + low1[m + SPARE : m + 2 * SPARE], zeros]
            notes += [note[s : s + SPARE], no_note]
    low = jnp.concatenate(lows, axis=0)
    note = jnp.concatenate(notes, axis=0)
    delta = low_delta(low, note[:, :1], first_ref[0], rank, up_ref[...]).astype(jnp.bfloat16)
    shape = (delta.shape[0], PLANE * planes * EXTRA)
    row, column = (lax.broadcasted_iota(jnp.int32, shape, axis) for axis in (0, 1))
    own = (note[:, :1].astype(jnp.int32) - 1) // (down_ref.shape[0] // rank) == first_ref[
        0
    ] // (down_ref.shape[0] // rank)
    own = own & (note[:, :1] > 0)
    put = (note[:, 1:2].astype(jnp.int32) == 16 + column % EXTRA) & (row // 16 == column // EXTRA)
    extra = lax.dot_general(
        one_hot(put & own), delta, (((0,), (0,)), ((), ())), preferred_element_type=jnp.float32
    )
    for g in range(PLANE * planes):
        out[g] = extra[g * EXTRA : (g + 1) * EXTRA]
    flags = [jnp.max(r[:, half : half + NOTE].astype(jnp.float32), axis=0) for r in rows_refs]
    most = functools.reduce(jnp.maximum, flags).reshape(1, NOTE)
    flag_out[...] = most.astype(jnp.int32)


def final_body(at_ref, base_ref, back_ref, out):
    row = lax.broadcasted_iota(jnp.int32, (back_ref.shape[0], at_ref.shape[1]), 0)
    delta = lax.dot_general(
        one_hot(row == at_ref[...]),
        back_ref[...],
        (((0,), (0,)), ((), ())),
        preferred_element_type=jnp.float32,
    )
    out[...] = (base_ref[...] + delta).astype(jnp.bfloat16)


def swap(x, k):
    count = lax.axis_size("ad")
    return lax.ppermute(x, "ad", [(s, s ^ k) for s in range(count)])


def route(tenant_ids, tenant_slot, local):
    tenant = tenant_ids[:, 0]
    tenant_match = tenant[:, None] == jnp.arange(TENANTS, dtype=jnp.int32)[None, :]
    slot = jnp.sum(jnp.where(tenant_match, tenant_slot[None, :], 0), axis=1)
    owner = slot // local
    order = jnp.arange(tenant.shape[0], dtype=jnp.int32)
    before = order[None, :] < order[:, None]
    place = jnp.sum(((owner[:, None] == owner[None, :]) & before).astype(jnp.int32), axis=1)
    return slot, owner, place


def on_device(tokens, value_weight, adapt_down, adapt_up, tenant_ids, tenant_slot):
    row_count, depth = tokens.shape
    count = lax.axis_size("ad")
    me = lax.axis_index("ad")
    local, _, rank = adapt_down.shape
    width = adapt_up.shape[2]
    base_value = jnp.dot(tokens, value_weight, preferred_element_type=jnp.float32)
    room = row_count // count
    planes = count // PLANE
    if count != 16 or room != 16 or depth % (2 * STEP):
        slot, owner, place = route(tenant_ids, tenant_slot, local)
        delta = exchange(tokens, slot, owner, place, CAP * local, adapt_down, adapt_up)
        return (base_value + delta).astype(jnp.bfloat16)

    main_rows = count * room
    *spare, at, at_back, note = pl.pallas_call(
        functools.partial(route_body, room, local),
        in_specs=[SMEM, VMEM, VMEM, ANY],
        out_specs=[VMEM] * (planes + 3),
        out_shape=[jax.ShapeDtypeStruct((2 * SPARE, depth // 2 + NOTE), jnp.bfloat16)] * planes
        + [
            jax.ShapeDtypeStruct((1, row_count), jnp.int32),
            jax.ShapeDtypeStruct((1, row_count), jnp.int32),
            jax.ShapeDtypeStruct((NOTE, row_count), jnp.bfloat16),
        ],
        scratch_shapes=[
            pltpu.VMEM(tokens.shape, jnp.bfloat16),
            pltpu.SemaphoreType.DMA((PARTS,)),
        ],
        compiler_params=pltpu.CompilerParams(vmem_limit_bytes=24 * 2**20),
        cost_estimate=pl.CostEstimate(
            flops=4 * 96 * row_count * depth, bytes_accessed=6 * 2**20, transcendentals=0
        ),
    )(me.reshape(1), tenant_ids.reshape(1, row_count), tenant_slot.reshape(1, TENANTS), tokens)

    along = [swap(spare[b], b * PLANE) for b in range(planes - 1, 0, -1)]
    along = list(lax.optimization_barrier(tuple(along)))
    blocks = pack(main_rows, at, note, tokens)

    along = jnp.concatenate([spare[0]] + along[::-1], axis=0)
    shared = [along] + [swap(along, a) for a in range(1, PLANE)]

    got = lax.all_to_all(
        blocks.reshape(count, room, depth + NOTE), "ad", split_axis=0, concat_axis=0, tiled=True
    ).reshape(main_rows, depth + NOTE)

    first = (me * local).reshape(1)
    down = adapt_down.transpose(0, 2, 1).reshape(local * rank, depth)
    up = adapt_up.reshape(local * rank, width)

    shared[0], base_value = lax.optimization_barrier((shared[0], base_value))
    extra, flag = pl.pallas_call(
        functools.partial(adapt_over_body, planes, rank),
        in_specs=[SMEM, ANY] + [VMEM] * (1 + PLANE),
        out_specs=[VMEM, VMEM],
        out_shape=[
            jax.ShapeDtypeStruct((count, EXTRA, width), jnp.float32),
            jax.ShapeDtypeStruct((1, NOTE), jnp.int32),
        ],
        scratch_shapes=[pltpu.VMEM(down.shape, jnp.bfloat16), pltpu.SemaphoreType.DMA((PARTS,))],
        compiler_params=pltpu.CompilerParams(vmem_limit_bytes=40 * 2**20),
        cost_estimate=pl.CostEstimate(
            flops=10**12,
            bytes_accessed=6 * 2**20,
            transcendentals=0,
        ),
    )(first, down, up, *shared)

    got, extra = lax.optimization_barrier((got, extra))
    delta = adapt(rank, me.reshape(1), down, up, got, extra)
    delta, flag = lax.optimization_barrier((delta, flag))
    back = lax.all_to_all(delta, "ad", split_axis=0, concat_axis=0, tiled=True)
    back = back.reshape(count * (room + EXTRA), width)

    groups = lax.axis_size("grp")
    own = flag[0, 2]
    seen = own
    for g in range(1, groups):
        other = lax.ppermute(own, "grp", [(s, (s + g) % groups) for s in range(groups)])
        seen = jnp.maximum(seen, other)

    def finish(base):
        return pl.pallas_call(
            final_body,
            in_specs=[VMEM] * 3,
            out_specs=VMEM,
            out_shape=jax.ShapeDtypeStruct((row_count, width), jnp.bfloat16),
        )(at_back, base, back)

    def more():
        slot, owner, place = route(tenant_ids, tenant_slot, local)
        extra = exchange(
            tokens,
            slot,
            owner,
            jnp.where(at[0] < 0, place - room, -1),
            CAP * local - room,
            adapt_down,
            adapt_up,
        )
        return finish(base_value + extra)

    return lax.cond(seen > 0, more, lambda: finish(base_value))


def solution(mesh):
    placed = (
        P(("grp", "ad"), None),
        P(),
        P(("grp", "ad"), None, None),
        P(("grp", "ad"), None, None),
        P(("grp", "ad"), None),
        P("grp"),
    )
    return jax.shard_map(
        on_device, mesh=mesh, in_specs=placed, out_specs=P(("grp", "ad"), None), check_vma=False
    )
```

```python
import functools

import jax
import jax.numpy as jnp
from jax import lax
from jax.experimental import pallas as pl
from jax.experimental.pallas import tpu as pltpu
from jax.sharding import PartitionSpec as P

TENANTS = 256
CAP = 2
PLANE = 4
SPARE = 12
EXTRA = 8
NOTE = 128
STEP = 1024
WIDE = 1664
PARTS = 8
VMEM = pl.BlockSpec(memory_space=pltpu.VMEM)
ANY = pl.BlockSpec(memory_space=pl.ANY)
SMEM = pl.BlockSpec(memory_space=pltpu.SMEM)


def exchange(tokens, slot, owner, place, room, down, up):
    count = lax.axis_size("ad")
    local, depth, rank = down.shape
    width = up.shape[2]
    at = jnp.where((place >= 0) & (place < room), owner * room + place, -1)
    hits = at[None, :] == jnp.arange(count * room, dtype=jnp.int32)[:, None]
    slots = jnp.sum(jnp.where(hits, slot[None, :] + 1, 0), axis=1) - 1
    pick = hits.astype(jnp.bfloat16)
    sent = jnp.dot(pick, tokens, preferred_element_type=jnp.float32).astype(jnp.bfloat16)
    got = lax.all_to_all(
        sent.reshape(count, room, depth), "ad", split_axis=0, concat_axis=0, tiled=True
    ).reshape(count * room, depth)
    got_slots = lax.all_to_all(
        slots.reshape(count, room), "ad", split_axis=0, concat_axis=0, tiled=True
    ).reshape(count * room)
    low_rank = jnp.einsum("td,ldr->tlr", got, down, preferred_element_type=jnp.float32)
    own = (got_slots - lax.axis_index("ad") * local)[:, None] == jnp.arange(local)[None, :]
    low_rank = jnp.where(own[:, :, None], low_rank, 0.0).astype(jnp.bfloat16)
    delta = jnp.dot(
        low_rank.reshape(count * room, local * rank),
        up.reshape(local * rank, width),
        preferred_element_type=jnp.float32,
    ).astype(jnp.bfloat16)
    back = lax.all_to_all(
        delta.reshape(count, room, width), "ad", split_axis=0, concat_axis=0, tiled=True
    )
    return jnp.dot(
        pick.T, back.reshape(count * room, width), preferred_element_type=jnp.float32
    )


def row_copies(source, target, sems, parts):
    rows = target.shape[0] // parts
    return [
        pltpu.make_async_copy(
            source.at[i * rows : (i + 1) * rows], target.at[i * rows : (i + 1) * rows], sems.at[i]
        )
        for i in range(parts)
    ]


def one_hot(hit):
    return hit.astype(jnp.float32).astype(jnp.bfloat16)


def earlier(hit, until):
    counts = jnp.dot(one_hot(hit), until, preferred_element_type=jnp.float32)
    return jnp.sum(jnp.where(hit, counts, 0.0), axis=0, keepdims=True).astype(jnp.int32)


def route_body(room, local, me_ref, tenant_ref, slot_ref, tokens_hbm, *refs):
    *outs, at_ref, back_ref, note_ref, tokens_ref, sems = refs
    half = tokens_ref.shape[1] // 2
    copies = row_copies(tokens_hbm, tokens_ref, sems, PARTS)
    for copy in copies:
        copy.start()
    tenant = tenant_ref[...]
    rows = tenant.shape[1]
    planes = len(outs)
    main_rows = planes * PLANE * room

    def iota(size, axis=0):
        return lax.broadcasted_iota(jnp.int32, (size, rows), axis)

    table = jnp.broadcast_to(slot_ref[...].astype(jnp.float32), (16, TENANTS)).astype(jnp.bfloat16)
    slot = jnp.dot(table, one_hot(iota(TENANTS) == tenant), preferred_element_type=jnp.float32)[:1]
    owner = slot.astype(jnp.int32) // local
    until = one_hot(iota(rows) < iota(rows, 1))
    place = earlier(iota(planes * PLANE) == owner, until)
    plane = (owner ^ me_ref[0]) // PLANE
    over = place >= room
    over_place = earlier((iota(16) == plane) & over, until)
    left = over & ((over_place >= SPARE) | (place >= room + EXTRA))
    at = jnp.where(over, main_rows + plane * SPARE + over_place, owner * room + place)
    at = jnp.where(left, -1, at)
    at_ref[...] = at
    back_ref[...] = jnp.where(left, -1, owner * (room + EXTRA) + place)
    note = jnp.where(iota(NOTE) == 0, slot + 1.0, 0.0)
    note = jnp.where(iota(NOTE) == 1, place.astype(jnp.float32), note).astype(jnp.bfloat16)
    note_ref[...] = note
    most = jnp.max(left.astype(jnp.float32), axis=1, keepdims=True)

    row = iota(2 * SPARE)
    upper = row >= SPARE
    ids = jnp.where(upper, row - SPARE, row)
    ids = jnp.concatenate([ids + main_rows + b * SPARE for b in range(planes)], axis=0)
    upper = jnp.concatenate([upper] * planes, axis=0)
    hit = ids == at
    first, second = one_hot(hit & ~upper), one_hot(hit & upper)

    def put(value, columns):
        for b in range(planes):
            outs[b][:, columns] = value[2 * SPARE * b : 2 * SPARE * (b + 1)].astype(jnp.bfloat16)

    notes = notes_of(one_hot(hit), note)
    flag = lax.broadcasted_iota(jnp.int32, notes.shape, 1) == 2
    put(jnp.where(flag, most, notes), slice(half, half + NOTE))
    for copy in copies:
        copy.wait()
    for c in range(0, half, STEP):
        put(
            jnp.dot(first, tokens_ref[:, c : c + STEP], preferred_element_type=jnp.float32)
            + jnp.dot(
                second,
                tokens_ref[:, half + c : half + c + STEP],
                preferred_element_type=jnp.float32,
            ),
            slice(c, c + STEP),
        )


def notes_of(pick, note):
    return lax.dot_general(
        pick, note, (((1,), (1,)), ((), ())), preferred_element_type=jnp.float32
    )


def pack_body(at_ref, note_ref, tokens_ref, out_hbm, out_ref, sems):
    depth = tokens_ref.shape[1]
    stores = row_copies(out_ref, out_hbm, sems, PARTS)
    half = out_ref.shape[0] // 2
    row = lax.broadcasted_iota(jnp.int32, (half, at_ref.shape[1]), 0)
    for h in range(2):
        own = slice(h * half, (h + 1) * half)
        pick = one_hot(row + h * half == at_ref[...])
        for c in range(0, depth, STEP):
            out_ref[own, c : c + STEP] = jnp.dot(
                pick, tokens_ref[:, c : c + STEP], preferred_element_type=jnp.float32
            ).astype(jnp.bfloat16)
        out_ref[own, depth:] = notes_of(pick, note_ref[...]).astype(jnp.bfloat16)
        for store in stores[h * PARTS // 2 : (h + 1) * PARTS // 2]:
            store.start()
    for store in stores:
        store.wait()


def pack(main_rows, at, note, tokens):
    rows, depth = tokens.shape
    out = jax.ShapeDtypeStruct((main_rows, depth + NOTE), jnp.bfloat16)
    return pl.pallas_call(
        pack_body,
        in_specs=[VMEM, VMEM, VMEM],
        out_specs=pl.BlockSpec(memory_space=pltpu.HBM),
        out_shape=out,
        scratch_shapes=[
            pltpu.VMEM(out.shape, jnp.bfloat16),
            pltpu.SemaphoreType.DMA((PARTS,)),
        ],
        compiler_params=pltpu.CompilerParams(vmem_limit_bytes=52 * 2**20),
        cost_estimate=pl.CostEstimate(
            flops=2 * main_rows * rows * depth, bytes_accessed=8 * 2**20, transcendentals=0
        ),
    )(at, note, tokens)


def low_delta(low, note, first, rank, up):
    column = lax.broadcasted_iota(jnp.int32, low.shape, 1) // rank + (first + 1)
    low = jnp.where(note.astype(jnp.float32) == column.astype(jnp.float32), low, 0.0)
    return jnp.dot(low.astype(jnp.bfloat16), up, preferred_element_type=jnp.float32)


def adapt_body(rank, me_ref, down_hbm, up_ref, rows_hbm, extra_ref, out, *scratch):
    down_ref, rows_ref, down_sems, sems = scratch
    depth = down_ref.shape[1]
    spans = [slice(c, min(c + WIDE, depth + NOTE)) for c in range(0, depth + NOTE, WIDE)]
    copies = []
    for i, span in enumerate(spans):
        kept = slice(span.start, min(span.stop, depth))
        copies.append(
            (
                pltpu.make_async_copy(rows_hbm.at[:, span], rows_ref.at[:, span], sems.at[i]),
                pltpu.make_async_copy(down_hbm.at[:, kept], down_ref.at[:, kept], down_sems.at[i]),
            )
        )
    for copy in copies[0] + copies[1]:
        copy.start()
    low = jnp.zeros((rows_ref.shape[0], down_ref.shape[0]), jnp.float32)
    for i, span in enumerate(spans):
        for copy in copies[i]:
            copy.wait()
        if i + 2 < len(spans):
            for copy in copies[i + 2]:
                copy.start()
        span = slice(span.start, min(span.stop, depth))
        low += lax.dot_general(
            rows_ref[:, span],
            down_ref[:, span],
            (((1,), (1,)), ((), ())),
            preferred_element_type=jnp.float32,
        )
    note = rows_ref[:, depth:].astype(jnp.float32)
    sources = out.shape[0]
    first = me_ref[0] * (down_ref.shape[0] // rank)
    delta = low_delta(low, note[:, :1], first, rank, up_ref[...])
    room = delta.shape[0] // sources
    for s in range(sources):
        k = me_ref[0] ^ s
        extra = extra_ref[(k % PLANE) * (sources // PLANE) + k // PLANE]
        rows = jnp.concatenate([delta[s * room : (s + 1) * room], extra], axis=0)
        out[s] = rows.astype(jnp.bfloat16)


def adapt(rank, me, down, up, got, extra):
    rows, width = got.shape[0], up.shape[1]
    count = extra.shape[0]
    return pl.pallas_call(
        functools.partial(adapt_body, rank),
        in_specs=[SMEM, ANY, VMEM, ANY, VMEM],
        out_specs=VMEM,
        out_shape=jax.ShapeDtypeStruct((count, rows // count + EXTRA, width), jnp.bfloat16),
        scratch_shapes=[
            pltpu.VMEM(down.shape, jnp.bfloat16),
            pltpu.VMEM(got.shape, jnp.bfloat16),
            pltpu.SemaphoreType.DMA((pl.cdiv(got.shape[1], WIDE),)),
            pltpu.SemaphoreType.DMA((pl.cdiv(got.shape[1], WIDE),)),
        ],
        compiler_params=pltpu.CompilerParams(vmem_limit_bytes=24 * 2**20),
        cost_estimate=pl.CostEstimate(
            flops=2 * rows * down.size, bytes_accessed=8 * 2**20, transcendentals=0
        ),
    )(me, down, up, got, extra)


def adapt_over_body(planes, rank, first_ref, down_hbm, up_ref, *refs):
    rows_refs = refs[:PLANE]
    out, flag_out, down_ref, sems = refs[PLANE:]
    half = down_ref.shape[1] // 2
    copies = row_copies(down_hbm, down_ref, sems, PARTS)
    for copy in copies:
        copy.start()
    each = rows_refs[0].shape[0]
    shape = (PLANE * each, down_ref.shape[0])
    dims = (((1,), (1,)), ((), ()))
    low0, low1 = jnp.zeros(shape, jnp.float32), jnp.zeros(shape, jnp.float32)
    for copy in copies:
        copy.wait()
    for c in range(0, half, STEP):
        rows = jnp.concatenate([r[:, c : c + STEP] for r in rows_refs], axis=0)
        low0 += lax.dot_general(
            rows, down_ref[:, c : c + STEP], dims, preferred_element_type=jnp.float32
        )
        low1 += lax.dot_general(
            rows, down_ref[:, half + c : half + c + STEP], dims, preferred_element_type=jnp.float32
        )
    zeros = jnp.zeros((16 - SPARE, shape[1]), jnp.float32)
    no_note = jnp.zeros((16 - SPARE, NOTE), jnp.float32)
    lows, notes = [], []
    for a in range(PLANE):
        note = rows_refs[a][:, half : half + NOTE].astype(jnp.float32)
        for b in range(planes):
            s = 2 * SPARE * b
            m = a * each + s
            lows += [low0[m : m + SPARE] + low1[m + SPARE : m + 2 * SPARE], zeros]
            notes += [note[s : s + SPARE], no_note]
    low = jnp.concatenate(lows, axis=0)
    note = jnp.concatenate(notes, axis=0)
    delta = low_delta(low, note[:, :1], first_ref[0], rank, up_ref[...]).astype(jnp.bfloat16)
    shape = (delta.shape[0], PLANE * planes * EXTRA)
    row, column = (lax.broadcasted_iota(jnp.int32, shape, axis) for axis in (0, 1))
    own = (note[:, :1].astype(jnp.int32) - 1) // (down_ref.shape[0] // rank) == first_ref[
        0
    ] // (down_ref.shape[0] // rank)
    own = own & (note[:, :1] > 0)
    put = (note[:, 1:2].astype(jnp.int32) == 16 + column % EXTRA) & (row // 16 == column // EXTRA)
    extra = lax.dot_general(
        one_hot(put & own), delta, (((0,), (0,)), ((), ())), preferred_element_type=jnp.float32
    )
    for g in range(PLANE * planes):
        out[g] = extra[g * EXTRA : (g + 1) * EXTRA]
    flags = [jnp.max(r[:, half : half + NOTE].astype(jnp.float32), axis=0) for r in rows_refs]
    most = functools.reduce(jnp.maximum, flags).reshape(1, NOTE)
    flag_out[...] = most.astype(jnp.int32)


def final_body(at_ref, base_ref, back_ref, out):
    row = lax.broadcasted_iota(jnp.int32, (back_ref.shape[0], at_ref.shape[1]), 0)
    delta = lax.dot_general(
        one_hot(row == at_ref[...]),
        back_ref[...],
        (((0,), (0,)), ((), ())),
        preferred_element_type=jnp.float32,
    )
    out[...] = (base_ref[...] + delta).astype(jnp.bfloat16)


def swap(x, k):
    count = lax.axis_size("ad")
    return lax.ppermute(x, "ad", [(s, s ^ k) for s in range(count)])


def route(tenant_ids, tenant_slot, local):
    tenant = tenant_ids[:, 0]
    tenant_match = tenant[:, None] == jnp.arange(TENANTS, dtype=jnp.int32)[None, :]
    slot = jnp.sum(jnp.where(tenant_match, tenant_slot[None, :], 0), axis=1)
    owner = slot // local
    order = jnp.arange(tenant.shape[0], dtype=jnp.int32)
    before = order[None, :] < order[:, None]
    place = jnp.sum(((owner[:, None] == owner[None, :]) & before).astype(jnp.int32), axis=1)
    return slot, owner, place


def on_device(tokens, value_weight, adapt_down, adapt_up, tenant_ids, tenant_slot):
    row_count, depth = tokens.shape
    count = lax.axis_size("ad")
    me = lax.axis_index("ad")
    local, _, rank = adapt_down.shape
    width = adapt_up.shape[2]
    base_value = jnp.dot(tokens, value_weight, preferred_element_type=jnp.float32)
    room = row_count // count
    planes = count // PLANE
    if count != 16 or room != 16 or depth % (2 * STEP):
        slot, owner, place = route(tenant_ids, tenant_slot, local)
        delta = exchange(tokens, slot, owner, place, CAP * local, adapt_down, adapt_up)
        return (base_value + delta).astype(jnp.bfloat16)

    main_rows = count * room
    *spare, at, at_back, note = pl.pallas_call(
        functools.partial(route_body, room, local),
        in_specs=[SMEM, VMEM, VMEM, ANY],
        out_specs=[VMEM] * (planes + 3),
        out_shape=[jax.ShapeDtypeStruct((2 * SPARE, depth // 2 + NOTE), jnp.bfloat16)] * planes
        + [
            jax.ShapeDtypeStruct((1, row_count), jnp.int32),
            jax.ShapeDtypeStruct((1, row_count), jnp.int32),
            jax.ShapeDtypeStruct((NOTE, row_count), jnp.bfloat16),
        ],
        scratch_shapes=[
            pltpu.VMEM(tokens.shape, jnp.bfloat16),
            pltpu.SemaphoreType.DMA((PARTS,)),
        ],
        compiler_params=pltpu.CompilerParams(vmem_limit_bytes=24 * 2**20),
        cost_estimate=pl.CostEstimate(
            flops=4 * 96 * row_count * depth, bytes_accessed=6 * 2**20, transcendentals=0
        ),
    )(me.reshape(1), tenant_ids.reshape(1, row_count), tenant_slot.reshape(1, TENANTS), tokens)

    along = [swap(spare[b], b * PLANE) for b in range(planes - 1, 0, -1)]
    along = list(lax.optimization_barrier(tuple(along)))
    blocks = pack(main_rows, at, note, tokens)

    along = jnp.concatenate([spare[0]] + along[::-1], axis=0)
    shared = [along] + [swap(along, a) for a in range(1, PLANE)]

    got = lax.all_to_all(
        blocks.reshape(count, room, depth + NOTE), "ad", split_axis=0, concat_axis=0, tiled=True
    ).reshape(main_rows, depth + NOTE)

    first = (me * local).reshape(1)
    down = adapt_down.transpose(0, 2, 1).reshape(local * rank, depth)
    up = adapt_up.reshape(local * rank, width)

    shared[0], base_value = lax.optimization_barrier((shared[0], base_value))
    extra, flag = pl.pallas_call(
        functools.partial(adapt_over_body, planes, rank),
        in_specs=[SMEM, ANY] + [VMEM] * (1 + PLANE),
        out_specs=[VMEM, VMEM],
        out_shape=[
            jax.ShapeDtypeStruct((count, EXTRA, width), jnp.float32),
            jax.ShapeDtypeStruct((1, NOTE), jnp.int32),
        ],
        scratch_shapes=[pltpu.VMEM(down.shape, jnp.bfloat16), pltpu.SemaphoreType.DMA((PARTS,))],
        compiler_params=pltpu.CompilerParams(vmem_limit_bytes=40 * 2**20),
        cost_estimate=pl.CostEstimate(
            flops=10**12,
            bytes_accessed=6 * 2**20,
            transcendentals=0,
        ),
    )(first, down, up, *shared)

    got, extra = lax.optimization_barrier((got, extra))
    delta = adapt(rank, me.reshape(1), down, up, got, extra)
    delta, flag = lax.optimization_barrier((delta, flag))
    back = lax.all_to_all(delta, "ad", split_axis=0, concat_axis=0, tiled=True)
    back = back.reshape(count * (room + EXTRA), width)

    groups = lax.axis_size("grp")
    own = flag[0, 2]
    seen = own
    for g in range(1, groups):
        other = lax.ppermute(own, "grp", [(s, (s + g) % groups) for s in range(groups)])
        seen = jnp.maximum(seen, other)

    def finish(base):
        return pl.pallas_call(
            final_body,
            in_specs=[VMEM] * 3,
            out_specs=VMEM,
            out_shape=jax.ShapeDtypeStruct((row_count, width), jnp.bfloat16),
        )(at_back, base, back)

    def more():
        slot, owner, place = route(tenant_ids, tenant_slot, local)
        extra = exchange(
            tokens,
            slot,
            owner,
            jnp.where(at[0] < 0, place - room, -1),
            CAP * local - room,
            adapt_down,
            adapt_up,
        )
        return finish(base_value + extra)

    return lax.cond(seen > 0, more, lambda: finish(base_value))


def solution(mesh):
    placed = (
        P(("grp", "ad"), None),
        P(),
        P(("grp", "ad"), None, None),
        P(("grp", "ad"), None, None),
        P(("grp", "ad"), None),
        P("grp"),
    )
    return jax.shard_map(
        on_device, mesh=mesh, in_specs=placed, out_specs=P(("grp", "ad"), None), check_vma=False
    )
```

```python
import functools

import jax
import jax.numpy as jnp
from jax import lax
from jax.experimental import pallas as pl
from jax.experimental.pallas import tpu as pltpu
from jax.sharding import PartitionSpec as P

TENANTS = 256
CAP = 2
PLANE = 4
SPARE = 12
EXTRA = 8
NOTE = 128
STEP = 1024
WIDE = 1664
PARTS = 8
VMEM = pl.BlockSpec(memory_space=pltpu.VMEM)
ANY = pl.BlockSpec(memory_space=pl.ANY)
SMEM = pl.BlockSpec(memory_space=pltpu.SMEM)


def exchange(tokens, slot, owner, place, room, down, up):
    count = lax.axis_size("ad")
    local, depth, rank = down.shape
    width = up.shape[2]
    at = jnp.where((place >= 0) & (place < room), owner * room + place, -1)
    hits = at[None, :] == jnp.arange(count * room, dtype=jnp.int32)[:, None]
    slots = jnp.sum(jnp.where(hits, slot[None, :] + 1, 0), axis=1) - 1
    pick = hits.astype(jnp.bfloat16)
    sent = jnp.dot(pick, tokens, preferred_element_type=jnp.float32).astype(jnp.bfloat16)
    got = lax.all_to_all(
        sent.reshape(count, room, depth), "ad", split_axis=0, concat_axis=0, tiled=True
    ).reshape(count * room, depth)
    got_slots = lax.all_to_all(
        slots.reshape(count, room), "ad", split_axis=0, concat_axis=0, tiled=True
    ).reshape(count * room)
    low_rank = jnp.einsum("td,ldr->tlr", got, down, preferred_element_type=jnp.float32)
    own = (got_slots - lax.axis_index("ad") * local)[:, None] == jnp.arange(local)[None, :]
    low_rank = jnp.where(own[:, :, None], low_rank, 0.0).astype(jnp.bfloat16)
    delta = jnp.dot(
        low_rank.reshape(count * room, local * rank),
        up.reshape(local * rank, width),
        preferred_element_type=jnp.float32,
    ).astype(jnp.bfloat16)
    back = lax.all_to_all(
        delta.reshape(count, room, width), "ad", split_axis=0, concat_axis=0, tiled=True
    )
    return jnp.dot(
        pick.T, back.reshape(count * room, width), preferred_element_type=jnp.float32
    )


def row_copies(source, target, sems, parts):
    rows = target.shape[0] // parts
    return [
        pltpu.make_async_copy(
            source.at[i * rows : (i + 1) * rows], target.at[i * rows : (i + 1) * rows], sems.at[i]
        )
        for i in range(parts)
    ]


def one_hot(hit):
    return hit.astype(jnp.float32).astype(jnp.bfloat16)


def earlier(hit, until):
    counts = jnp.dot(one_hot(hit), until, preferred_element_type=jnp.float32)
    return jnp.sum(jnp.where(hit, counts, 0.0), axis=0, keepdims=True).astype(jnp.int32)


def route_body(room, local, me_ref, tenant_ref, slot_ref, tokens_hbm, *refs):
    *outs, at_ref, back_ref, note_ref, tokens_ref, sems = refs
    half = tokens_ref.shape[1] // 2
    copies = row_copies(tokens_hbm, tokens_ref, sems, PARTS)
    for copy in copies:
        copy.start()
    tenant = tenant_ref[...]
    rows = tenant.shape[1]
    planes = len(outs)
    main_rows = planes * PLANE * room

    def iota(size, axis=0):
        return lax.broadcasted_iota(jnp.int32, (size, rows), axis)

    table = jnp.broadcast_to(slot_ref[...].astype(jnp.float32), (16, TENANTS)).astype(jnp.bfloat16)
    slot = jnp.dot(table, one_hot(iota(TENANTS) == tenant), preferred_element_type=jnp.float32)[:1]
    owner = slot.astype(jnp.int32) // local
    until = one_hot(iota(rows) < iota(rows, 1))
    place = earlier(iota(planes * PLANE) == owner, until)
    plane = (owner ^ me_ref[0]) // PLANE
    over = place >= room
    over_place = earlier((iota(16) == plane) & over, until)
    left = over & ((over_place >= SPARE) | (place >= room + EXTRA))
    at = jnp.where(over, main_rows + plane * SPARE + over_place, owner * room + place)
    at = jnp.where(left, -1, at)
    at_ref[...] = at
    back_ref[...] = jnp.where(left, -1, owner * (room + EXTRA) + place)
    note = jnp.where(iota(NOTE) == 0, slot + 1.0, 0.0)
    note = jnp.where(iota(NOTE) == 1, place.astype(jnp.float32), note).astype(jnp.bfloat16)
    note_ref[...] = note
    most = jnp.max(left.astype(jnp.float32), axis=1, keepdims=True)

    row = iota(2 * SPARE)
    upper = row >= SPARE
    ids = jnp.where(upper, row - SPARE, row)
    ids = jnp.concatenate([ids + main_rows + b * SPARE for b in range(planes)], axis=0)
    upper = jnp.concatenate([upper] * planes, axis=0)
    hit = ids == at
    first, second = one_hot(hit & ~upper), one_hot(hit & upper)

    def put(value, columns):
        for b in range(planes):
            outs[b][:, columns] = value[2 * SPARE * b : 2 * SPARE * (b + 1)].astype(jnp.bfloat16)

    notes = notes_of(one_hot(hit), note)
    flag = lax.broadcasted_iota(jnp.int32, notes.shape, 1) == 2
    put(jnp.where(flag, most, notes), slice(half, half + NOTE))
    for copy in copies:
        copy.wait()
    for c in range(0, half, STEP):
        put(
            jnp.dot(first, tokens_ref[:, c : c + STEP], preferred_element_type=jnp.float32)
            + jnp.dot(
                second,
                tokens_ref[:, half + c : half + c + STEP],
                preferred_element_type=jnp.float32,
            ),
            slice(c, c + STEP),
        )


def notes_of(pick, note):
    return lax.dot_general(
        pick, note, (((1,), (1,)), ((), ())), preferred_element_type=jnp.float32
    )


def pack_body(at_ref, note_ref, tokens_ref, out_hbm, out_ref, sems):
    depth = tokens_ref.shape[1]
    stores = row_copies(out_ref, out_hbm, sems, PARTS)
    half = out_ref.shape[0] // 2
    row = lax.broadcasted_iota(jnp.int32, (half, at_ref.shape[1]), 0)
    for h in range(2):
        own = slice(h * half, (h + 1) * half)
        pick = one_hot(row + h * half == at_ref[...])
        for c in range(0, depth, STEP):
            out_ref[own, c : c + STEP] = jnp.dot(
                pick, tokens_ref[:, c : c + STEP], preferred_element_type=jnp.float32
            ).astype(jnp.bfloat16)
        out_ref[own, depth:] = notes_of(pick, note_ref[...]).astype(jnp.bfloat16)
        for store in stores[h * PARTS // 2 : (h + 1) * PARTS // 2]:
            store.start()
    for store in stores:
        store.wait()


def pack(main_rows, at, note, tokens):
    rows, depth = tokens.shape
    out = jax.ShapeDtypeStruct((main_rows, depth + NOTE), jnp.bfloat16)
    return pl.pallas_call(
        pack_body,
        in_specs=[VMEM, VMEM, VMEM],
        out_specs=pl.BlockSpec(memory_space=pltpu.HBM),
        out_shape=out,
        scratch_shapes=[
            pltpu.VMEM(out.shape, jnp.bfloat16),
            pltpu.SemaphoreType.DMA((PARTS,)),
        ],
        compiler_params=pltpu.CompilerParams(vmem_limit_bytes=52 * 2**20),
        cost_estimate=pl.CostEstimate(
            flops=2 * main_rows * rows * depth, bytes_accessed=8 * 2**20, transcendentals=0
        ),
    )(at, note, tokens)


def low_delta(low, note, first, rank, up):
    column = lax.broadcasted_iota(jnp.int32, low.shape, 1) // rank + (first + 1)
    low = jnp.where(note.astype(jnp.float32) == column.astype(jnp.float32), low, 0.0)
    return jnp.dot(low.astype(jnp.bfloat16), up, preferred_element_type=jnp.float32)


def adapt_body(rank, me_ref, down_hbm, up_ref, rows_hbm, extra_ref, out, *scratch):
    down_ref, rows_ref, down_sems, sems = scratch
    depth = down_ref.shape[1]
    spans = [slice(c, min(c + WIDE, depth + NOTE)) for c in range(0, depth + NOTE, WIDE)]
    copies = []
    for i, span in enumerate(spans):
        kept = slice(span.start, min(span.stop, depth))
        copies.append(
            (
                pltpu.make_async_copy(rows_hbm.at[:, span], rows_ref.at[:, span], sems.at[i]),
                pltpu.make_async_copy(down_hbm.at[:, kept], down_ref.at[:, kept], down_sems.at[i]),
            )
        )
    for pair in copies:
        pair[0].start()
        pair[1].start()
    low = jnp.zeros((rows_ref.shape[0], down_ref.shape[0]), jnp.float32)
    for pair, span in zip(copies, spans, strict=True):
        pair[0].wait()
        pair[1].wait()
        span = slice(span.start, min(span.stop, depth))
        low += lax.dot_general(
            rows_ref[:, span],
            down_ref[:, span],
            (((1,), (1,)), ((), ())),
            preferred_element_type=jnp.float32,
        )
    note = rows_ref[:, depth:].astype(jnp.float32)
    sources = out.shape[0]
    first = me_ref[0] * (down_ref.shape[0] // rank)
    delta = low_delta(low, note[:, :1], first, rank, up_ref[...])
    room = delta.shape[0] // sources
    for s in range(sources):
        k = me_ref[0] ^ s
        extra = extra_ref[(k % PLANE) * (sources // PLANE) + k // PLANE]
        rows = jnp.concatenate([delta[s * room : (s + 1) * room], extra], axis=0)
        out[s] = rows.astype(jnp.bfloat16)


def adapt(rank, me, down, up, got, extra):
    rows, width = got.shape[0], up.shape[1]
    count = extra.shape[0]
    return pl.pallas_call(
        functools.partial(adapt_body, rank),
        in_specs=[SMEM, ANY, VMEM, ANY, VMEM],
        out_specs=VMEM,
        out_shape=jax.ShapeDtypeStruct((count, rows // count + EXTRA, width), jnp.bfloat16),
        scratch_shapes=[
            pltpu.VMEM(down.shape, jnp.bfloat16),
            pltpu.VMEM(got.shape, jnp.bfloat16),
            pltpu.SemaphoreType.DMA((pl.cdiv(got.shape[1], WIDE),)),
            pltpu.SemaphoreType.DMA((pl.cdiv(got.shape[1], WIDE),)),
        ],
        compiler_params=pltpu.CompilerParams(vmem_limit_bytes=24 * 2**20),
        cost_estimate=pl.CostEstimate(
            flops=2 * rows * down.size, bytes_accessed=8 * 2**20, transcendentals=0
        ),
    )(me, down, up, got, extra)


def adapt_over_body(planes, rank, first_ref, down_hbm, up_ref, *refs):
    rows_refs = refs[:PLANE]
    out, flag_out, down_ref, sems = refs[PLANE:]
    half = down_ref.shape[1] // 2
    copies = row_copies(down_hbm, down_ref, sems, PARTS)
    for copy in copies:
        copy.start()
    each = rows_refs[0].shape[0]
    shape = (PLANE * each, down_ref.shape[0])
    dims = (((1,), (1,)), ((), ()))
    low0, low1 = jnp.zeros(shape, jnp.float32), jnp.zeros(shape, jnp.float32)
    for copy in copies:
        copy.wait()
    for c in range(0, half, STEP):
        rows = jnp.concatenate([r[:, c : c + STEP] for r in rows_refs], axis=0)
        low0 += lax.dot_general(
            rows, down_ref[:, c : c + STEP], dims, preferred_element_type=jnp.float32
        )
        low1 += lax.dot_general(
            rows, down_ref[:, half + c : half + c + STEP], dims, preferred_element_type=jnp.float32
        )
    zeros = jnp.zeros((16 - SPARE, shape[1]), jnp.float32)
    no_note = jnp.zeros((16 - SPARE, NOTE), jnp.float32)
    lows, notes = [], []
    for a in range(PLANE):
        note = rows_refs[a][:, half : half + NOTE].astype(jnp.float32)
        for b in range(planes):
            s = 2 * SPARE * b
            m = a * each + s
            lows += [low0[m : m + SPARE] + low1[m + SPARE : m + 2 * SPARE], zeros]
            notes += [note[s : s + SPARE], no_note]
    low = jnp.concatenate(lows, axis=0)
    note = jnp.concatenate(notes, axis=0)
    delta = low_delta(low, note[:, :1], first_ref[0], rank, up_ref[...]).astype(jnp.bfloat16)
    shape = (delta.shape[0], PLANE * planes * EXTRA)
    row, column = (lax.broadcasted_iota(jnp.int32, shape, axis) for axis in (0, 1))
    own = (note[:, :1].astype(jnp.int32) - 1) // (down_ref.shape[0] // rank) == first_ref[
        0
    ] // (down_ref.shape[0] // rank)
    own = own & (note[:, :1] > 0)
    put = (note[:, 1:2].astype(jnp.int32) == 16 + column % EXTRA) & (row // 16 == column // EXTRA)
    extra = lax.dot_general(
        one_hot(put & own), delta, (((0,), (0,)), ((), ())), preferred_element_type=jnp.float32
    )
    for g in range(PLANE * planes):
        out[g] = extra[g * EXTRA : (g + 1) * EXTRA]
    flags = [jnp.max(r[:, half : half + NOTE].astype(jnp.float32), axis=0) for r in rows_refs]
    most = functools.reduce(jnp.maximum, flags).reshape(1, NOTE)
    flag_out[...] = most.astype(jnp.int32)


def final_body(at_ref, base_ref, back_ref, out):
    row = lax.broadcasted_iota(jnp.int32, (back_ref.shape[0], at_ref.shape[1]), 0)
    delta = lax.dot_general(
        one_hot(row == at_ref[...]),
        back_ref[...],
        (((0,), (0,)), ((), ())),
        preferred_element_type=jnp.float32,
    )
    out[...] = (base_ref[...] + delta).astype(jnp.bfloat16)


def swap(x, k):
    count = lax.axis_size("ad")
    return lax.ppermute(x, "ad", [(s, s ^ k) for s in range(count)])


def route(tenant_ids, tenant_slot, local):
    tenant = tenant_ids[:, 0]
    tenant_match = tenant[:, None] == jnp.arange(TENANTS, dtype=jnp.int32)[None, :]
    slot = jnp.sum(jnp.where(tenant_match, tenant_slot[None, :], 0), axis=1)
    owner = slot // local
    order = jnp.arange(tenant.shape[0], dtype=jnp.int32)
    before = order[None, :] < order[:, None]
    place = jnp.sum(((owner[:, None] == owner[None, :]) & before).astype(jnp.int32), axis=1)
    return slot, owner, place


def on_device(tokens, value_weight, adapt_down, adapt_up, tenant_ids, tenant_slot):
    row_count, depth = tokens.shape
    count = lax.axis_size("ad")
    me = lax.axis_index("ad")
    local, _, rank = adapt_down.shape
    width = adapt_up.shape[2]
    base_value = jnp.dot(tokens, value_weight, preferred_element_type=jnp.float32)
    room = row_count // count
    planes = count // PLANE
    if count != 16 or planes != 4 or room != 16 or depth % (2 * STEP):
        slot, owner, place = route(tenant_ids, tenant_slot, local)
        delta = exchange(tokens, slot, owner, place, CAP * local, adapt_down, adapt_up)
        return (base_value + delta).astype(jnp.bfloat16)

    main_rows = count * room
    *spare, at, at_back, note = pl.pallas_call(
        functools.partial(route_body, room, local),
        in_specs=[SMEM, VMEM, VMEM, ANY],
        out_specs=[VMEM] * (planes + 3),
        out_shape=[jax.ShapeDtypeStruct((2 * SPARE, depth // 2 + NOTE), jnp.bfloat16)] * planes
        + [
            jax.ShapeDtypeStruct((1, row_count), jnp.int32),
            jax.ShapeDtypeStruct((1, row_count), jnp.int32),
            jax.ShapeDtypeStruct((NOTE, row_count), jnp.bfloat16),
        ],
        scratch_shapes=[
            pltpu.VMEM(tokens.shape, jnp.bfloat16),
            pltpu.SemaphoreType.DMA((PARTS,)),
        ],
        compiler_params=pltpu.CompilerParams(vmem_limit_bytes=24 * 2**20),
        cost_estimate=pl.CostEstimate(
            flops=4 * 96 * row_count * depth, bytes_accessed=6 * 2**20, transcendentals=0
        ),
    )(me.reshape(1), tenant_ids.reshape(1, row_count), tenant_slot.reshape(1, TENANTS), tokens)

    along = [swap(spare[b], b * PLANE) for b in (2, 3, 1)]
    along = list(lax.optimization_barrier(tuple(along)))
    blocks = pack(main_rows, at, note, tokens)

    along = jnp.concatenate([spare[0], along[2], along[0], along[1]], axis=0)
    shared = [along] + [swap(along, a) for a in range(1, PLANE)]

    got = lax.all_to_all(
        blocks.reshape(count, room, depth + NOTE), "ad", split_axis=0, concat_axis=0, tiled=True
    ).reshape(main_rows, depth + NOTE)

    first = (me * local).reshape(1)
    down = adapt_down.transpose(0, 2, 1).reshape(local * rank, depth)
    up = adapt_up.reshape(local * rank, width)

    shared[0], base_value = lax.optimization_barrier((shared[0], base_value))
    extra, flag = pl.pallas_call(
        functools.partial(adapt_over_body, planes, rank),
        in_specs=[SMEM, ANY] + [VMEM] * (1 + PLANE),
        out_specs=[VMEM, VMEM],
        out_shape=[
            jax.ShapeDtypeStruct((count, EXTRA, width), jnp.float32),
            jax.ShapeDtypeStruct((1, NOTE), jnp.int32),
        ],
        scratch_shapes=[pltpu.VMEM(down.shape, jnp.bfloat16), pltpu.SemaphoreType.DMA((PARTS,))],
        compiler_params=pltpu.CompilerParams(vmem_limit_bytes=40 * 2**20),
        cost_estimate=pl.CostEstimate(
            flops=10**12,
            bytes_accessed=6 * 2**20,
            transcendentals=0,
        ),
    )(first, down, up, *shared)

    got, extra = lax.optimization_barrier((got, extra))
    delta = adapt(rank, me.reshape(1), down, up, got, extra)
    delta, flag = lax.optimization_barrier((delta, flag))
    back = lax.all_to_all(delta, "ad", split_axis=0, concat_axis=0, tiled=True)
    back = back.reshape(count * (room + EXTRA), width)

    groups = lax.axis_size("grp")
    own = flag[0, 2]
    seen = own
    for g in range(1, groups):
        other = lax.ppermute(own, "grp", [(s, (s + g) % groups) for s in range(groups)])
        seen = jnp.maximum(seen, other)

    def finish(base):
        return pl.pallas_call(
            final_body,
            in_specs=[VMEM] * 3,
            out_specs=VMEM,
            out_shape=jax.ShapeDtypeStruct((row_count, width), jnp.bfloat16),
        )(at_back, base, back)

    def more():
        slot, owner, place = route(tenant_ids, tenant_slot, local)
        extra = exchange(
            tokens,
            slot,
            owner,
            jnp.where(at[0] < 0, place - room, -1),
            CAP * local - room,
            adapt_down,
            adapt_up,
        )
        return finish(base_value + extra)

    return lax.cond(seen > 0, more, lambda: finish(base_value))


def solution(mesh):
    placed = (
        P(("grp", "ad"), None),
        P(),
        P(("grp", "ad"), None, None),
        P(("grp", "ad"), None, None),
        P(("grp", "ad"), None),
        P("grp"),
    )
    return jax.shard_map(
        on_device, mesh=mesh, in_specs=placed, out_specs=P(("grp", "ad"), None), check_vma=False
    )
```

```python
import functools

import jax
import jax.numpy as jnp
from jax import lax
from jax.experimental import pallas as pl
from jax.experimental.pallas import tpu as pltpu
from jax.sharding import PartitionSpec as P

TENANTS = 256
CAP = 2
PLANE = 4
SPARE = 12
EXTRA = 8
NOTE = 128
STEP = 1024
WIDE = 2816
PARTS = 8
VMEM = pl.BlockSpec(memory_space=pltpu.VMEM)
ANY = pl.BlockSpec(memory_space=pl.ANY)
SMEM = pl.BlockSpec(memory_space=pltpu.SMEM)


def exchange(tokens, slot, owner, place, room, down, up):
    count = lax.axis_size("ad")
    local, depth, rank = down.shape
    width = up.shape[2]
    at = jnp.where((place >= 0) & (place < room), owner * room + place, -1)
    hits = at[None, :] == jnp.arange(count * room, dtype=jnp.int32)[:, None]
    slots = jnp.sum(jnp.where(hits, slot[None, :] + 1, 0), axis=1) - 1
    pick = hits.astype(jnp.bfloat16)
    sent = jnp.dot(pick, tokens, preferred_element_type=jnp.float32).astype(jnp.bfloat16)
    got = lax.all_to_all(
        sent.reshape(count, room, depth), "ad", split_axis=0, concat_axis=0, tiled=True
    ).reshape(count * room, depth)
    got_slots = lax.all_to_all(
        slots.reshape(count, room), "ad", split_axis=0, concat_axis=0, tiled=True
    ).reshape(count * room)
    low_rank = jnp.einsum("td,ldr->tlr", got, down, preferred_element_type=jnp.float32)
    own = (got_slots - lax.axis_index("ad") * local)[:, None] == jnp.arange(local)[None, :]
    low_rank = jnp.where(own[:, :, None], low_rank, 0.0).astype(jnp.bfloat16)
    delta = jnp.dot(
        low_rank.reshape(count * room, local * rank),
        up.reshape(local * rank, width),
        preferred_element_type=jnp.float32,
    ).astype(jnp.bfloat16)
    back = lax.all_to_all(
        delta.reshape(count, room, width), "ad", split_axis=0, concat_axis=0, tiled=True
    )
    return jnp.dot(
        pick.T, back.reshape(count * room, width), preferred_element_type=jnp.float32
    )


def row_copies(source, target, sems, parts):
    rows = target.shape[0] // parts
    return [
        pltpu.make_async_copy(
            source.at[i * rows : (i + 1) * rows], target.at[i * rows : (i + 1) * rows], sems.at[i]
        )
        for i in range(parts)
    ]


def one_hot(hit):
    return hit.astype(jnp.float32).astype(jnp.bfloat16)


def earlier(hit, until):
    counts = jnp.dot(one_hot(hit), until, preferred_element_type=jnp.float32)
    return jnp.sum(jnp.where(hit, counts, 0.0), axis=0, keepdims=True).astype(jnp.int32)


def route_body(room, local, me_ref, tenant_ref, slot_ref, tokens_hbm, *refs):
    *outs, at_ref, back_ref, note_ref, tokens_ref, sems = refs
    half = tokens_ref.shape[1] // 2
    copies = row_copies(tokens_hbm, tokens_ref, sems, PARTS)
    for copy in copies:
        copy.start()
    tenant = tenant_ref[...]
    rows = tenant.shape[1]
    planes = len(outs)
    main_rows = planes * PLANE * room

    def iota(size, axis=0):
        return lax.broadcasted_iota(jnp.int32, (size, rows), axis)

    table = jnp.broadcast_to(slot_ref[...].astype(jnp.float32), (16, TENANTS)).astype(jnp.bfloat16)
    slot = jnp.dot(table, one_hot(iota(TENANTS) == tenant), preferred_element_type=jnp.float32)[:1]
    owner = slot.astype(jnp.int32) // local
    until = one_hot(iota(rows) < iota(rows, 1))
    place = earlier(iota(planes * PLANE) == owner, until)
    plane = (owner ^ me_ref[0]) // PLANE
    over = place >= room
    over_place = earlier((iota(16) == plane) & over, until)
    left = over & ((over_place >= SPARE) | (place >= room + EXTRA))
    at = jnp.where(over, main_rows + plane * SPARE + over_place, owner * room + place)
    at = jnp.where(left, -1, at)
    at_ref[...] = at
    back_ref[...] = jnp.where(left, -1, owner * (room + EXTRA) + place)
    note = jnp.where(iota(NOTE) == 0, slot + 1.0, 0.0)
    note = jnp.where(iota(NOTE) == 1, place.astype(jnp.float32), note).astype(jnp.bfloat16)
    note_ref[...] = note
    most = jnp.max(left.astype(jnp.float32), axis=1, keepdims=True)

    row = iota(2 * SPARE)
    upper = row >= SPARE
    ids = jnp.where(upper, row - SPARE, row)
    ids = jnp.concatenate([ids + main_rows + b * SPARE for b in range(planes)], axis=0)
    upper = jnp.concatenate([upper] * planes, axis=0)
    hit = ids == at
    first, second = one_hot(hit & ~upper), one_hot(hit & upper)

    def put(value, columns):
        for b in range(planes):
            outs[b][:, columns] = value[2 * SPARE * b : 2 * SPARE * (b + 1)].astype(jnp.bfloat16)

    notes = notes_of(one_hot(hit), note)
    flag = lax.broadcasted_iota(jnp.int32, notes.shape, 1) == 2
    put(jnp.where(flag, most, notes), slice(half, half + NOTE))
    for copy in copies:
        copy.wait()
    for c in range(0, half, STEP):
        put(
            jnp.dot(first, tokens_ref[:, c : c + STEP], preferred_element_type=jnp.float32)
            + jnp.dot(
                second,
                tokens_ref[:, half + c : half + c + STEP],
                preferred_element_type=jnp.float32,
            ),
            slice(c, c + STEP),
        )


def notes_of(pick, note):
    return lax.dot_general(
        pick, note, (((1,), (1,)), ((), ())), preferred_element_type=jnp.float32
    )


def pack_body(at_ref, note_ref, tokens_ref, out_hbm, out_ref, sems):
    depth = tokens_ref.shape[1]
    stores = row_copies(out_ref, out_hbm, sems, PARTS)
    half = out_ref.shape[0] // 2
    row = lax.broadcasted_iota(jnp.int32, (half, at_ref.shape[1]), 0)
    for h in range(2):
        own = slice(h * half, (h + 1) * half)
        pick = one_hot(row + h * half == at_ref[...])
        for c in range(0, depth, STEP):
            out_ref[own, c : c + STEP] = jnp.dot(
                pick, tokens_ref[:, c : c + STEP], preferred_element_type=jnp.float32
            ).astype(jnp.bfloat16)
        out_ref[own, depth:] = notes_of(pick, note_ref[...]).astype(jnp.bfloat16)
        for store in stores[h * PARTS // 2 : (h + 1) * PARTS // 2]:
            store.start()
    for store in stores:
        store.wait()


def pack(main_rows, at, note, tokens):
    rows, depth = tokens.shape
    out = jax.ShapeDtypeStruct((main_rows, depth + NOTE), jnp.bfloat16)
    return pl.pallas_call(
        pack_body,
        in_specs=[VMEM, VMEM, VMEM],
        out_specs=pl.BlockSpec(memory_space=pltpu.HBM),
        out_shape=out,
        scratch_shapes=[
            pltpu.VMEM(out.shape, jnp.bfloat16),
            pltpu.SemaphoreType.DMA((PARTS,)),
        ],
        compiler_params=pltpu.CompilerParams(vmem_limit_bytes=52 * 2**20),
        cost_estimate=pl.CostEstimate(
            flops=2 * main_rows * rows * depth, bytes_accessed=8 * 2**20, transcendentals=0
        ),
    )(at, note, tokens)


def low_delta(low, note, first, rank, up):
    column = lax.broadcasted_iota(jnp.int32, low.shape, 1) // rank + (first + 1)
    low = jnp.where(note.astype(jnp.float32) == column.astype(jnp.float32), low, 0.0)
    return jnp.dot(low.astype(jnp.bfloat16), up, preferred_element_type=jnp.float32)


def adapt_body(rank, me_ref, down_hbm, up_ref, rows_hbm, extra_ref, out, *scratch):
    down_ref, rows_ref, down_sems, sems = scratch
    depth = down_ref.shape[1]
    spans = [slice(c, min(c + WIDE, depth + NOTE)) for c in range(0, depth + NOTE, WIDE)]
    copies = []
    for i, span in enumerate(spans):
        kept = slice(span.start, min(span.stop, depth))
        copies.append(
            (
                pltpu.make_async_copy(rows_hbm.at[:, span], rows_ref.at[:, span], sems.at[i]),
                pltpu.make_async_copy(down_hbm.at[:, kept], down_ref.at[:, kept], down_sems.at[i]),
            )
        )
    for pair in copies:
        pair[0].start()
        pair[1].start()
    low = jnp.zeros((rows_ref.shape[0], down_ref.shape[0]), jnp.float32)
    for pair, span in zip(copies, spans, strict=True):
        pair[0].wait()
        pair[1].wait()
        span = slice(span.start, min(span.stop, depth))
        low += lax.dot_general(
            rows_ref[:, span],
            down_ref[:, span],
            (((1,), (1,)), ((), ())),
            preferred_element_type=jnp.float32,
        )
    note = rows_ref[:, depth:].astype(jnp.float32)
    sources = out.shape[0]
    first = me_ref[0] * (down_ref.shape[0] // rank)
    delta = low_delta(low, note[:, :1], first, rank, up_ref[...])
    room = delta.shape[0] // sources
    for s in range(sources):
        k = me_ref[0] ^ s
        extra = extra_ref[(k % PLANE) * (sources // PLANE) + k // PLANE]
        rows = jnp.concatenate([delta[s * room : (s + 1) * room], extra], axis=0)
        out[s] = rows.astype(jnp.bfloat16)


def adapt(rank, me, down, up, got, extra):
    rows, width = got.shape[0], up.shape[1]
    count = extra.shape[0]
    return pl.pallas_call(
        functools.partial(adapt_body, rank),
        in_specs=[SMEM, ANY, VMEM, ANY, VMEM],
        out_specs=VMEM,
        out_shape=jax.ShapeDtypeStruct((count, rows // count + EXTRA, width), jnp.bfloat16),
        scratch_shapes=[
            pltpu.VMEM(down.shape, jnp.bfloat16),
            pltpu.VMEM(got.shape, jnp.bfloat16),
            pltpu.SemaphoreType.DMA((pl.cdiv(got.shape[1], WIDE),)),
            pltpu.SemaphoreType.DMA((pl.cdiv(got.shape[1], WIDE),)),
        ],
        compiler_params=pltpu.CompilerParams(vmem_limit_bytes=24 * 2**20),
        cost_estimate=pl.CostEstimate(
            flops=2 * rows * down.size, bytes_accessed=8 * 2**20, transcendentals=0
        ),
    )(me, down, up, got, extra)


def adapt_over_body(planes, rank, first_ref, down_hbm, up_ref, *refs):
    rows_refs = refs[:PLANE]
    out, flag_out, down_ref, sems = refs[PLANE:]
    half = down_ref.shape[1] // 2
    copies = row_copies(down_hbm, down_ref, sems, PARTS)
    for copy in copies:
        copy.start()
    each = rows_refs[0].shape[0]
    shape = (PLANE * each, down_ref.shape[0])
    dims = (((1,), (1,)), ((), ()))
    low0, low1 = jnp.zeros(shape, jnp.float32), jnp.zeros(shape, jnp.float32)
    for copy in copies:
        copy.wait()
    for c in range(0, half, STEP):
        rows = jnp.concatenate([r[:, c : c + STEP] for r in rows_refs], axis=0)
        low0 += lax.dot_general(
            rows, down_ref[:, c : c + STEP], dims, preferred_element_type=jnp.float32
        )
        low1 += lax.dot_general(
            rows, down_ref[:, half + c : half + c + STEP], dims, preferred_element_type=jnp.float32
        )
    zeros = jnp.zeros((16 - SPARE, shape[1]), jnp.float32)
    no_note = jnp.zeros((16 - SPARE, NOTE), jnp.float32)
    lows, notes = [], []
    for a in range(PLANE):
        note = rows_refs[a][:, half : half + NOTE].astype(jnp.float32)
        for b in range(planes):
            s = 2 * SPARE * b
            m = a * each + s
            lows += [low0[m : m + SPARE] + low1[m + SPARE : m + 2 * SPARE], zeros]
            notes += [note[s : s + SPARE], no_note]
    low = jnp.concatenate(lows, axis=0)
    note = jnp.concatenate(notes, axis=0)
    delta = low_delta(low, note[:, :1], first_ref[0], rank, up_ref[...]).astype(jnp.bfloat16)
    shape = (delta.shape[0], PLANE * planes * EXTRA)
    row, column = (lax.broadcasted_iota(jnp.int32, shape, axis) for axis in (0, 1))
    own = (note[:, :1].astype(jnp.int32) - 1) // (down_ref.shape[0] // rank) == first_ref[
        0
    ] // (down_ref.shape[0] // rank)
    own = own & (note[:, :1] > 0)
    put = (note[:, 1:2].astype(jnp.int32) == 16 + column % EXTRA) & (row // 16 == column // EXTRA)
    extra = lax.dot_general(
        one_hot(put & own), delta, (((0,), (0,)), ((), ())), preferred_element_type=jnp.float32
    )
    for g in range(PLANE * planes):
        out[g] = extra[g * EXTRA : (g + 1) * EXTRA]
    flags = [jnp.max(r[:, half : half + NOTE].astype(jnp.float32), axis=0) for r in rows_refs]
    most = functools.reduce(jnp.maximum, flags).reshape(1, NOTE)
    flag_out[...] = most.astype(jnp.int32)


def final_body(at_ref, base_ref, back_ref, out):
    row = lax.broadcasted_iota(jnp.int32, (back_ref.shape[0], at_ref.shape[1]), 0)
    delta = lax.dot_general(
        one_hot(row == at_ref[...]),
        back_ref[...],
        (((0,), (0,)), ((), ())),
        preferred_element_type=jnp.float32,
    )
    out[...] = (base_ref[...] + delta).astype(jnp.bfloat16)


def swap(x, k):
    count = lax.axis_size("ad")
    return lax.ppermute(x, "ad", [(s, s ^ k) for s in range(count)])


def route(tenant_ids, tenant_slot, local):
    tenant = tenant_ids[:, 0]
    tenant_match = tenant[:, None] == jnp.arange(TENANTS, dtype=jnp.int32)[None, :]
    slot = jnp.sum(jnp.where(tenant_match, tenant_slot[None, :], 0), axis=1)
    owner = slot // local
    order = jnp.arange(tenant.shape[0], dtype=jnp.int32)
    before = order[None, :] < order[:, None]
    place = jnp.sum(((owner[:, None] == owner[None, :]) & before).astype(jnp.int32), axis=1)
    return slot, owner, place


def on_device(tokens, value_weight, adapt_down, adapt_up, tenant_ids, tenant_slot):
    row_count, depth = tokens.shape
    count = lax.axis_size("ad")
    me = lax.axis_index("ad")
    local, _, rank = adapt_down.shape
    width = adapt_up.shape[2]
    base_value = jnp.dot(tokens, value_weight, preferred_element_type=jnp.float32)
    room = row_count // count
    planes = count // PLANE
    if count != 16 or room != 16 or depth % (2 * STEP):
        slot, owner, place = route(tenant_ids, tenant_slot, local)
        delta = exchange(tokens, slot, owner, place, CAP * local, adapt_down, adapt_up)
        return (base_value + delta).astype(jnp.bfloat16)

    main_rows = count * room
    *spare, at, at_back, note = pl.pallas_call(
        functools.partial(route_body, room, local),
        in_specs=[SMEM, VMEM, VMEM, ANY],
        out_specs=[VMEM] * (planes + 3),
        out_shape=[jax.ShapeDtypeStruct((2 * SPARE, depth // 2 + NOTE), jnp.bfloat16)] * planes
        + [
            jax.ShapeDtypeStruct((1, row_count), jnp.int32),
            jax.ShapeDtypeStruct((1, row_count), jnp.int32),
            jax.ShapeDtypeStruct((NOTE, row_count), jnp.bfloat16),
        ],
        scratch_shapes=[
            pltpu.VMEM(tokens.shape, jnp.bfloat16),
            pltpu.SemaphoreType.DMA((PARTS,)),
        ],
        compiler_params=pltpu.CompilerParams(vmem_limit_bytes=24 * 2**20),
        cost_estimate=pl.CostEstimate(
            flops=4 * 96 * row_count * depth, bytes_accessed=6 * 2**20, transcendentals=0
        ),
    )(me.reshape(1), tenant_ids.reshape(1, row_count), tenant_slot.reshape(1, TENANTS), tokens)

    along = [swap(spare[b], b * PLANE) for b in range(planes - 1, 0, -1)]
    along = list(lax.optimization_barrier(tuple(along)))
    blocks = pack(main_rows, at, note, tokens)

    along = jnp.concatenate([spare[0]] + along[::-1], axis=0)
    shared = [along] + [swap(along, a) for a in range(1, PLANE)]

    got = lax.all_to_all(
        blocks.reshape(count, room, depth + NOTE), "ad", split_axis=0, concat_axis=0, tiled=True
    ).reshape(main_rows, depth + NOTE)

    first = (me * local).reshape(1)
    down = adapt_down.transpose(0, 2, 1).reshape(local * rank, depth)
    up = adapt_up.reshape(local * rank, width)

    shared[0], base_value = lax.optimization_barrier((shared[0], base_value))
    extra, flag = pl.pallas_call(
        functools.partial(adapt_over_body, planes, rank),
        in_specs=[SMEM, ANY] + [VMEM] * (1 + PLANE),
        out_specs=[VMEM, VMEM],
        out_shape=[
            jax.ShapeDtypeStruct((count, EXTRA, width), jnp.float32),
            jax.ShapeDtypeStruct((1, NOTE), jnp.int32),
        ],
        scratch_shapes=[pltpu.VMEM(down.shape, jnp.bfloat16), pltpu.SemaphoreType.DMA((PARTS,))],
        compiler_params=pltpu.CompilerParams(vmem_limit_bytes=40 * 2**20),
        cost_estimate=pl.CostEstimate(
            flops=10**12,
            bytes_accessed=6 * 2**20,
            transcendentals=0,
        ),
    )(first, down, up, *shared)

    got, extra = lax.optimization_barrier((got, extra))
    delta = adapt(rank, me.reshape(1), down, up, got, extra)
    delta, flag = lax.optimization_barrier((delta, flag))
    back = lax.all_to_all(delta, "ad", split_axis=0, concat_axis=0, tiled=True)
    back = back.reshape(count * (room + EXTRA), width)

    groups = lax.axis_size("grp")
    own = flag[0, 2]
    seen = own
    for g in range(1, groups):
        other = lax.ppermute(own, "grp", [(s, (s + g) % groups) for s in range(groups)])
        seen = jnp.maximum(seen, other)

    def finish(base):
        return pl.pallas_call(
            final_body,
            in_specs=[VMEM] * 3,
            out_specs=VMEM,
            out_shape=jax.ShapeDtypeStruct((row_count, width), jnp.bfloat16),
        )(at_back, base, back)

    def more():
        slot, owner, place = route(tenant_ids, tenant_slot, local)
        extra = exchange(
            tokens,
            slot,
            owner,
            jnp.where(at[0] < 0, place - room, -1),
            CAP * local - room,
            adapt_down,
            adapt_up,
        )
        return finish(base_value + extra)

    return lax.cond(seen > 0, more, lambda: finish(base_value))


def solution(mesh):
    placed = (
        P(("grp", "ad"), None),
        P(),
        P(("grp", "ad"), None, None),
        P(("grp", "ad"), None, None),
        P(("grp", "ad"), None),
        P("grp"),
    )
    return jax.shard_map(
        on_device, mesh=mesh, in_specs=placed, out_specs=P(("grp", "ad"), None), check_vma=False
    )
```

```python
import functools

import jax
import jax.numpy as jnp
from jax import lax
from jax.experimental import pallas as pl
from jax.experimental.pallas import tpu as pltpu
from jax.sharding import PartitionSpec as P

TENANTS = 256
CAP = 2
PLANE = 4
SPARE = 12
EXTRA = 8
NOTE = 128
STEP = 1024
WIDE = 2816
PARTS = 8
VMEM = pl.BlockSpec(memory_space=pltpu.VMEM)
ANY = pl.BlockSpec(memory_space=pl.ANY)
SMEM = pl.BlockSpec(memory_space=pltpu.SMEM)


def exchange(tokens, slot, owner, place, room, down, up):
    count = lax.axis_size("ad")
    local, depth, rank = down.shape
    width = up.shape[2]
    at = jnp.where((place >= 0) & (place < room), owner * room + place, -1)
    hits = at[None, :] == jnp.arange(count * room, dtype=jnp.int32)[:, None]
    slots = jnp.sum(jnp.where(hits, slot[None, :] + 1, 0), axis=1) - 1
    pick = hits.astype(jnp.bfloat16)
    sent = jnp.dot(pick, tokens, preferred_element_type=jnp.float32).astype(jnp.bfloat16)
    got = lax.all_to_all(
        sent.reshape(count, room, depth), "ad", split_axis=0, concat_axis=0, tiled=True
    ).reshape(count * room, depth)
    got_slots = lax.all_to_all(
        slots.reshape(count, room), "ad", split_axis=0, concat_axis=0, tiled=True
    ).reshape(count * room)
    low_rank = jnp.einsum("td,ldr->tlr", got, down, preferred_element_type=jnp.float32)
    own = (got_slots - lax.axis_index("ad") * local)[:, None] == jnp.arange(local)[None, :]
    low_rank = jnp.where(own[:, :, None], low_rank, 0.0).astype(jnp.bfloat16)
    delta = jnp.dot(
        low_rank.reshape(count * room, local * rank),
        up.reshape(local * rank, width),
        preferred_element_type=jnp.float32,
    ).astype(jnp.bfloat16)
    back = lax.all_to_all(
        delta.reshape(count, room, width), "ad", split_axis=0, concat_axis=0, tiled=True
    )
    return jnp.dot(
        pick.T, back.reshape(count * room, width), preferred_element_type=jnp.float32
    )


def row_copies(source, target, sems, parts):
    rows = target.shape[0] // parts
    return [
        pltpu.make_async_copy(
            source.at[i * rows : (i + 1) * rows], target.at[i * rows : (i + 1) * rows], sems.at[i]
        )
        for i in range(parts)
    ]


def one_hot(hit):
    return hit.astype(jnp.float32).astype(jnp.bfloat16)


def earlier(hit, until):
    counts = jnp.dot(one_hot(hit), until, preferred_element_type=jnp.float32)
    return jnp.sum(jnp.where(hit, counts, 0.0), axis=0, keepdims=True).astype(jnp.int32)


def route_body(room, local, me_ref, tenant_ref, slot_ref, tokens_hbm, *refs):
    *outs, at_ref, back_ref, note_ref, tokens_ref, sems = refs
    half = tokens_ref.shape[1] // 2
    copies = row_copies(tokens_hbm, tokens_ref, sems, PARTS)
    for copy in copies:
        copy.start()
    tenant = tenant_ref[...]
    rows = tenant.shape[1]
    planes = len(outs)
    main_rows = planes * PLANE * room

    def iota(size, axis=0):
        return lax.broadcasted_iota(jnp.int32, (size, rows), axis)

    table = jnp.broadcast_to(slot_ref[...].astype(jnp.float32), (16, TENANTS)).astype(jnp.bfloat16)
    slot = jnp.dot(table, one_hot(iota(TENANTS) == tenant), preferred_element_type=jnp.float32)[:1]
    owner = slot.astype(jnp.int32) // local
    until = one_hot(iota(rows) < iota(rows, 1))
    place = earlier(iota(planes * PLANE) == owner, until)
    plane = (owner ^ me_ref[0]) // PLANE
    over = place >= room
    over_place = earlier((iota(16) == plane) & over, until)
    left = over & ((over_place >= SPARE) | (place >= room + EXTRA))
    at = jnp.where(over, main_rows + plane * SPARE + over_place, owner * room + place)
    at = jnp.where(left, -1, at)
    at_ref[...] = at
    back_ref[...] = jnp.where(left, -1, owner * (room + EXTRA) + place)
    note = jnp.where(iota(NOTE) == 0, slot + 1.0, 0.0)
    note = jnp.where(iota(NOTE) == 1, place.astype(jnp.float32), note).astype(jnp.bfloat16)
    note_ref[...] = note
    most = jnp.max(left.astype(jnp.float32), axis=1, keepdims=True)

    row = iota(2 * SPARE)
    upper = row >= SPARE
    ids = jnp.where(upper, row - SPARE, row)
    ids = jnp.concatenate([ids + main_rows + b * SPARE for b in range(planes)], axis=0)
    upper = jnp.concatenate([upper] * planes, axis=0)
    hit = ids == at
    first, second = one_hot(hit & ~upper), one_hot(hit & upper)

    def put(value, columns):
        for b in range(planes):
            outs[b][:, columns] = value[2 * SPARE * b : 2 * SPARE * (b + 1)].astype(jnp.bfloat16)

    notes = notes_of(one_hot(hit), note)
    flag = lax.broadcasted_iota(jnp.int32, notes.shape, 1) == 2
    put(jnp.where(flag, most, notes), slice(half, half + NOTE))
    for copy in copies:
        copy.wait()
    for c in range(0, half, STEP):
        put(
            jnp.dot(first, tokens_ref[:, c : c + STEP], preferred_element_type=jnp.float32)
            + jnp.dot(
                second,
                tokens_ref[:, half + c : half + c + STEP],
                preferred_element_type=jnp.float32,
            ),
            slice(c, c + STEP),
        )


def notes_of(pick, note):
    return lax.dot_general(
        pick, note, (((1,), (1,)), ((), ())), preferred_element_type=jnp.float32
    )


def pack_body(at_ref, note_ref, tokens_ref, out_hbm, out_ref, sems):
    depth = tokens_ref.shape[1]
    stores = row_copies(out_ref, out_hbm, sems, PARTS)
    half = out_ref.shape[0] // 2
    row = lax.broadcasted_iota(jnp.int32, (half, at_ref.shape[1]), 0)
    for h in range(2):
        own = slice(h * half, (h + 1) * half)
        pick = one_hot(row + h * half == at_ref[...])
        for c in range(0, depth, STEP):
            out_ref[own, c : c + STEP] = jnp.dot(
                pick, tokens_ref[:, c : c + STEP], preferred_element_type=jnp.float32
            ).astype(jnp.bfloat16)
        out_ref[own, depth:] = notes_of(pick, note_ref[...]).astype(jnp.bfloat16)
        for store in stores[h * PARTS // 2 : (h + 1) * PARTS // 2]:
            store.start()
    for store in stores:
        store.wait()


def pack(main_rows, at, note, tokens):
    rows, depth = tokens.shape
    out = jax.ShapeDtypeStruct((main_rows, depth + NOTE), jnp.bfloat16)
    return pl.pallas_call(
        pack_body,
        in_specs=[VMEM, VMEM, VMEM],
        out_specs=pl.BlockSpec(memory_space=pltpu.HBM),
        out_shape=out,
        scratch_shapes=[
            pltpu.VMEM(out.shape, jnp.bfloat16),
            pltpu.SemaphoreType.DMA((PARTS,)),
        ],
        compiler_params=pltpu.CompilerParams(vmem_limit_bytes=48 * 2**20),
        cost_estimate=pl.CostEstimate(
            flops=2 * main_rows * rows * depth, bytes_accessed=8 * 2**20, transcendentals=0
        ),
    )(at, note, tokens)


def low_delta(low, note, first, rank, up):
    column = lax.broadcasted_iota(jnp.int32, low.shape, 1) // rank + (first + 1)
    low = jnp.where(note.astype(jnp.float32) == column.astype(jnp.float32), low, 0.0)
    return jnp.dot(low.astype(jnp.bfloat16), up, preferred_element_type=jnp.float32)


def adapt_body(rank, me_ref, down_hbm, up_ref, rows_hbm, extra_ref, out, *scratch):
    down_ref, rows_ref, down_sems, sems = scratch
    depth = down_ref.shape[1]
    spans = [slice(c, min(c + WIDE, depth + NOTE)) for c in range(0, depth + NOTE, WIDE)]
    copies = []
    for i, span in enumerate(spans):
        kept = slice(span.start, min(span.stop, depth))
        copies.append(
            (
                pltpu.make_async_copy(rows_hbm.at[:, span], rows_ref.at[:, span], sems.at[i]),
                pltpu.make_async_copy(down_hbm.at[:, kept], down_ref.at[:, kept], down_sems.at[i]),
            )
        )
    for pair in copies:
        pair[0].start()
        pair[1].start()
    low = jnp.zeros((rows_ref.shape[0], down_ref.shape[0]), jnp.float32)
    for pair, span in zip(copies, spans, strict=True):
        pair[0].wait()
        pair[1].wait()
        span = slice(span.start, min(span.stop, depth))
        low += lax.dot_general(
            rows_ref[:, span],
            down_ref[:, span],
            (((1,), (1,)), ((), ())),
            preferred_element_type=jnp.float32,
        )
    note = rows_ref[:, depth:].astype(jnp.float32)
    sources = out.shape[0]
    first = me_ref[0] * (down_ref.shape[0] // rank)
    delta = low_delta(low, note[:, :1], first, rank, up_ref[...])
    room = delta.shape[0] // sources
    for s in range(sources):
        k = me_ref[0] ^ s
        extra = extra_ref[(k % PLANE) * (sources // PLANE) + k // PLANE]
        rows = jnp.concatenate([delta[s * room : (s + 1) * room], extra], axis=0)
        out[s] = rows.astype(jnp.bfloat16)


def adapt(rank, me, down, up, got, extra):
    rows, width = got.shape[0], up.shape[1]
    count = extra.shape[0]
    return pl.pallas_call(
        functools.partial(adapt_body, rank),
        in_specs=[SMEM, ANY, VMEM, ANY, VMEM],
        out_specs=VMEM,
        out_shape=jax.ShapeDtypeStruct((count, rows // count + EXTRA, width), jnp.bfloat16),
        scratch_shapes=[
            pltpu.VMEM(down.shape, jnp.bfloat16),
            pltpu.VMEM(got.shape, jnp.bfloat16),
            pltpu.SemaphoreType.DMA((pl.cdiv(got.shape[1], WIDE),)),
            pltpu.SemaphoreType.DMA((pl.cdiv(got.shape[1], WIDE),)),
        ],
        compiler_params=pltpu.CompilerParams(vmem_limit_bytes=24 * 2**20),
        cost_estimate=pl.CostEstimate(
            flops=2 * rows * down.size, bytes_accessed=8 * 2**20, transcendentals=0
        ),
    )(me, down, up, got, extra)


def adapt_over_body(planes, rank, first_ref, down_hbm, up_ref, *refs):
    rows_refs = refs[:PLANE]
    out, flag_out, down_ref, sems = refs[PLANE:]
    half = down_ref.shape[1] // 2
    copies = row_copies(down_hbm, down_ref, sems, PARTS)
    for copy in copies:
        copy.start()
    each = rows_refs[0].shape[0]
    shape = (PLANE * each, down_ref.shape[0])
    dims = (((1,), (1,)), ((), ()))
    low0, low1 = jnp.zeros(shape, jnp.float32), jnp.zeros(shape, jnp.float32)
    for copy in copies:
        copy.wait()
    for c in range(0, half, STEP):
        rows = jnp.concatenate([r[:, c : c + STEP] for r in rows_refs], axis=0)
        low0 += lax.dot_general(
            rows, down_ref[:, c : c + STEP], dims, preferred_element_type=jnp.float32
        )
        low1 += lax.dot_general(
            rows, down_ref[:, half + c : half + c + STEP], dims, preferred_element_type=jnp.float32
        )
    zeros = jnp.zeros((16 - SPARE, shape[1]), jnp.float32)
    no_note = jnp.zeros((16 - SPARE, NOTE), jnp.float32)
    lows, notes = [], []
    for a in range(PLANE):
        note = rows_refs[a][:, half : half + NOTE].astype(jnp.float32)
        for b in range(planes):
            s = 2 * SPARE * b
            m = a * each + s
            lows += [low0[m : m + SPARE] + low1[m + SPARE : m + 2 * SPARE], zeros]
            notes += [note[s : s + SPARE], no_note]
    low = jnp.concatenate(lows, axis=0)
    note = jnp.concatenate(notes, axis=0)
    delta = low_delta(low, note[:, :1], first_ref[0], rank, up_ref[...]).astype(jnp.bfloat16)
    shape = (delta.shape[0], PLANE * planes * EXTRA)
    row, column = (lax.broadcasted_iota(jnp.int32, shape, axis) for axis in (0, 1))
    own = (note[:, :1].astype(jnp.int32) - 1) // (down_ref.shape[0] // rank) == first_ref[
        0
    ] // (down_ref.shape[0] // rank)
    own = own & (note[:, :1] > 0)
    put = (note[:, 1:2].astype(jnp.int32) == 16 + column % EXTRA) & (row // 16 == column // EXTRA)
    extra = lax.dot_general(
        one_hot(put & own), delta, (((0,), (0,)), ((), ())), preferred_element_type=jnp.float32
    )
    for g in range(PLANE * planes):
        out[g] = extra[g * EXTRA : (g + 1) * EXTRA]
    flags = [jnp.max(r[:, half : half + NOTE].astype(jnp.float32), axis=0) for r in rows_refs]
    most = functools.reduce(jnp.maximum, flags).reshape(1, NOTE)
    flag_out[...] = most.astype(jnp.int32)


def final_body(at_ref, base_ref, back_ref, out):
    row = lax.broadcasted_iota(jnp.int32, (back_ref.shape[0], at_ref.shape[1]), 0)
    delta = lax.dot_general(
        one_hot(row == at_ref[...]),
        back_ref[...],
        (((0,), (0,)), ((), ())),
        preferred_element_type=jnp.float32,
    )
    out[...] = (base_ref[...] + delta).astype(jnp.bfloat16)


def swap(x, k):
    count = lax.axis_size("ad")
    return lax.ppermute(x, "ad", [(s, s ^ k) for s in range(count)])


def route(tenant_ids, tenant_slot, local):
    tenant = tenant_ids[:, 0]
    tenant_match = tenant[:, None] == jnp.arange(TENANTS, dtype=jnp.int32)[None, :]
    slot = jnp.sum(jnp.where(tenant_match, tenant_slot[None, :], 0), axis=1)
    owner = slot // local
    order = jnp.arange(tenant.shape[0], dtype=jnp.int32)
    before = order[None, :] < order[:, None]
    place = jnp.sum(((owner[:, None] == owner[None, :]) & before).astype(jnp.int32), axis=1)
    return slot, owner, place


def on_device(tokens, value_weight, adapt_down, adapt_up, tenant_ids, tenant_slot):
    row_count, depth = tokens.shape
    count = lax.axis_size("ad")
    me = lax.axis_index("ad")
    local, _, rank = adapt_down.shape
    width = adapt_up.shape[2]
    base_value = jnp.dot(tokens, value_weight, preferred_element_type=jnp.float32)
    room = row_count // count
    planes = count // PLANE
    if count != 16 or room != 16 or depth % (2 * STEP):
        slot, owner, place = route(tenant_ids, tenant_slot, local)
        delta = exchange(tokens, slot, owner, place, CAP * local, adapt_down, adapt_up)
        return (base_value + delta).astype(jnp.bfloat16)

    main_rows = count * room
    *spare, at, at_back, note, near = pl.pallas_call(
        functools.partial(route_body, room, local),
        in_specs=[SMEM, VMEM, VMEM, ANY],
        out_specs=[VMEM] * (planes + 4),
        out_shape=[jax.ShapeDtypeStruct((2 * SPARE, depth // 2 + NOTE), jnp.bfloat16)] * planes
        + [
            jax.ShapeDtypeStruct((1, row_count), jnp.int32),
            jax.ShapeDtypeStruct((1, row_count), jnp.int32),
            jax.ShapeDtypeStruct((NOTE, row_count), jnp.bfloat16),
            jax.ShapeDtypeStruct(tokens.shape, jnp.bfloat16),
        ],
        scratch_shapes=[
            pltpu.SemaphoreType.DMA((PARTS,)),
        ],
        compiler_params=pltpu.CompilerParams(vmem_limit_bytes=24 * 2**20),
        cost_estimate=pl.CostEstimate(
            flops=4 * 96 * row_count * depth, bytes_accessed=6 * 2**20, transcendentals=0
        ),
    )(me.reshape(1), tenant_ids.reshape(1, row_count), tenant_slot.reshape(1, TENANTS), tokens)

    along = [swap(spare[b], b * PLANE) for b in range(planes - 1, 0, -1)]
    along = list(lax.optimization_barrier(tuple(along)))
    blocks = pack(main_rows, at, note, near)

    along = jnp.concatenate([spare[0]] + along[::-1], axis=0)
    shared = [along] + [swap(along, a) for a in range(1, PLANE)]

    got = lax.all_to_all(
        blocks.reshape(count, room, depth + NOTE), "ad", split_axis=0, concat_axis=0, tiled=True
    ).reshape(main_rows, depth + NOTE)

    first = (me * local).reshape(1)
    down = adapt_down.transpose(0, 2, 1).reshape(local * rank, depth)
    up = adapt_up.reshape(local * rank, width)

    shared[0], base_value = lax.optimization_barrier((shared[0], base_value))
    extra, flag = pl.pallas_call(
        functools.partial(adapt_over_body, planes, rank),
        in_specs=[SMEM, ANY] + [VMEM] * (1 + PLANE),
        out_specs=[VMEM, VMEM],
        out_shape=[
            jax.ShapeDtypeStruct((count, EXTRA, width), jnp.float32),
            jax.ShapeDtypeStruct((1, NOTE), jnp.int32),
        ],
        scratch_shapes=[pltpu.VMEM(down.shape, jnp.bfloat16), pltpu.SemaphoreType.DMA((PARTS,))],
        compiler_params=pltpu.CompilerParams(vmem_limit_bytes=40 * 2**20),
        cost_estimate=pl.CostEstimate(
            flops=10**12,
            bytes_accessed=6 * 2**20,
            transcendentals=0,
        ),
    )(first, down, up, *shared)

    got, extra = lax.optimization_barrier((got, extra))
    delta = adapt(rank, me.reshape(1), down, up, got, extra)
    delta, flag = lax.optimization_barrier((delta, flag))
    back = lax.all_to_all(delta, "ad", split_axis=0, concat_axis=0, tiled=True)
    back = back.reshape(count * (room + EXTRA), width)

    groups = lax.axis_size("grp")
    own = flag[0, 2]
    seen = own
    for g in range(1, groups):
        other = lax.ppermute(own, "grp", [(s, (s + g) % groups) for s in range(groups)])
        seen = jnp.maximum(seen, other)

    def finish(base):
        return pl.pallas_call(
            final_body,
            in_specs=[VMEM] * 3,
            out_specs=VMEM,
            out_shape=jax.ShapeDtypeStruct((row_count, width), jnp.bfloat16),
        )(at_back, base, back)

    def more():
        slot, owner, place = route(tenant_ids, tenant_slot, local)
        extra = exchange(
            tokens,
            slot,
            owner,
            jnp.where(at[0] < 0, place - room, -1),
            CAP * local - room,
            adapt_down,
            adapt_up,
        )
        return finish(base_value + extra)

    return lax.cond(seen > 0, more, lambda: finish(base_value))


def solution(mesh):
    placed = (
        P(("grp", "ad"), None),
        P(),
        P(("grp", "ad"), None, None),
        P(("grp", "ad"), None, None),
        P(("grp", "ad"), None),
        P("grp"),
    )
    return jax.shard_map(
        on_device, mesh=mesh, in_specs=placed, out_specs=P(("grp", "ad"), None), check_vma=False
    )
```
